32 devices in a mesh: rows: 4 (over y, x), batch: 8 (over z, core).
Axes of the slice: x: 2, y: 2, z: 4, core: 2. Of those that a mesh axis runs over, the one named last changes fastest.
Arguments:
- pixels: float32 [64, 32, 32, 3], P('batch', 'rows'), may hold values from 0 to 256
- valid: int32 [64, 32, 32], P('batch', 'rows'), may hold values from 0 to 1, as said below
- entry_conv: float32 [2, 3, 3, 6, 64], replicated, may hold values from -0.875 to 0.875
- entry_first: float32 [2, 3, 3, 6, 64], replicated, may hold values from -0.0068359375 to 0.0068359375
- entry_second: float32 [2, 3, 3, 6, 64], replicated, may hold values from 1.525879e-08 to 6.103516e-08
- block_conv: float32 [2, 2, 2, 3, 3, 64, 64], replicated, may hold values from -0.25 to 0.25
- block_first: float32 [2, 2, 2, 3, 3, 64, 64], replicated, may hold values from -0.0068359375 to 0.0068359375
- block_second: float32 [2, 2, 2, 3, 3, 64, 64], replicated, may hold values from 1.525879e-08 to 6.103516e-08
- exit_one: float32 [3, 3, 64, 6], replicated, may hold values from -0.25 to 0.25
- exit_one_first: float32 [3, 3, 64, 6], replicated, may hold values from -0.0068359375 to 0.0068359375
- exit_one_second: float32 [3, 3, 64, 6], replicated, may hold values from 1.525879e-08 to 6.103516e-08
- exit_two: float32 [3, 3, 64, 12], replicated, may hold values from -0.25 to 0.25
- exit_two_first: float32 [3, 3, 64, 12], replicated, may hold values from -0.0068359375 to 0.0068359375
- exit_two_second: float32 [3, 3, 64, 12], replicated, may hold values from 1.525879e-08 to 6.103516e-08
- norm_params: float32 [2, 5, 2, 64], replicated, may hold values from 0.5 to 1.5
- norm_first: float32 [2, 5, 2, 64], replicated, may hold values from -0.015625 to 0.015625
- norm_second: float32 [2, 5, 2, 64], replicated, may hold values from 1.2207032e-07 to 4.882813e-07
- head_params: float32 [27], replicated, may hold values from -1.5 to 1.5
- head_first: float32 [27], replicated, may hold values from -0.4375 to 0.4375
- head_second: float32 [27], replicated, may hold values from 0.0001 to 0.0004
Outputs:
- loss_sum: float32 [], replicated
- valid_count: float32 [], replicated
- entry_new: float32 [2, 3, 3, 6, 64], replicated
- entry_first_new: float32 [2, 3, 3, 6, 64], replicated
- entry_second_new: float32 [2, 3, 3, 6, 64], replicated
- entry_copy: bfloat16 [2, 3, 3, 6, 64], replicated
- block_new: float32 [2, 2, 2, 3, 3, 64, 64], replicated
- block_first_new: float32 [2, 2, 2, 3, 3, 64, 64], replicated
- block_second_new: float32 [2, 2, 2, 3, 3, 64, 64], replicated
- block_copy: bfloat16 [2, 2, 2, 3, 3, 64, 64], replicated
- exit_one_new: float32 [3, 3, 64, 6], replicated
- exit_one_first_new: float32 [3, 3, 64, 6], replicated
- exit_one_second_new: float32 [3, 3, 64, 6], replicated
- exit_one_copy: bfloat16 [3, 3, 64, 6], replicated
- exit_two_new: float32 [3, 3, 64, 12], replicated
- exit_two_first_new: float32 [3, 3, 64, 12], replicated
- exit_two_second_new: float32 [3, 3, 64, 12], replicated
- exit_two_copy: bfloat16 [3, 3, 64, 12], replicated
- norm_new: float32 [2, 5, 2, 64], replicated
- norm_first_new: float32 [2, 5, 2, 64], replicated
- norm_second_new: float32 [2, 5, 2, 64], replicated
- norm_copy: bfloat16 [2, 5, 2, 64], replicated
- head_new: float32 [27], replicated
- head_first_new: float32 [27], replicated
- head_second_new: float32 [27], replicated
- head_copy: bfloat16 [27], replicated
The draws below stay inside these ranges and needn't reach their ends.
Inputs may be any that keep to these rules, and one draw needn't show every extreme that they name: `valid`: each image's ones form one rectangle of at least 4 rows and 16 columns.
All inputs are finite; a program needn't handle non-finite values.
Results may differ from the reference program's by a relative error of at most 0.012.
The reference program's roundings to bfloat16 on the way count: a program that leaves them out, or rounds other values in their place, can miss the bound.
Values may be sent and summed in bfloat16 or wider, within the bound.
No kernel may reach another device: no remote copies, remote signals or barrier semaphores. Data moves between devices by JAX's collectives and lax.ppermute only.
A program may use at most 192 MiB of HBM per device.

```python
import math
import jax
import jax.numpy as jnp
from jax import lax

F = 64
C = 3
H = 32
W = 32
BLOCKS = 2
STEP = 10
BATCH = 64
NORMS = 5
HEAD = 27


def draw_pixels(key, part):
    key = jax.random.fold_in(key, 11)
    level_key, extra_key = jax.random.split(key)
    image_number = jnp.arange(BATCH, dtype=jnp.int32)[:, None, None, None]
    row_number = jnp.arange(H, dtype=jnp.int32)[None, :, None, None]
    product = (row_number + 1) * (image_number + 1)
    center = 48 + 160 * product // (H * BATCH)
    spread = 24 + 23 * product // (H * BATCH)
    values = jax.random.randint(level_key, (BATCH, H, W, C), center - spread, center + spread)
    values = values.at[BATCH - 1, H - 1, 0, 0].set(255)
    values = values.at[BATCH - 1, H - 1, 1, 0].set(0)
    fraction = jax.random.uniform(extra_key, (BATCH, H, W, C), jnp.float32, 0.0, 0.999)
    return values.astype(jnp.float32) + fraction


def draw_valid(key, part):
    key = jax.random.fold_in(key, 23)
    subkeys = jax.random.split(key, 4)
    image_number = jnp.arange(BATCH, dtype=jnp.int32)
    remaining = BATCH - image_number
    top_limit = 3 * H // 4 * remaining * remaining // (BATCH * BATCH)
    side_limit = W // 4 * remaining * remaining // (BATCH * BATCH)
    top_cut = jax.random.randint(subkeys[0], (BATCH,), 0, top_limit + 1)
    bottom_cut = jax.random.randint(subkeys[1], (BATCH,), 0, H // 8 + 1)
    left_cut = jax.random.randint(subkeys[2], (BATCH,), 0, side_limit + 1)
    right_cut = jax.random.randint(subkeys[3], (BATCH,), 0, side_limit + 1)
    rowpos = jnp.arange(H, dtype=jnp.int32)[None, :, None]
    colpos = jnp.arange(W, dtype=jnp.int32)[None, None, :]
    inside = (rowpos >= top_cut[:, None, None]) & (rowpos < H - bottom_cut[:, None, None])
    inside = inside & (colpos >= left_cut[:, None, None]) & (colpos < W - right_cut[:, None, None])
    return inside.astype(jnp.int32)


def draw_head_params(key, part):
    key = jax.random.fold_in(key, 31)
    subkeys = jax.random.split(key, 3)
    magnitude = jnp.exp(jax.random.uniform(subkeys[0], (HEAD,), jnp.float32, math.log(0.5), math.log(1.5)))
    signs = (2 * jax.random.randint(subkeys[1], (HEAD,), 0, 2) - 1).astype(jnp.float32)
    biases = jnp.clip(0.5 * jax.random.normal(subkeys[2], (HEAD,), jnp.float32), -1.25, 1.25)
    position = jnp.arange(HEAD, dtype=jnp.int32)
    return jnp.where(position < 3 * C, signs * magnitude, biases).astype(jnp.float32)


def scatter_about(stream_key, shape, deviation, reach, held_as=jnp.bfloat16):
    entries = jax.random.normal(stream_key, shape, jnp.float32) * deviation
    return jnp.minimum(jnp.maximum(entries, -reach), reach).astype(held_as)


def setup_inputs(seed: int = 0) -> dict:
    key_list = jax.random.split(jax.random.key(seed), 21)
    return {
        "pixels": draw_pixels(jax.random.fold_in(key_list[20], 71), 0),
        "valid": draw_valid(jax.random.fold_in(key_list[20], 71), 0),
        "entry_conv": scatter_about(key_list[2], (2, 3, 3, 2 * C, F), (18 * C) ** -0.5, 0.875, jnp.float32),
        "entry_first": scatter_about(key_list[3], (2, 3, 3, 2 * C, F), (0.11 / (BATCH * H * W) ** 0.5), 0.0068359375, jnp.float32),
        "entry_second": jnp.clip(jnp.exp(jax.random.uniform(key_list[4], (2, 3, 3, 2 * C, F), jnp.float32, math.log(1.525878978725359e-08), math.log(6.103515914901436e-08))), 1.525878978725359e-08, 6.103515914901436e-08),
        "block_conv": scatter_about(key_list[5], (2, BLOCKS, 2, 3, 3, F, F), (9 * F) ** -0.5, 0.25, jnp.float32),
        "block_first": scatter_about(key_list[6], (2, BLOCKS, 2, 3, 3, F, F), (0.11 / (BATCH * H * W) ** 0.5), 0.0068359375, jnp.float32),
        "block_second": jnp.clip(jnp.exp(jax.random.uniform(key_list[7], (2, BLOCKS, 2, 3, 3, F, F), jnp.float32, math.log(1.525878978725359e-08), math.log(6.103515914901436e-08))), 1.525878978725359e-08, 6.103515914901436e-08),
        "exit_one": scatter_about(key_list[8], (3, 3, F, 2 * C), (9 * F) ** -0.5, 0.25, jnp.float32),
        "exit_one_first": scatter_about(key_list[9], (3, 3, F, 2 * C), (0.11 / (BATCH * H * W) ** 0.5), 0.0068359375, jnp.float32),
        "exit_one_second": jnp.clip(jnp.exp(jax.random.uniform(key_list[10], (3, 3, F, 2 * C), jnp.float32, math.log(1.525878978725359e-08), math.log(6.103515914901436e-08))), 1.525878978725359e-08, 6.103515914901436e-08),
        "exit_two": scatter_about(key_list[11], (3, 3, F, 4 * C), (9 * F) ** -0.5, 0.25, jnp.float32),
        "exit_two_first": scatter_about(key_list[12], (3, 3, F, 4 * C), (0.11 / (BATCH * H * W) ** 0.5), 0.0068359375, jnp.float32),
        "exit_two_second": jnp.clip(jnp.exp(jax.random.uniform(key_list[13], (3, 3, F, 4 * C), jnp.float32, math.log(1.525878978725359e-08), math.log(6.103515914901436e-08))), 1.525878978725359e-08, 6.103515914901436e-08),
        "norm_params": jnp.clip(1.0 + 0.1 * jax.random.normal(key_list[14], (2, NORMS, 2, F), jnp.float32), 0.5, 1.5),
        "norm_first": scatter_about(key_list[15], (2, NORMS, 2, F), (0.3 / (BATCH * H * W) ** 0.5), 0.015625, jnp.float32),
        "norm_second": jnp.clip(jnp.exp(jax.random.uniform(key_list[16], (2, NORMS, 2, F), jnp.float32, math.log(1.2207031829802872e-07), math.log(4.882812731921149e-07))), 1.2207031829802872e-07, 4.882812731921149e-07),
        "head_params": draw_head_params(jax.random.fold_in(key_list[20], 71), 0),
        "head_first": scatter_about(key_list[18], (HEAD,), 0.03, 0.4375, jnp.float32),
        "head_second": jnp.clip(jnp.exp(jax.random.uniform(key_list[19], (HEAD,), jnp.float32, math.log(0.0001), math.log(0.0004))), 0.0001, 0.0004),
    }


@jax.custom_vjp
def low(v):
    return lax.optimization_barrier(v.astype(jnp.bfloat16)).astype(jnp.float32)

@jax.custom_vjp
def low_back(v):
    return v

def low_keep(v):
    return (low(v), None)

def low_pass(kept, grad):
    return (grad,)

def back_keep(v):
    return (v, None)

def back_low(kept, grad):
    return (low(grad),)
low.defvjp(low_keep, low_pass)
low_back.defvjp(back_keep, back_low)
ALPHA = 0.05
NORM_EPS = 1e-05
BETA_ONE = 0.9
BETA_TWO = 0.999
ADAM_EPS = 1e-08
DECAY = 0.01
RATE_CONV = 1.0
RATE_SMALL = 10.0
LOG_TWO = math.log(2.0)
HALF_LOG_TAU = 0.5 * math.log(2.0 * math.pi)
LOG_LEVELS = math.log(256.0)

def convolve(inputs, kernel):
    result = lax.conv_general_dilated(low(inputs), low(kernel), (1, 1), 'SAME', dimension_numbers=('NHWC', 'HWIO', 'NHWC'), precision=lax.Precision.HIGHEST)
    return low_back(result)

def norm_act(value, params):
    average = lax.optimization_barrier(jnp.mean(value, axis=(0, 1, 2)))
    centered = value - average
    variance = lax.optimization_barrier(jnp.mean(centered * centered, axis=(0, 1, 2)))
    normed = centered * lax.rsqrt(variance + NORM_EPS)
    return jax.nn.silu(normed * params[0] + params[1])

def coupling_net(inputs, entry, blocks, exit_kernel, norms, bias):
    hidden = convolve(inputs, entry)
    for block_index in range(BLOCKS):
        middle = convolve(norm_act(hidden, norms[2 * block_index]), blocks[block_index, 0])
        hidden = hidden + convolve(norm_act(middle, norms[2 * block_index + 1]), blocks[block_index, 1])
    return convolve(norm_act(hidden, norms[2 * BLOCKS]), exit_kernel) + bias

def squeeze(array):
    batch_n, height, columns, channels = array.shape
    grouped = array.reshape(batch_n, height // 2, 2, columns // 2, 2, channels).transpose(0, 1, 3, 2, 4, 5)
    return grouped.reshape(batch_n, height // 2, columns // 2, 4 * channels)

def adamw(master, first, second, grad, rate):
    first_new = BETA_ONE * first + (1.0 - BETA_ONE) * grad
    second_new = BETA_TWO * second + (1.0 - BETA_TWO) * grad * grad
    direction = first_new / (1.0 - BETA_ONE ** STEP) / (jnp.sqrt(second_new / (1.0 - BETA_TWO ** STEP)) + ADAM_EPS)
    master_new = master - rate * (direction + DECAY * master)
    return (master_new, first_new, second_new, master_new.astype(jnp.bfloat16))

def reference(pixels, valid, entry_conv, entry_first, entry_second, block_conv, block_first, block_second, exit_one, exit_one_first, exit_one_second, exit_two, exit_two_first, exit_two_second, norm_params, norm_first, norm_second, head_params, head_first, head_second):
    scaled = pixels / 256.0
    prob = ALPHA + (1.0 - 2.0 * ALPHA) * scaled
    logits = jnp.log(prob) - jnp.log(1.0 - prob)
    jacobian = squeeze(math.log(1.0 - 2.0 * ALPHA) - jnp.log(prob) - jnp.log(1.0 - prob))
    rowpos = jnp.arange(H, dtype=jnp.int32)[:, None]
    colpos = jnp.arange(W, dtype=jnp.int32)[None, :]
    parity = ((rowpos + colpos) % 2 == 0).astype(jnp.float32)[None, :, :, None]
    dim_mask = squeeze(jnp.broadcast_to(valid.astype(jnp.float32)[..., None], logits.shape))
    total_valid = jnp.sum(dim_mask)
    first_in = jnp.concatenate([logits * parity, jnp.broadcast_to(parity, logits.shape)], axis=3)

    def loss_of(params):
        entry, blocks, exit_a, exit_b, norms, head = params
        out_one = coupling_net(first_in, entry[0], blocks[0], exit_a, norms[0], head[3 * C:5 * C])
        scale_one = head[0:C] * jnp.tanh(out_one[..., :C])
        coupled = logits * parity + (1.0 - parity) * (logits * jnp.exp(scale_one) + out_one[..., C:])
        squeezed = squeeze(coupled)
        logdet = squeeze((1.0 - parity) * scale_one)
        first_half = squeezed[..., :2 * C]
        out_two = coupling_net(first_half, entry[1], blocks[1], exit_b, norms[1], head[5 * C:9 * C])
        scale_two = head[C:3 * C] * jnp.tanh(out_two[..., :2 * C])
        latent = jnp.concatenate([first_half, squeezed[..., 2 * C:] * jnp.exp(scale_two) + out_two[..., 2 * C:]], axis=3)
        logdet = logdet + jnp.concatenate([jnp.zeros_like(scale_two), scale_two], axis=3)
        neg_loglik = 0.5 * latent * latent + HALF_LOG_TAU - logdet - jacobian + LOG_LEVELS
        summed = jnp.sum(dim_mask * neg_loglik) / LOG_TWO
        return (summed / total_valid, summed)
    params = (entry_conv, block_conv, exit_one, exit_two, norm_params, head_params)
    loss, grad_fn, loss_total = jax.vjp(loss_of, params, has_aux=True)
    grads = grad_fn(jnp.ones_like(loss))[0]
    entry_out = adamw(entry_conv, entry_first, entry_second, grads[0], RATE_CONV)
    block_out = adamw(block_conv, block_first, block_second, grads[1], RATE_CONV)
    exit_a_out = adamw(exit_one, exit_one_first, exit_one_second, grads[2], RATE_CONV)
    exit_b_out = adamw(exit_two, exit_two_first, exit_two_second, grads[3], RATE_CONV)
    norm_out = adamw(norm_params, norm_first, norm_second, grads[4], RATE_SMALL)
    head_out = adamw(head_params, head_first, head_second, grads[5], RATE_SMALL)
    return (loss_total, total_valid, entry_out[0], entry_out[1], entry_out[2], entry_out[3], block_out[0], block_out[1], block_out[2], block_out[3], exit_a_out[0], exit_a_out[1], exit_a_out[2], exit_a_out[3], exit_b_out[0], exit_b_out[1], exit_b_out[2], exit_b_out[3], norm_out[0], norm_out[1], norm_out[2], norm_out[3], head_out[0], head_out[1], head_out[2], head_out[3])
```

```python
import math

import jax
import jax.numpy as jnp
from jax import lax
from jax.sharding import PartitionSpec as P

STEP = 10
ALPHA = 0.05
NORM_EPS = 1e-05
BETA_ONE = 0.9
BETA_TWO = 0.999
ADAM_EPS = 1e-08
DECAY = 0.01
RATE_CONV = 1.0
RATE_SMALL = 10.0
LOG_TWO = math.log(2.0)
HALF_LOG_TAU = 0.5 * math.log(2.0 * math.pi)
LOG_LEVELS = math.log(256.0)
IMAGES = 8
BITS = (("batch", 1), ("rows", 1), ("rows", 2), ("batch", 2), ("batch", 4), ("batch", 8), ("batch", 16), ("batch", 32))


def axis_bits():
    return [bit for bit in BITS if bit[1] < lax.axis_size(bit[0])]


def group_bits(batch):
    bits = axis_bits()
    count = max(batch // IMAGES, 1).bit_length() - 1
    return bits[: min(count, len(bits))]


def swap(value, bit):
    axis, mask = bit
    return lax.ppermute(value, axis, [(i, i ^ mask) for i in range(lax.axis_size(axis))])


def side(bit):
    return (lax.axis_index(bit[0]) // bit[1]) % 2


def group_sum(value, bits):
    for bit in bits:
        value = jax.tree.map(lambda own: own + swap(own, bit), value)
    return value


def distribute(cells, group):
    for bit in sorted(axis_bits(), key=lambda b: (b[0] != "rows", b[1])):
        mine = side(bit)
        dim = 1 if bit[0] == "rows" else 0
        if bit in group:
            if bit[0] == "batch":
                continue
            half = cells.shape[0] // 2
            away = lax.dynamic_slice_in_dim(cells, (1 - mine) * half, half, 0)
            cells = lax.dynamic_slice_in_dim(cells, mine * half, half, 0)
        else:
            away = cells
        other = swap(away, bit)
        first = jnp.where(mine == 0, cells, other)
        second = jnp.where(mine == 0, other, cells)
        cells = jnp.concatenate([first, second], axis=dim)
    return cells


def squeeze(array):
    batch_n, height, columns, channels = array.shape
    grouped = array.reshape(batch_n, height // 2, 2, columns // 2, 2, channels).transpose(
        0, 1, 3, 2, 4, 5
    )
    return grouped.reshape(batch_n, height // 2, columns // 2, 4 * channels)


def unsqueeze(array):
    batch_n, height, columns, channels = array.shape
    grouped = array.reshape(batch_n, height, columns, 2, 2, channels // 4).transpose(
        0, 1, 3, 2, 4, 5
    )
    return grouped.reshape(batch_n, 2 * height, 2 * columns, channels // 4)


def conv(inputs, kernel):
    return lax.conv_general_dilated(
        inputs,
        kernel,
        (1, 1),
        "SAME",
        dimension_numbers=("NHWC", "HWIO", "NHWC"),
        preferred_element_type=jnp.float32,
    )


def conv_backward(inputs, kernel, grad_out, need_input):
    grad_low = grad_out.astype(jnp.bfloat16)
    kernel_grad = lax.conv_general_dilated(
        inputs,
        grad_low,
        (1, 1),
        ((1, 1), (1, 1)),
        dimension_numbers=("CHWN", "IHWO", "HWNC"),
        preferred_element_type=jnp.float32,
    )
    grad_in = None
    if need_input:
        grad_in = conv(grad_low, jnp.flip(kernel, (0, 1)).transpose(0, 1, 3, 2))
    return (kernel_grad, grad_in)


def norm_forward(value, params, group):
    count = value.shape[0] * value.shape[1] * value.shape[2]
    average = jnp.mean(value, axis=(0, 1, 2))
    spread = jnp.sum(jnp.square(value - average), axis=(0, 1, 2))
    both = jnp.stack([average, spread])
    for bit in group:
        other = swap(both, bit)
        gap = both[0] - other[0]
        both = jnp.stack([0.5 * (both[0] + other[0]), both[1] + other[1] + gap * gap * (0.5 * count)])
        count = 2 * count
    inv_std = lax.rsqrt(both[1] / count + NORM_EPS)
    normed = (value - both[0]) * inv_std
    return (jax.nn.silu(normed * params[0] + params[1]).astype(jnp.bfloat16), (normed, inv_std, count))


def norm_backward(grad_act, stored, params, group):
    normed, inv_std, cells = stored
    affine = normed * params[0] + params[1]
    sigmoid_val = jax.nn.sigmoid(affine)
    grad_affine = grad_act * sigmoid_val * (1.0 + affine * (1.0 - sigmoid_val))
    both = group_sum(
        jnp.stack([jnp.sum(grad_affine * normed, axis=(0, 1, 2)), jnp.sum(grad_affine, axis=(0, 1, 2))]),
        group,
    )
    grad_in = params[0] * inv_std * (grad_affine - both[1] / cells - normed * both[0] / cells)
    return (grad_in, both)


def net_forward(inputs, entry, blocks, exit_kernel, norms, bias, group):
    entry_in = inputs.astype(jnp.bfloat16)
    hidden = conv(entry_in, entry)
    stored_blocks = []
    for block_index in range(blocks.shape[0]):
        act_one, norm_one = norm_forward(hidden, norms[2 * block_index], group)
        middle = conv(act_one, blocks[block_index, 0])
        act_two, norm_two = norm_forward(middle, norms[2 * block_index + 1], group)
        hidden = hidden + conv(act_two, blocks[block_index, 1])
        stored_blocks.append((norm_one, act_one, norm_two, act_two))
    act_last, norm_last = norm_forward(hidden, norms[-1], group)
    return (conv(act_last, exit_kernel) + bias, (entry_in, stored_blocks, norm_last, act_last))


def net_backward(grad_out, stored, entry, blocks, exit_kernel, norms, need_input, group):
    entry_in, stored_blocks, norm_last, act_last = stored
    exit_grad, grad_act = conv_backward(act_last, exit_kernel, grad_out, True)
    grad_hidden, last_norm_grad = norm_backward(grad_act, norm_last, norms[-1], group)
    block_grads = [None] * blocks.shape[0]
    norm_grads = [None] * norms.shape[0]
    norm_grads[-1] = last_norm_grad
    for block_index in reversed(range(blocks.shape[0])):
        norm_one, act_one, norm_two, act_two = stored_blocks[block_index]
        second_grad, grad_two = conv_backward(act_two, blocks[block_index, 1], grad_hidden, True)
        grad_middle, norm_grads[2 * block_index + 1] = norm_backward(
            grad_two, norm_two, norms[2 * block_index + 1], group
        )
        first_grad, grad_one = conv_backward(act_one, blocks[block_index, 0], grad_middle, True)
        grad_part, norm_grads[2 * block_index] = norm_backward(
            grad_one, norm_one, norms[2 * block_index], group
        )
        grad_hidden = grad_hidden + grad_part
        block_grads[block_index] = jnp.stack([first_grad, second_grad])
    entry_grad, input_grad = conv_backward(entry_in, entry, grad_hidden, need_input)
    return (entry_grad, jnp.stack(block_grads), exit_grad, jnp.stack(norm_grads), input_grad)


def adamw(master, first, second, grad, rate):
    first_new = BETA_ONE * first + (1.0 - BETA_ONE) * grad
    second_new = BETA_TWO * second + (1.0 - BETA_TWO) * grad * grad
    direction = (
        first_new
        / (1.0 - BETA_ONE**STEP)
        / (jnp.sqrt(second_new / (1.0 - BETA_TWO**STEP)) + ADAM_EPS)
    )
    master_new = master - rate * (direction + DECAY * master)
    return (master_new, first_new, second_new, master_new.astype(jnp.bfloat16))


def body(
    pixels,
    valid,
    entry_conv,
    entry_first,
    entry_second,
    block_conv,
    block_first,
    block_second,
    exit_one,
    exit_one_first,
    exit_one_second,
    exit_two,
    exit_two_first,
    exit_two_second,
    norm_params,
    norm_first,
    norm_second,
    head_params,
    head_first,
    head_second,
):
    chans = pixels.shape[3]
    group = group_bits(pixels.shape[0] * lax.axis_size("batch"))
    cells = distribute(jnp.concatenate([pixels, valid[..., None].astype(jnp.float32)], axis=3), group)
    pixels = cells[..., :chans]
    valid_float = cells[..., chans]
    rowpos = jnp.arange(pixels.shape[1], dtype=jnp.int32)[:, None]
    colpos = jnp.arange(pixels.shape[2], dtype=jnp.int32)[None, :]
    parity = ((rowpos + colpos) % 2 == 0).astype(jnp.float32)[None, :, :, None]
    scaled = pixels / 256.0
    prob = ALPHA + (1.0 - 2.0 * ALPHA) * scaled
    logits = jnp.log(prob) - jnp.log(1.0 - prob)
    jacobian = squeeze(math.log(1.0 - 2.0 * ALPHA) - jnp.log(prob) - jnp.log(1.0 - prob))
    dim_mask = squeeze(jnp.broadcast_to(valid_float[..., None], logits.shape))
    total_valid = group_sum(jnp.sum(dim_mask)[None], group)[0]
    first_in = jnp.concatenate([logits * parity, jnp.broadcast_to(parity, logits.shape)], axis=3)
    entry_low = entry_conv.astype(jnp.bfloat16)
    block_low = block_conv.astype(jnp.bfloat16)
    exit_one_low = exit_one.astype(jnp.bfloat16)
    exit_two_low = exit_two.astype(jnp.bfloat16)
    out_one, stored_one = net_forward(
        first_in,
        entry_low[0],
        block_low[0],
        exit_one_low,
        norm_params[0],
        head_params[3 * chans : 5 * chans],
        group,
    )
    tanh_one = jnp.tanh(out_one[..., :chans])
    scale_one = head_params[0:chans] * tanh_one
    exp_one = jnp.exp(scale_one)
    coupled = logits * parity + (1.0 - parity) * (logits * exp_one + out_one[..., chans:])
    squeezed = squeeze(coupled)
    logdet = squeeze((1.0 - parity) * scale_one)
    first_half = squeezed[..., : 2 * chans]
    second_half = squeezed[..., 2 * chans :]
    out_two, stored_two = net_forward(
        first_half,
        entry_low[1],
        block_low[1],
        exit_two_low,
        norm_params[1],
        head_params[5 * chans : 9 * chans],
        group,
    )
    tanh_two = jnp.tanh(out_two[..., : 2 * chans])
    scale_two = head_params[chans : 3 * chans] * tanh_two
    exp_two = jnp.exp(scale_two)
    latent = jnp.concatenate(
        [first_half, second_half * exp_two + out_two[..., 2 * chans :]], axis=3
    )
    logdet = logdet + jnp.concatenate([jnp.zeros_like(scale_two), scale_two], axis=3)
    neg_loglik = 0.5 * latent * latent + HALF_LOG_TAU - logdet - jacobian + LOG_LEVELS
    loss_part = jnp.sum(dim_mask * neg_loglik) / LOG_TWO
    grad_nll = dim_mask / (LOG_TWO * total_valid)
    grad_latent = grad_nll * latent
    grad_moved = grad_latent[..., 2 * chans :]
    grad_scale_two = grad_moved * second_half * exp_two - grad_nll[..., 2 * chans :]
    grad_raw_two = grad_scale_two * head_params[chans : 3 * chans] * (1.0 - tanh_two * tanh_two)
    grad_out_two = jnp.concatenate([grad_raw_two, grad_moved], axis=3)
    extra_two = jnp.concatenate(
        [jnp.sum(grad_scale_two * tanh_two, axis=(0, 1, 2)), jnp.sum(grad_out_two, axis=(0, 1, 2))]
    )
    entry_two, blocks_two, exit_two_grad, norms_two, grad_first_net = net_backward(
        grad_out_two,
        stored_two,
        entry_low[1],
        block_low[1],
        exit_two_low,
        norm_params[1],
        True,
        group,
    )
    grad_squeezed = jnp.concatenate(
        [grad_latent[..., : 2 * chans] + grad_first_net, grad_moved * exp_two], axis=3
    )
    grad_coupled = unsqueeze(grad_squeezed)
    grad_logdet = unsqueeze(-grad_nll)
    grad_scale_one = (1.0 - parity) * (grad_coupled * logits * exp_one + grad_logdet)
    grad_shift_one = (1.0 - parity) * grad_coupled
    grad_raw_one = grad_scale_one * head_params[0:chans] * (1.0 - tanh_one * tanh_one)
    grad_out_one = jnp.concatenate([grad_raw_one, grad_shift_one], axis=3)
    extra_one = jnp.concatenate(
        [jnp.sum(grad_scale_one * tanh_one, axis=(0, 1, 2)), jnp.sum(grad_out_one, axis=(0, 1, 2))]
    )
    entry_one, blocks_one, exit_one_grad, norms_one, unused_input = net_backward(
        grad_out_one,
        stored_one,
        entry_low[0],
        block_low[0],
        exit_one_low,
        norm_params[0],
        False,
        group,
    )
    norm_grad = jnp.stack([norms_one, norms_two])
    head_grad = jnp.concatenate(
        [extra_one[:chans], extra_two[: 2 * chans], extra_one[chans:], extra_two[2 * chans :]]
    )
    parts = [
        jnp.stack([entry_one, entry_two]),
        jnp.stack([blocks_one, blocks_two]),
        exit_one_grad,
        exit_two_grad,
        head_grad,
        loss_part[None],
    ]
    sizes = [part.size for part in parts]
    total = sum(sizes)
    flat = jnp.concatenate([part.reshape(-1) for part in parts] + [jnp.zeros((-total % 1024,), jnp.float32)])
    flat = group_sum(flat.reshape(-1, 128), group).reshape(-1)
    grads = []
    start = 0
    for part in parts:
        grads.append(flat[start : start + part.size].reshape(part.shape))
        start += part.size
    entry_grad, block_grad, exit_one_grad, exit_two_grad, head_grad, loss_total = grads
    entry_out = adamw(entry_conv, entry_first, entry_second, entry_grad, RATE_CONV)
    block_out = adamw(block_conv, block_first, block_second, block_grad, RATE_CONV)
    exit_a_out = adamw(exit_one, exit_one_first, exit_one_second, exit_one_grad, RATE_CONV)
    exit_b_out = adamw(exit_two, exit_two_first, exit_two_second, exit_two_grad, RATE_CONV)
    norm_out = adamw(norm_params, norm_first, norm_second, norm_grad, RATE_SMALL)
    head_out = adamw(head_params, head_first, head_second, head_grad, RATE_SMALL)
    return (
        (loss_total[0], total_valid)
        + entry_out
        + block_out
        + exit_a_out
        + exit_b_out
        + norm_out
        + head_out
    )


def solution(mesh):
    placed = (P("batch", "rows", None, None), P("batch", "rows", None)) + (P(),) * 18
    return jax.shard_map(body, mesh=mesh, in_specs=placed, out_specs=(P(),) * 26, check_vma=False)
```

```python
import functools
import math

import jax
import jax.numpy as jnp
import numpy as np
from jax import lax
from jax.experimental import pallas as pl
from jax.experimental.pallas import tpu as pltpu
from jax.sharding import PartitionSpec as P

STEP = 10
ALPHA = 0.05
NORM_EPS = 1e-05
BETA_ONE = 0.9
BETA_TWO = 0.999
ADAM_EPS = 1e-08
DECAY = 0.01
RATE_CONV = 1.0
RATE_SMALL = 10.0
LOG_TWO = math.log(2.0)
HALF_LOG_TAU = 0.5 * math.log(2.0 * math.pi)
LOG_LEVELS = math.log(256.0)
IMAGES = 16
BITS = (("batch", 1), ("rows", 1), ("rows", 2), ("batch", 2), ("batch", 4), ("batch", 8), ("batch", 16), ("batch", 32))
LOW = jnp.bfloat16
WIDE = jnp.float32


def axis_bits():
    return [bit for bit in BITS if bit[1] < lax.axis_size(bit[0])]


def group_bits(batch):
    bits = axis_bits()
    count = max(batch // IMAGES, 1).bit_length() - 1
    return bits[: min(count, len(bits))]


def swap(value, bit):
    axis, mask = bit
    return lax.ppermute(value, axis, [(i, i ^ mask) for i in range(lax.axis_size(axis))])


def side(bit):
    return (lax.axis_index(bit[0]) // bit[1]) % 2


def group_sum(value, bits):
    for bit in bits:
        value = jax.tree.map(lambda own: own + swap(own, bit), value)
    return value


def joined(own, other, mine, dim):
    first = jnp.where(mine == 0, own, other)
    second = jnp.where(mine == 0, other, own)
    return jnp.concatenate([first, second], axis=dim)


def distribute(cells, group):
    for bit in sorted(axis_bits(), key=lambda b: (b[0] != "rows", b[1])):
        mine = side(bit)
        dim = 0 if bit[0] == "rows" else 1
        if bit in group:
            if bit[0] == "batch":
                continue
            half = cells.shape[1] // 2
            away = lax.dynamic_slice_in_dim(cells, (1 - mine) * half, half, 1)
            cells = lax.dynamic_slice_in_dim(cells, mine * half, half, 1)
        else:
            away = cells
        cells = joined(cells, swap(away, bit), mine, dim)
    return cells


def merge_stats(both, count, group):
    for bit in group:
        other = swap(both, bit)
        gap = both[0] - other[0]
        both = jnp.stack([0.5 * (both[0] + other[0]), both[1] + other[1] + gap * gap * (0.5 * count)])
        count = 2 * count
    return both


def blockify(kernel):
    rows = np.stack([np.pad(kernel, ((q, 1 - q), (0, 0), (0, 0), (0, 0))) for q in range(2)], axis=3)
    return np.stack([np.pad(rows, ((0, 0), (s, 1 - s), (0, 0), (0, 0), (0, 0))) for s in range(2)], axis=4)


def turned(kernel):
    return np.flip(kernel, (0, 1)).transpose(0, 1, 3, 2)


def views(blocked):
    rest = blocked.shape[2:]
    split = blocked.reshape((2, 2, 2, 2) + rest)
    return split.transpose((0, 2, 1, 3) + tuple(range(4, 4 + len(rest)))).reshape((16,) + rest)


def mates(blocked):
    return np.flip(blocked.reshape(4, 2, 2, *blocked.shape[2:]), 2).reshape(blocked.shape)


def spread(values, axis):
    shape = values.shape
    cut = values.reshape(shape[:axis] + (2, 3) + shape[axis + 1 :])
    pad = [(0, 0)] * cut.ndim
    pad[axis + 1] = (0, 1)
    return np.pad(cut, pad).reshape(shape[:axis] + (8,) + shape[axis + 1 :])


def window_rows(weights):
    flat = weights.reshape(4, -1, 4)
    return np.pad(flat, ((0, 0), (0, 128 - flat.shape[1]), (0, 0))).reshape(512, 4)


def checker(odd):
    return ((np.arange(4)[:, None] + np.arange(4)[None, :]) % 2 == odd).reshape(4, 4, 1, 1)


def chosen(blocked, odd):
    both = np.where(checker(odd), blocked[:, :, :3], mates(blocked)[:, :, 3:])
    return window_rows(np.pad(both, ((0, 0), (0, 0), (0, 1), (0, 0))))


def numbered(channels, last):
    number = np.arange(1, 9 * channels + 1).reshape(3, 3, 1, channels)
    return number if last else number.transpose(0, 1, 3, 2)


def hot(numbers, count):
    return (numbers[..., None] == np.arange(1, count + 1)).astype(np.float32)


@functools.cache
def placements():
    odd = (np.arange(2)[:, None] + np.arange(2)[None, :]) % 2 == 1
    found = {}
    blocked = blockify(numbered(6, False)).reshape(4, 4, 6, 4)
    found["entry_one"] = hot(chosen(blocked, 0).T, 54)
    found["entry_two"] = hot(window_rows(spread(blocked, 2)).T, 54)
    blocked = views(blockify(turned(numbered(6, False))))
    lanes = spread(blocked.reshape(16, 2, 2, 6), 3).reshape(16, 2, 16)
    lanes = np.pad(lanes, ((0, 0), (0, 0), (0, 48))).reshape(16, 128)
    found["entry_two_turned"] = hot(lanes, 54).transpose(0, 2, 1)
    blocked = views(blockify(numbered(6, True))).reshape(16, 2, 2, 6)
    both = np.where(odd[None, :, :, None], blocked[..., :3], np.flip(blocked, 2)[..., 3:])
    lanes = np.pad(both, ((0, 0), (0, 0), (0, 0), (0, 1))).reshape(16, 2, 8)
    lanes = np.pad(lanes, ((0, 0), (0, 0), (0, 56))).reshape(16, 128)
    found["exit_one"] = hot(lanes, 54).transpose(0, 2, 1)
    blocked = blockify(turned(numbered(6, True))).reshape(4, 4, 6, 4)
    found["exit_one_turned"] = hot(chosen(blocked, 1).T, 54)
    blocked = views(blockify(numbered(12, True))).reshape(16, 2, 2, 2, 6)
    lanes = spread(blocked, 4).transpose(0, 1, 3, 2, 4).reshape(16, 4, 16)
    lanes = np.pad(lanes, ((0, 0), (0, 0), (0, 16))).reshape(16, 128)
    found["exit_two"] = hot(lanes, 108).transpose(0, 2, 1)
    blocked = blockify(turned(numbered(12, True))).reshape(4, 4, 12, 4)
    pair = [window_rows(spread(blocked[:, :, 6 * s : 6 * s + 6], 2)) for s in range(2)]
    found["exit_two_turned"] = hot(np.concatenate(pair).T, 108)
    number = np.arange(1, 28)

    def line(values, lanes):
        cut = np.pad(values.reshape(-1, 3), ((0, 0), (0, 1))).reshape(-1)
        return np.tile(cut, 128 // lanes)

    pick = (np.arange(128) // 4) % 2
    scale, shift = line(number[9:12], 4), line(number[12:15], 4)
    lines = [
        line(number[0:3], 4),
        np.where(pick == 1, scale, shift),
        np.where(pick == 0, scale, shift),
        line(number[3:9], 8),
        line(number[15:21], 8),
        line(number[21:27], 8),
        np.zeros(128, int),
        np.zeros(128, int),
    ]
    found["head"] = hot(np.stack(lines), 27).transpose(2, 0, 1).reshape(27, 1024)
    return found


def exact_dot(left, right, dims):
    return lax.dot_general(
        left, right, (dims, ((), ())), precision=lax.Precision.HIGHEST, preferred_element_type=WIDE
    )


def place_rows(place_ref, kernel, o_ref):
    for p in range(4):
        part = jnp.dot(place_ref[p], kernel, preferred_element_type=WIDE)
        o_ref[:, 64 * p : 64 * p + 64] = part.astype(LOW)


def place_lanes(place_ref, kernel, o_ref):
    for p in range(16):
        part = lax.dot_general(kernel, place_ref[p], (((0,), (0,)), ((), ())), preferred_element_type=WIDE)
        o_ref[64 * p : 64 * p + 64] = part.astype(LOW)


def build_small(entry_ref, one_ref, two_ref, norm_ref, head_ref, *refs):
    places = refs[:8]
    entry_one_o, entry_two_o, entry_turned_o, one_o, one_turned_o, two_o, two_turned_o, par_o, line_o = refs[8:]
    entry_one = entry_ref[0].astype(LOW)
    entry_two = entry_ref[1].astype(LOW)
    exit_one = one_ref[...].astype(LOW)
    exit_two = two_ref[...].astype(LOW)
    place_rows(places[0], entry_one, entry_one_o)
    place_rows(places[1], entry_two, entry_two_o)
    place_lanes(places[2], entry_two, entry_turned_o)
    place_lanes(places[3], exit_one, one_o)
    place_rows(places[4], exit_one, one_turned_o)
    place_lanes(places[5], exit_two, two_o)
    place_rows(places[6], exit_two, two_turned_o)
    for spot in range(4):
        par_o[:, 64 * spot : 64 * spot + 64] = norm_ref[...]
    lines = exact_dot(head_ref[...], places[7][...], ((1,), (0,)))
    for spot in range(8):
        line_o[spot : spot + 1] = lines[:, 128 * spot : 128 * spot + 128]


def build_blocks(kernel_ref, o_ref):
    count = kernel_ref.shape[0]

    @pl.loop(0, count)
    def _(k):
        tap = [kernel_ref[k, t].astype(LOW) for t in range(9)]
        zero = jnp.zeros((64, 64), LOW)
        for r in range(4):
            for c in range(4):
                parts = [
                    tap[3 * (r - q) + c - s] if 0 <= r - q < 3 and 0 <= c - s < 3 else zero
                    for q in range(2)
                    for s in range(2)
                ]
                row = (((r // 2) * 2 + c // 2) * 4 + (r % 2) * 2 + c % 2) * 64
                o_ref[k, row : row + 64] = jnp.concatenate(parts, axis=1)


def groups(count):
    head = [(0, 1)] if count % 8 else []
    return head + [(start, 8) for start in range(count % 8, count, 8)]


def lane_fold(value):
    value = value + pltpu.roll(value, 128, 1)
    return value + pltpu.roll(value, 64, 1)


def total_rows(value):
    return jnp.sum(value, axis=0, keepdims=True)


def edge_masks(odd, count):
    if not odd:
        return None, None
    lane = lax.broadcasted_iota(jnp.int32, (count, 1, 256), 2)
    spot = lax.broadcasted_iota(jnp.int32, (count, 1, 256), 0)
    low = (lane // 64) % 2 == 0
    columns = jnp.where((spot == 0) & low | (spot == count - 1) & ~low, 0.0, 1.0)
    row_low = lax.broadcasted_iota(jnp.int32, (1, 1, 256), 2) < 128

    def row(i):
        return jnp.where((i == 0) & row_low | (i == count - 1) & ~row_low, 0.0, 1.0)

    return columns, row


def masked(value, masks, i):
    columns, row = masks
    if columns is None:
        return value
    return value * (columns * row(i))


def norm_lines(st_ref, par_ref, cells):
    mean = st_ref[0:1, :]
    inv = lax.rsqrt(st_ref[1:2, :] / cells + NORM_EPS)
    return mean, inv, par_ref[0:1, :], par_ref[1:2, :]


def clear_border(ref, count):
    ref[0] = jnp.zeros(ref.shape[1:], ref.dtype)
    ref[count + 1] = jnp.zeros(ref.shape[1:], ref.dtype)
    ref[:, 0] = jnp.zeros((ref.shape[0],) + ref.shape[2:], ref.dtype)
    ref[:, count + 1] = jnp.zeros((ref.shape[0],) + ref.shape[2:], ref.dtype)


def activate(v_ref, st_ref, par_ref, a_ref, odd, cells):
    count, n = v_ref.shape[0], v_ref.shape[2]
    pad = 0 if odd else 1
    mean, inv, gain, shift = norm_lines(st_ref, par_ref, cells)
    scale = 0.5 * gain * inv
    offset = 0.5 * shift - mean * scale
    masks = edge_masks(odd, count)
    if pad:
        clear_border(a_ref, count)

    @pl.loop(0, count)
    def _(i):
        half = v_ref[i] * scale + offset
        act = half + half * jnp.tanh(half)
        a_ref[i + pad, pad : pad + count] = masked(act, masks, i).astype(LOW)


def four_views(ref, start, size, count):
    n = ref.shape[2]
    return [
        ref[start + vi : start + vi + size, vj : vj + count].reshape(size * count * n, 256)
        for vi in range(2)
        for vj in range(2)
    ]


def column_stats(o_ref, st_ref, odd, shift):
    count, n = o_ref.shape[0], o_ref.shape[2]
    masks = edge_masks(odd, count)

    def step(i, sums):
        gap = masked(o_ref[i] - shift, masks, i)
        rows = gap.reshape(-1, 8, 256)
        return sums[0] + jnp.sum(rows, 0), sums[1] + jnp.sum(rows * rows, 0)

    zero = jnp.zeros((8, 256), WIDE)
    first, second = lax.fori_loop(0, count, step, (zero, zero))
    cells = n * (count - 1 if odd else count) ** 2 * 4
    first = lane_fold(total_rows(first)) / cells
    second = lane_fold(total_rows(second))
    st_ref[0:1, :] = shift + first
    st_ref[1:2, :] = second - first * first * cells


def near_mean(o_ref):
    count, n = o_ref.shape[0], o_ref.shape[2]
    row = jnp.sum(o_ref[count // 2, 1 : count - 1].reshape(-1, 256), 0, keepdims=True)
    return lane_fold(row) / (4 * n * (count - 2))


def mid_forward(odd, cells, residual, *refs):
    st_ref, par_ref, v_ref, w_ref = refs[:4]
    res_ref = refs[4] if residual else None
    o_ref, out_st_ref, far_ref, a_ref, sem = refs[-5:]
    count = o_ref.shape[0]
    n = v_ref.shape[2]
    activate(v_ref, st_ref, par_ref, a_ref, odd, cells)
    copies = []
    for index, (start, size) in enumerate(groups(count)):
        left = jnp.concatenate(four_views(a_ref, start, size, count), axis=1)
        value = jnp.dot(left, w_ref[...], preferred_element_type=WIDE).reshape(size, count, n, 256)
        if residual:
            value = value + res_ref[start : start + size]
        o_ref[start : start + size] = value
        copies.append(
            pltpu.make_async_copy(
                o_ref.at[start : start + size], far_ref.at[start : start + size], sem.at[index]
            )
        )
        copies[-1].start()
    column_stats(o_ref, out_st_ref, not odd, near_mean(o_ref))
    for copy in copies:
        copy.wait()


def rolled(value, shift):
    shift = shift % 128
    return value if shift == 0 else pltpu.roll(value, shift, 1)


def window_left(x_ref, spot, width):
    count = x_ref.shape[0] // 2 - 1
    n = x_ref.shape[1]
    columns = 128 // width
    first = 2 * spot - 2
    value = rolled(x_ref[...].reshape(-1, 128), -width * first).reshape(count + 1, 2, n, 128)
    if first < 0 or first + 4 > columns:
        column = lax.broadcasted_iota(jnp.int32, (count + 1, 2, n, 128), 3) // width + first
        value = jnp.where((column >= 0) & (column < columns), value, jnp.zeros_like(value))
    return jnp.concatenate(
        [value[r // 2 : r // 2 + count, r % 2].reshape(count * n, 128) for r in range(4)], axis=1
    ).astype(LOW)


def window_forward(width, x_ref, w_ref, o_ref, st_ref, far_ref, sem):
    count, n = o_ref.shape[0], o_ref.shape[2]
    for spot in range(count):
        left = window_left(x_ref, spot, width)
        value = jnp.dot(left, w_ref[...], preferred_element_type=WIDE)
        o_ref[:, spot] = value.reshape(count, n, 256)
    copy = pltpu.make_async_copy(o_ref, far_ref, sem.at[0])
    copy.start()
    column_stats(o_ref, st_ref, True, near_mean(o_ref))
    copy.wait()


def to_rows(value_ref, step, items, store):
    count, n = value_ref.shape[0], value_ref.shape[2]
    room = 128 // items
    per = count // items
    sums = []
    for part in range(items):
        total = None
        for spot in range(part * per, part * per + per):
            moved = rolled(value_ref[:, spot].reshape(-1, 128), step * spot)
            total = moved if total is None else total + moved
        sums.append(total)
    lane = lax.broadcasted_iota(jnp.int32, (count * n, 128), 1) // room
    for item in range(items):
        value = sums[0]
        for part in range(1, items):
            value = jnp.where(lane == (item + part) % items, sums[part], value)
        store(item, rolled(value, -room * item).reshape(count, n, 128))


def exit_forward(cells, step, items, st_ref, par_ref, v_ref, w_ref, o_ref, a_ref, value_ref):
    count = v_ref.shape[0] - 1
    n = v_ref.shape[2]
    activate(v_ref, st_ref, par_ref, a_ref, True, cells)
    for start, size in groups(count):
        left = jnp.concatenate(four_views(a_ref, start, size, count), axis=1)
        value = jnp.dot(left, w_ref[...], preferred_element_type=WIDE)
        value_ref[start : start + size] = value.reshape(size, count, n, 128)

    def store(item, value):
        o_ref[item] = value

    to_rows(value_ref, step, items, store)


def activation_grads(g_ref, v_ref, st_ref, par_ref, a_ref, sum_ref, odd, cells):
    count = v_ref.shape[0]
    pad = 0 if odd else 1
    mean, inv, gain, shift = norm_lines(st_ref, par_ref, cells)
    offset = -mean * inv
    masks = edge_masks(odd, count)
    if pad:
        clear_border(a_ref, count)

    def step(i, sums):
        normed = v_ref[i] * inv + offset
        half = normed * (0.5 * gain) + 0.5 * shift
        bend = jnp.tanh(half)
        a_ref[i + pad, pad : pad + count] = masked(half + half * bend, masks, i).astype(LOW)
        grad = masked(g_ref[i] * ((1.0 + bend) * (1.0 + half * (1.0 - bend))), masks, i)
        g_ref[i] = grad
        rows = grad.reshape(-1, 8, 256)
        other = (grad * normed).reshape(-1, 8, 256)
        return sums[0] + jnp.sum(rows, 0), sums[1] + jnp.sum(other, 0)

    zero = jnp.zeros((8, 256), WIDE)
    first, second = lax.fori_loop(0, count, step, (zero, zero))
    sum_ref[0:1, :] = lane_fold(total_rows(first))
    sum_ref[1:2, :] = lane_fold(total_rows(second))


def norm_input_grads(sum_ref, st_ref, par_ref, g_ref, v_ref, res_ref, low_ref, keep_ref, odd, cells):
    count = v_ref.shape[0]
    pad = 0 if odd else 1
    mean, inv, gain, shift = norm_lines(st_ref, par_ref, cells)
    scale = 0.5 * gain * inv
    slope = -scale * inv * sum_ref[1:2, :] / cells
    offset = -scale * sum_ref[0:1, :] / cells - slope * mean
    masks = edge_masks(odd, count)
    if pad:
        clear_border(low_ref, count)

    @pl.loop(0, count)
    def _(i):
        grad = masked(g_ref[i] * scale + v_ref[i] * slope + offset, masks, i)
        if res_ref is not None:
            grad = grad + res_ref[i]
        if keep_ref is not None:
            keep_ref[i] = grad
        low_ref[i + pad, pad : pad + count] = grad.astype(LOW)


def mid_backward(odd, cells, residual, keep, *refs):
    refs = list(refs)
    sum_ref, st_ref, par_ref, g_ref, v_ref, w_ref, in_st_ref, in_par_ref, in_v_ref = refs[:9]
    rest = refs[9:]
    res_ref = rest.pop(0) if residual else None
    low_ref, out_g_ref, a_ref, out_sum_ref, near_ref = rest[:5]
    keep_ref = rest[5] if keep else None
    sem = rest[-1]
    copy = pltpu.make_async_copy(in_v_ref, near_ref, sem.at[0])
    copy.start()
    norm_input_grads(sum_ref, st_ref, par_ref, g_ref, v_ref, res_ref, low_ref, keep_ref, odd, cells)
    count, n = in_v_ref.shape[0], in_v_ref.shape[2]
    for start, size in groups(count):
        value = None
        for spot, left in enumerate(four_views(low_ref, start, size, count)):
            right = w_ref[256 * (3 - spot) : 256 * (4 - spot)]
            part = lax.dot_general(left, right, (((1,), (1,)), ((), ())), preferred_element_type=WIDE)
            value = part if value is None else value + part
        out_g_ref[start : start + size] = value.reshape(size, count, n, 256)
    copy.wait()
    activation_grads(out_g_ref, near_ref, in_st_ref, in_par_ref, a_ref, out_sum_ref, not odd, cells)


def window_backward(width, arrays, cells, *refs):
    d_refs = refs[:arrays]
    w_ref, st_ref, par_ref, v_ref, g_ref, a_ref, sum_ref, near_ref, sem = refs[arrays:]
    count, n = v_ref.shape[0], v_ref.shape[2]
    copy = pltpu.make_async_copy(v_ref, near_ref, sem.at[0])
    copy.start()
    for spot in range(count):
        left = jnp.concatenate([window_left(d_ref, spot, width) for d_ref in d_refs], axis=1)
        value = jnp.dot(left, w_ref[...], preferred_element_type=WIDE)
        g_ref[:, spot] = value.reshape(count, n, 256)
    copy.wait()
    activation_grads(g_ref, near_ref, st_ref, par_ref, a_ref, sum_ref, True, cells)


def entry_backward(cells, inputs, *refs):
    sum_ref, st_ref, par_ref, g_ref, v_ref, res_ref = refs[:6]
    low_ref = refs[7] if inputs else refs[6]
    norm_input_grads(sum_ref, st_ref, par_ref, g_ref, v_ref, res_ref, low_ref, None, True, cells)
    if inputs:
        w_ref, low_ref, o_ref, value_ref = refs[6:]
        count = v_ref.shape[0] - 1
        n = v_ref.shape[2]
        for start, size in groups(count):
            left = jnp.concatenate(four_views(low_ref, start, size, count), axis=1)
            value = jnp.dot(left, w_ref[...], preferred_element_type=WIDE)
            value_ref[start : start + size] = value.reshape(size, count, n, 128)

        def store(item, value):
            o_ref[item] = value

        to_rows(value_ref, 16, 2, store)


def block_weight_grad(odd, low_ref, a_ref, o_ref, acc_ref):
    pad = 0 if odd else 1
    count = low_ref.shape[0] - 2 * pad
    n = low_ref.shape[2]
    for index, (start, size) in enumerate(groups(count)):
        grad = low_ref[start + pad : start + pad + size, pad : pad + count].reshape(size * count * n, 256)
        right = jnp.concatenate(four_views(a_ref, start, size, count), axis=1)
        part = lax.dot_general(grad, right, (((0,), (0,)), ((), ())), preferred_element_type=WIDE)
        if index == 0:
            acc_ref[...] = part
        else:
            acc_ref[...] += part
    for dy in range(3):
        for dx in range(3):
            total = None
            for q in range(2):
                for s in range(2):
                    r, c = dy + q, dx + s
                    lane = ((r // 2) * 2 + c // 2) * 256 + ((r % 2) * 2 + c % 2) * 64
                    part = acc_ref[(2 * q + s) * 64 : (2 * q + s) * 64 + 64, lane : lane + 64]
                    total = part if total is None else total + part
            o_ref[dy, dx] = total.T


def window_weight_grad(width, arrays, *refs):
    x_refs = refs[:arrays]
    b_ref, place_ref, o_ref, acc_ref = refs[arrays:]
    count, n = b_ref.shape[0], b_ref.shape[2]
    for spot in range(count):
        right = jnp.concatenate([window_left(x_ref, spot, width) for x_ref in x_refs], axis=1)
        left = b_ref[:, spot].reshape(count * n, 256)
        part = lax.dot_general(left, right, (((0,), (0,)), ((), ())), preferred_element_type=WIDE)
        if spot == 0:
            acc_ref[...] = part
        else:
            acc_ref[...] += part
    total = None
    for p in range(4):
        part = exact_dot(place_ref[p].astype(WIDE), acc_ref[64 * p : 64 * p + 64], ((0,), (1,)))
        total = part if total is None else total + part
    o_ref[...] = total


def lane_ids(shape):
    return lax.broadcasted_iota(jnp.int32, shape, len(shape) - 1)


def flat_roll(value, shift):
    return rolled(value.reshape(-1, 128), shift).reshape(value.shape)


def valid_lanes(cells):
    held = jnp.where(lane_ids(cells.shape) % 4 == 3, cells, 0.0)
    return flat_roll(held, -1) + flat_roll(held, -2) + flat_roll(held, -3)


def pad_rows(x_ref, values):
    rows, n = values.shape[0], values.shape[1]
    x_ref[0:2] = jnp.zeros((2, n, 128), x_ref.dtype)
    x_ref[2 : 2 + rows] = values.astype(x_ref.dtype)
    x_ref[2 + rows :] = jnp.zeros((2, n, 128), x_ref.dtype)


def column_line(value):
    return jnp.sum(value.reshape(-1, 128), axis=0, keepdims=True)


def checks(shape):
    lane = lane_ids(shape)
    row = lax.broadcasted_iota(jnp.int32, shape, 0)
    return ((row + lane // 4) % 2 == 1) & (lane % 4 != 3)


def prepare(cells_ref, x_ref, logits_ref, sum_ref):
    cells = cells_ref[...]
    lane = lane_ids(cells.shape)
    channel = lane % 4 != 3
    valid = valid_lanes(cells)
    prob = ALPHA + (1.0 - 2.0 * ALPHA) * (cells / 256.0)
    log_in = jnp.log(prob)
    log_out = jnp.log(1.0 - prob)
    logits = jnp.where(channel, log_in - log_out, 0.0)
    jacobian = math.log(1.0 - 2.0 * ALPHA) - log_in - log_out
    logits_ref[...] = logits
    sum_ref[0:1] = column_line(valid)
    sum_ref[1:2] = column_line(valid * (HALF_LOG_TAU + LOG_LEVELS - jacobian))
    odd = checks(cells.shape)
    pad_rows(x_ref, jnp.where(odd, 1.0, logits))


def couple(line_ref, raw_ref, logits_ref, cells_ref, o_ref, bend_ref, sum_ref):
    logits = logits_ref[...]
    valid = valid_lanes(cells_ref[...])
    gain = line_ref[0:1].reshape(1, 1, 128)
    total = jnp.zeros((1, 128), WIDE)
    for q in range(2):
        raw = raw_ref[q] + line_ref[1 + q : 2 + q].reshape(1, 1, 128)
        own = logits_ref[pl.ds(q, raw.shape[0], 2)]
        cells = cells_ref[pl.ds(q, raw.shape[0], 2)]
        lane = lane_ids(raw.shape)
        odd = ((q + lane // 4) % 2 == 1) & (lane % 4 != 3)
        shift = flat_roll(raw, 4 if q == 0 else -4)
        bend = jnp.where(odd, jnp.tanh(raw), 0.0)
        scale = gain * bend
        coupled = jnp.where(odd, own * jnp.exp(scale) + shift, own)
        bend_ref[q] = bend
        total = total - column_line(valid_lanes(cells) * scale)
        o_ref[pl.ds(q, raw.shape[0], 2)] = jnp.where(lane % 4 == 3, cells, coupled)
    sum_ref[...] = total


def enter_two(coupled_ref, x_ref):
    value = coupled_ref[pl.ds(0, coupled_ref.shape[0] // 2, 2)]
    pad_rows(x_ref, jnp.where(lane_ids(value.shape) % 4 == 3, 0.0, value))


def losses(line_ref, unit_ref, raw_ref, coupled_ref, scale_d_ref, shift_d_ref, grad_ref, sum_ref):
    half = coupled_ref.shape[0] // 2
    shape = (half, coupled_ref.shape[1], 128)
    channel = lane_ids(shape) % 4 != 3
    top = coupled_ref[pl.ds(0, half, 2)]
    low = coupled_ref[pl.ds(1, half, 2)]
    top_valid = valid_lanes(top)
    low_valid = valid_lanes(low)
    top = jnp.where(channel, top, 0.0)
    low = jnp.where(channel, low, 0.0)

    def rows(item):
        pair = jnp.stack([raw_ref[item], raw_ref[2 + item]], axis=1)
        return pair.reshape(shape) + line_ref[4 + item : 5 + item].reshape(1, 1, 128)

    gain = line_ref[3:4].reshape(1, 1, 128)
    unit = unit_ref[...].reshape(1, 1, 128)
    bend = jnp.tanh(rows(0))
    scale = gain * bend
    grow = jnp.exp(scale)
    latent = jnp.where(channel, low * grow + rows(1), 0.0)
    sum_ref[0:1] = column_line(top_valid * (0.5 * top * top) + low_valid * (0.5 * latent * latent - scale))
    moved = low_valid * unit * latent
    grad_scale = moved * low * grow - low_valid * unit
    raw_grad = grad_scale * gain * (1.0 - bend * bend)
    sum_ref[1:2] = column_line(grad_scale * bend)
    sum_ref[2:3] = column_line(raw_grad)
    sum_ref[3:4] = column_line(moved)
    pad_rows(scale_d_ref, raw_grad)
    pad_rows(shift_d_ref, moved)
    grad_ref[pl.ds(0, half, 2)] = top_valid * unit * top
    grad_ref[pl.ds(1, half, 2)] = moved * grow


def uncouple(line_ref, unit_ref, entry_ref, grad_ref, logits_ref, bend_ref, cells_ref, d_ref, sum_ref):
    half = logits_ref.shape[0] // 2
    n = logits_ref.shape[1]
    gain = line_ref[0:1].reshape(1, 1, 128)
    unit = unit_ref[...].reshape(1, 1, 128)
    lines = [jnp.zeros((1, 128), WIDE)] * 3
    d_ref[0:2] = jnp.zeros((2, n, 128), d_ref.dtype)
    d_ref[2 * half + 2 :] = jnp.zeros((d_ref.shape[0] - 2 * half - 2, n, 128), d_ref.dtype)
    for q in range(2):
        grad = grad_ref[pl.ds(q, half, 2)]
        if q == 0:
            grad = grad + jnp.stack([entry_ref[0], entry_ref[1]], axis=1).reshape(half, n, 128)
        own = logits_ref[pl.ds(q, half, 2)]
        valid = valid_lanes(cells_ref[pl.ds(q, half, 2)])
        bend = bend_ref[q]
        lane = lane_ids(grad.shape)
        odd = ((q + lane // 4) % 2 == 1) & (lane % 4 != 3)
        grad = jnp.where(odd, grad, 0.0)
        grad_scale = jnp.where(odd, grad * own * jnp.exp(gain * bend) - valid * unit, 0.0)
        raw_grad = grad_scale * gain * (1.0 - bend * bend)
        lines[0] = lines[0] + column_line(grad_scale * bend)
        lines[1] = lines[1] + column_line(raw_grad)
        lines[2] = lines[2] + column_line(grad)
        value = raw_grad + flat_roll(grad, -4 if q == 0 else 4)
        d_ref[pl.ds(2 + q, half, 2)] = value.astype(d_ref.dtype)
    for spot in range(3):
        sum_ref[spot : spot + 1] = lines[spot]


def call(kernel, outs, args, name, scratch=(), limit=12, far_in=(), far_out=(), sems=0):
    spaces = [pltpu.HBM if spot in far_in else pltpu.VMEM for spot in range(len(args))]
    out_spaces = [pltpu.HBM if spot in far_out else pltpu.VMEM for spot in range(len(outs))]
    held = [pltpu.VMEM(shape, dtype) for shape, dtype in scratch]
    if sems:
        held.append(pltpu.SemaphoreType.DMA((sems,)))
    return pl.pallas_call(
        kernel,
        out_shape=[space(shape, dtype) for space, (shape, dtype) in zip(out_spaces, outs)],
        in_specs=[pl.BlockSpec(memory_space=space) for space in spaces],
        out_specs=[pl.BlockSpec(memory_space=space) for space in out_spaces],
        scratch_shapes=held,
        compiler_params=pltpu.CompilerParams(vmem_limit_bytes=limit * 2**20),
        name=name,
    )(*args)


class Net:
    def __init__(self, name, blocks, n, width, group, total, pars, weights):
        self.name = name
        self.even = blocks
        self.odd = blocks + 1
        self.n = n
        self.width = width
        self.group = group
        self.cells = float(total)
        self.own = float(n * blocks * blocks * 4)
        self.pars = pars
        self.weights = weights
        self.values = []
        self.far = []
        self.stats = []

    def shape(self, odd, padded=False):
        count = self.odd if odd else self.even
        pad = 2 if padded and not odd else 0
        return (count + pad, count + pad, self.n, 256)

    def keep(self, value, stats, far):
        self.values.append(value)
        self.far.append(far)
        self.stats.append(merge_stats(stats, self.own, self.group))

    def forward(self, x, entry, exit_weights, items):
        value, stats, far = call(
            functools.partial(window_forward, self.width),
            [(self.shape(True), WIDE), ((2, 256), WIDE), (self.shape(True), WIDE)],
            [x, entry],
            self.name + "_entry",
            far_out=(2,),
            sems=1,
        )
        self.keep(value, stats, far)
        for index in range(4):
            odd = index % 2 == 0
            residual = [self.values[index - 1]] if not odd else []
            value, stats, far = call(
                functools.partial(mid_forward, odd, self.cells, not odd),
                [(self.shape(not odd), WIDE), ((2, 256), WIDE), (self.shape(not odd), WIDE)],
                [self.stats[index], self.pars[index], self.values[index], self.weights[index]] + residual,
                self.name + "_forward",
                [(self.shape(odd, True), LOW)],
                far_out=(2,),
                sems=len(groups(self.odd)),
            )
            self.keep(value, stats, far)
        return call(
            functools.partial(exit_forward, self.cells, 2 * self.width, items),
            [((items, self.even, self.n, 128), WIDE)],
            [self.stats[4], self.pars[4], self.values[4], exit_weights],
            self.name + "_exit",
            [(self.shape(True), LOW), ((self.even, self.even, self.n, 128), WIDE)],
        )[0]

    def backward(self, grads, exit_turned, exit_place, x, entry_turned, entry_place):
        arrays = len(grads)
        g, act, sums, near = call(
            functools.partial(window_backward, self.width, arrays, self.cells),
            [(self.shape(True), WIDE), (self.shape(True), LOW), ((2, 256), WIDE), (self.shape(True), WIDE)],
            list(grads) + [exit_turned, self.stats[4], self.pars[4], self.far[4]],
            self.name + "_exit_back",
            far_in=(arrays + 3,),
            sems=1,
        )
        exit_grad = call(
            functools.partial(window_weight_grad, self.width, arrays),
            [((exit_place.shape[2], 64), WIDE)],
            list(grads) + [act, exit_place],
            self.name + "_exit_weights",
            [((256, 512 * arrays), WIDE)],
        )[0]
        sums = group_sum(sums, self.group)
        norm_grads = [None] * 5
        block_grads = [None] * 4
        norm_grads[4] = sums
        hidden = None
        for index in reversed(range(4)):
            odd = index % 2 == 1
            residual = [hidden] if odd and hidden is not None else []
            outs = [
                (self.shape(odd, True), LOW),
                (self.shape(not odd), WIDE),
                (self.shape(not odd, True), LOW),
                ((2, 256), WIDE),
                (self.shape(not odd), WIDE),
            ]
            if odd:
                outs.append((self.shape(True), WIDE))
            results = call(
                functools.partial(mid_backward, odd, self.cells, bool(residual), odd),
                outs,
                [
                    sums,
                    self.stats[index + 1],
                    self.pars[index + 1],
                    g,
                    near,
                    self.weights[index],
                    self.stats[index],
                    self.pars[index],
                    self.far[index],
                ]
                + residual,
                self.name + "_back",
                far_in=(8,),
                sems=1,
            )
            low, g, act, sums, near = results[:5]
            if odd:
                hidden = results[5]
            block_grads[index] = call(
                functools.partial(block_weight_grad, odd),
                [((3, 3, 64, 64), WIDE)],
                [low, act],
                self.name + "_weights",
                [((256, 1024), WIDE)],
            )[0]
            sums = group_sum(sums, self.group)
            norm_grads[index] = sums
        args = [sums, self.stats[0], self.pars[0], g, near, hidden]
        outs = [(self.shape(True), LOW)]
        scratch = []
        if entry_turned is not None:
            args.append(entry_turned)
            outs.append(((2, self.even, self.n, 128), WIDE))
            scratch.append(((self.even, self.even, self.n, 128), WIDE))
        results = call(
            functools.partial(entry_backward, self.cells, entry_turned is not None),
            outs,
            args,
            self.name + "_entry_back",
            scratch,
        )
        entry_grad = call(
            functools.partial(window_weight_grad, self.width, 1),
            [((54, 64), WIDE)],
            [x, results[0], entry_place],
            self.name + "_entry_weights",
            [((256, 512), WIDE)],
        )[0]
        norms = jnp.stack([jnp.stack([0.5 * pair[1, :64], 0.5 * pair[0, :64]]) for pair in norm_grads])
        return entry_grad, block_grads, exit_grad, norms, (results[1] if entry_turned is not None else None)


def adamw(master, first, second, grad, rate):
    first_new = BETA_ONE * first + (1.0 - BETA_ONE) * grad
    second_new = BETA_TWO * second + (1.0 - BETA_TWO) * grad * grad
    direction = (
        first_new
        / (1.0 - BETA_ONE**STEP)
        / (jnp.sqrt(second_new / (1.0 - BETA_TWO**STEP)) + ADAM_EPS)
    )
    master_new = master - rate * (direction + DECAY * master)
    return (master_new, first_new, second_new, master_new.astype(jnp.bfloat16))


def body(
    pixels,
    valid,
    entry_conv,
    entry_first,
    entry_second,
    block_conv,
    block_first,
    block_second,
    exit_one,
    exit_one_first,
    exit_one_second,
    exit_two,
    exit_two_first,
    exit_two_second,
    norm_params,
    norm_first,
    norm_second,
    head_params,
    head_first,
    head_second,
):
    batch = pixels.shape[0] * lax.axis_size("batch")
    height = pixels.shape[1] * lax.axis_size("rows")
    group = group_bits(batch)
    small = group[:-1]
    last = group[-1]
    own = batch >> len(group)
    wide = 2 * own
    cells = jnp.concatenate([pixels, valid[..., None].astype(WIDE)], axis=3)
    cells = cells.reshape(pixels.shape[0], pixels.shape[1], 128).transpose(1, 0, 2)
    cells = distribute(cells, group)

    place = placements()
    small_places = [
        jnp.asarray(place[key], LOW)
        for key in (
            "entry_one",
            "entry_two",
            "entry_two_turned",
            "exit_one",
            "exit_one_turned",
            "exit_two",
            "exit_two_turned",
        )
    ]
    (
        entry_one_w,
        entry_two_w,
        entry_turned_w,
        exit_one_w,
        exit_one_turned_w,
        exit_two_w,
        exit_two_turned_w,
        par_lines,
        head_lines,
    ) = call(
        build_small,
        [
            ((512, 256), LOW),
            ((512, 256), LOW),
            ((1024, 128), LOW),
            ((1024, 128), LOW),
            ((512, 256), LOW),
            ((1024, 128), LOW),
            ((1024, 256), LOW),
            ((20, 256), WIDE),
            ((8, 128), WIDE),
        ],
        [
            entry_conv.reshape(2, 54, 64),
            exit_one.transpose(0, 1, 3, 2).reshape(54, 64),
            exit_two.transpose(0, 1, 3, 2).reshape(108, 64),
            norm_params.reshape(20, 64),
            head_params[None],
        ]
        + small_places
        + [jnp.asarray(place["head"])],
        "build_small",
    )
    blocks = call(build_blocks, [((8, 1024, 256), LOW)], [block_conv.reshape(8, 9, 64, 64)], "build_blocks")[0]
    weights = [[blocks[4 * j + k] for k in range(4)] for j in range(2)]
    pars = [[par_lines[10 * j + 2 * k : 10 * j + 2 * k + 2] for k in range(5)] for j in range(2)]

    one = Net("one", height // 2, own, 4, group, batch * height * height, pars[0], weights[0])
    two = Net("two", height // 4, wide, 8, small, batch * (height // 2) ** 2, pars[1], weights[1])

    rows = height
    x_one, logits, first_sums = call(
        prepare,
        [((rows + 4, own, 128), WIDE), ((rows, own, 128), WIDE), ((2, 128), WIDE)],
        [cells],
        "prepare",
    )
    total_valid = group_sum(jnp.sum(first_sums[0])[None], group)[0]
    raw_one = one.forward(x_one, entry_one_w, exit_one_w, 2)
    coupled, bend_one, couple_sums = call(
        couple,
        [((rows, own, 128), WIDE), ((2, rows // 2, own, 128), WIDE), ((1, 128), WIDE)],
        [head_lines, raw_one, logits, cells],
        "couple",
    )
    coupled = joined(coupled, swap(coupled, last), side(last), 1)
    x_two = call(enter_two, [((rows // 2 + 4, wide, 128), WIDE)], [coupled], "enter_two")[0]
    raw_two = two.forward(x_two, entry_two_w, exit_two_w, 4)
    unit = jnp.broadcast_to(1.0 / (LOG_TWO * total_valid), (1, 128))
    scale_d, shift_d, grad_coupled, loss_sums = call(
        losses,
        [
            ((rows // 2 + 4, wide, 128), WIDE),
            ((rows // 2 + 4, wide, 128), WIDE),
            ((rows, wide, 128), WIDE),
            ((4, 128), WIDE),
        ],
        [
            head_lines,
            unit,
            raw_two,
            coupled,
        ],
        "losses",
    )
    entry_two, blocks_two, exit_two_part, norms_two, grad_first = two.backward(
        [scale_d, shift_d], exit_two_turned_w, small_places[6], x_two, entry_turned_w, small_places[1]
    )
    mine = side(last) * own
    grad_first = lax.dynamic_slice_in_dim(grad_first, mine, own, 2)
    grad_coupled = lax.dynamic_slice_in_dim(grad_coupled, mine, own, 1)
    one_d, one_sums = call(
        uncouple,
        [((rows + 4, own, 128), WIDE), ((3, 128), WIDE)],
        [head_lines, unit, grad_first, grad_coupled, logits, bend_one, cells],
        "uncouple",
    )
    entry_one, blocks_one, exit_one_part, norms_one, unused = one.backward(
        [one_d], exit_one_turned_w, small_places[4], x_one, None, small_places[0]
    )

    lines_one = jnp.sum(one_sums.reshape(3, 32, 4), axis=1)[:, :3]
    lines_two = jnp.sum(loss_sums.reshape(4, 16, 2, 4), axis=1)[..., :3].reshape(4, 6)
    loss_one = jnp.sum(first_sums[1]) + jnp.sum(couple_sums)
    blocks_two = [group_sum(part, small) for part in blocks_two]
    blocks_one = [group_sum(part, group) for part in blocks_one]
    entry_two, exit_two_part, sums_two = group_sum([entry_two, exit_two_part, lines_two], small)
    sums_one, loss_one = group_sum([lines_one, loss_one[None]], group)
    exit_one_part = group_sum(exit_one_part, group)
    entry_one = group_sum(entry_one, group)
    loss_total = (jnp.sum(sums_two[0]) + loss_one[0]) / LOG_TWO
    entry_grad = jnp.stack([entry_one, entry_two]).reshape(entry_conv.shape)
    block_grad = jnp.stack(blocks_one + blocks_two).reshape(block_conv.shape)
    exit_one_grad = exit_one_part.reshape(3, 3, 6, 64).transpose(0, 1, 3, 2)
    exit_two_grad = exit_two_part.reshape(3, 3, 12, 64).transpose(0, 1, 3, 2)
    norm_grad = jnp.stack([norms_one, norms_two])
    head_grad = jnp.concatenate(
        [sums_one[0], sums_two[1], sums_one[1], sums_one[2], sums_two[2], sums_two[3]]
    )
    return (
        (loss_total, total_valid)
        + adamw(entry_conv, entry_first, entry_second, entry_grad, RATE_CONV)
        + adamw(block_conv, block_first, block_second, block_grad, RATE_CONV)
        + adamw(exit_one, exit_one_first, exit_one_second, exit_one_grad, RATE_CONV)
        + adamw(exit_two, exit_two_first, exit_two_second, exit_two_grad, RATE_CONV)
        + adamw(norm_params, norm_first, norm_second, norm_grad, RATE_SMALL)
        + adamw(head_params, head_first, head_second, head_grad, RATE_SMALL)
    )


def solution(mesh):
    placed = (P("batch", "rows", None, None), P("batch", "rows", None)) + (P(),) * 18
    return jax.shard_map(body, mesh=mesh, in_specs=placed, out_specs=(P(),) * 26, check_vma=False)
```

```python
import functools
import math

import jax
import jax.numpy as jnp
import numpy as np
from jax import lax
from jax.experimental import pallas as pl
from jax.experimental.pallas import tpu as pltpu
from jax.sharding import PartitionSpec as P

STEP = 10
ALPHA = 0.05
NORM_EPS = 1e-05
BETA_ONE = 0.9
BETA_TWO = 0.999
ADAM_EPS = 1e-08
DECAY = 0.01
RATE_CONV = 1.0
RATE_SMALL = 10.0
LOG_TWO = math.log(2.0)
HALF_LOG_TAU = 0.5 * math.log(2.0 * math.pi)
LOG_LEVELS = math.log(256.0)
IMAGES = 16
BITS = (("batch", 1), ("rows", 1), ("rows", 2), ("batch", 2), ("batch", 4), ("batch", 8), ("batch", 16), ("batch", 32))
LOW = jnp.bfloat16
WIDE = jnp.float32


def axis_bits():
    return [bit for bit in BITS if bit[1] < lax.axis_size(bit[0])]


def group_bits(batch):
    bits = axis_bits()
    count = max(batch // IMAGES, 1).bit_length() - 1
    return bits[: min(count, len(bits))]


def swap(value, bit):
    axis, mask = bit
    return lax.ppermute(value, axis, [(i, i ^ mask) for i in range(lax.axis_size(axis))])


def side(bit):
    return (lax.axis_index(bit[0]) // bit[1]) % 2


def group_sum(value, bits):
    for bit in bits:
        value = jax.tree.map(lambda own: own + swap(own, bit), value)
    return value


def swap_terms(value, bits):
    value = group_sum(value, bits[:-1])
    return [value, swap(value, bits[-1])]


def joined(own, other, mine, dim):
    first = jnp.where(mine == 0, own, other)
    second = jnp.where(mine == 0, other, own)
    return jnp.concatenate([first, second], axis=dim)


def distribute(cells, group):
    for bit in sorted(axis_bits(), key=lambda b: (b[0] != "rows", b[1])):
        mine = side(bit)
        dim = 0 if bit[0] == "rows" else 1
        if bit in group:
            if bit[0] == "batch":
                continue
            half = cells.shape[1] // 2
            away = lax.dynamic_slice_in_dim(cells, (1 - mine) * half, half, 1)
            cells = lax.dynamic_slice_in_dim(cells, mine * half, half, 1)
        else:
            away = cells
        cells = joined(cells, swap(away, bit), mine, dim)
    return cells


def merge_stats(both, count, group):
    for bit in group:
        both = call(
            functools.partial(merge_pair, 0.5 * count), [((2, 256), WIDE)], [both, swap(both, bit)], "merge"
        )[0]
        count = 2 * count
    return both


def merge_pair(weight, own_ref, other_ref, o_ref):
    gap = own_ref[0:1] - other_ref[0:1]
    o_ref[0:1] = 0.5 * (own_ref[0:1] + other_ref[0:1])
    o_ref[1:2] = own_ref[1:2] + other_ref[1:2] + gap * gap * weight


def blockify(kernel):
    rows = np.stack([np.pad(kernel, ((q, 1 - q), (0, 0), (0, 0), (0, 0))) for q in range(2)], axis=3)
    return np.stack([np.pad(rows, ((0, 0), (s, 1 - s), (0, 0), (0, 0), (0, 0))) for s in range(2)], axis=4)


def turned(kernel):
    return np.flip(kernel, (0, 1)).transpose(0, 1, 3, 2)


def views(blocked):
    rest = blocked.shape[2:]
    split = blocked.reshape((2, 2, 2, 2) + rest)
    return split.transpose((0, 2, 1, 3) + tuple(range(4, 4 + len(rest)))).reshape((16,) + rest)


def mates(blocked):
    return np.flip(blocked.reshape(4, 2, 2, *blocked.shape[2:]), 2).reshape(blocked.shape)


def spread(values, axis):
    shape = values.shape
    cut = values.reshape(shape[:axis] + (2, 3) + shape[axis + 1 :])
    pad = [(0, 0)] * cut.ndim
    pad[axis + 1] = (0, 1)
    return np.pad(cut, pad).reshape(shape[:axis] + (8,) + shape[axis + 1 :])


def window_rows(weights):
    flat = weights.reshape(4, -1, 4)
    return np.pad(flat, ((0, 0), (0, 128 - flat.shape[1]), (0, 0))).reshape(512, 4)


def checker(odd):
    return ((np.arange(4)[:, None] + np.arange(4)[None, :]) % 2 == odd).reshape(4, 4, 1, 1)


def chosen(blocked, odd):
    both = np.where(checker(odd), blocked[:, :, :3], mates(blocked)[:, :, 3:])
    return window_rows(np.pad(both, ((0, 0), (0, 0), (0, 1), (0, 0))))


def numbered(channels, last):
    pad = 8 if channels == 6 else 16
    number = (pad * np.arange(9)[:, None] + np.arange(1, channels + 1)).reshape(3, 3, 1, channels)
    return number if last else number.transpose(0, 1, 3, 2)


@functools.cache
def placements():
    odd = (np.arange(2)[:, None] + np.arange(2)[None, :]) % 2 == 1
    found = {}
    blocked = blockify(numbered(6, False)).reshape(4, 4, 6, 4)
    found["entry_one"] = chosen(blocked, 0).T
    found["entry_two"] = window_rows(spread(blocked, 2)).T
    blocked = views(blockify(turned(numbered(6, False))))
    lanes = spread(blocked.reshape(16, 2, 2, 6), 3).reshape(16, 2, 16)
    lanes = np.pad(lanes, ((0, 0), (0, 0), (0, 48))).reshape(16, 128)
    found["entry_two_turned"] = lanes
    blocked = views(blockify(numbered(6, True))).reshape(16, 2, 2, 6)
    both = np.where(odd[None, :, :, None], blocked[..., :3], np.flip(blocked, 2)[..., 3:])
    lanes = np.pad(both, ((0, 0), (0, 0), (0, 0), (0, 1))).reshape(16, 2, 8)
    lanes = np.pad(lanes, ((0, 0), (0, 0), (0, 56))).reshape(16, 128)
    found["exit_one"] = lanes
    blocked = blockify(turned(numbered(6, True))).reshape(4, 4, 6, 4)
    found["exit_one_turned"] = chosen(blocked, 1).T
    blocked = views(blockify(numbered(12, True))).reshape(16, 2, 2, 2, 6)
    lanes = spread(blocked, 4).transpose(0, 1, 3, 2, 4).reshape(16, 4, 16)
    lanes = np.pad(lanes, ((0, 0), (0, 0), (0, 16))).reshape(16, 128)
    found["exit_two"] = lanes
    blocked = blockify(turned(numbered(12, True))).reshape(4, 4, 12, 4)
    pair = [window_rows(spread(blocked[:, :, 6 * s : 6 * s + 6], 2)) for s in range(2)]
    found["exit_two_turned"] = np.concatenate(pair).T
    for key in ("entry_one", "entry_two", "exit_one_turned", "exit_two_turned"):
        found[key + "_fold"] = found[key].reshape(4, -1, 128)[:, :, :32].reshape(4, -1)
    number = np.arange(1, 28)

    def line(values, lanes):
        cut = np.pad(values.reshape(-1, 3), ((0, 0), (0, 1))).reshape(-1)
        return np.tile(cut, 128 // lanes)

    pick = (np.arange(128) // 4) % 2
    scale, shift = line(number[9:12], 4), line(number[12:15], 4)
    lines = [
        line(number[0:3], 4),
        np.where(pick == 1, scale, shift),
        np.where(pick == 0, scale, shift),
        line(number[3:9], 8),
        line(number[15:21], 8),
        line(number[21:27], 8),
        np.zeros(128, int),
        np.zeros(128, int),
    ]
    found["head"] = np.stack(lines)
    return {key: value.astype(np.int32) for key, value in found.items()}


def exact_dot(left, right, dims):
    return lax.dot_general(
        left, right, (dims, ((), ())), precision=lax.Precision.HIGHEST, preferred_element_type=WIDE
    )


def hot(line, count):
    return lax.broadcasted_iota(jnp.int32, (count, line.shape[1]), 0) + 1 == line


def place_rows(place_ref, kernel, o_ref):
    for p in range(4):
        one = jnp.where(hot(place_ref[p : p + 1], kernel.shape[0]), 1.0, 0.0).astype(LOW)
        part = lax.dot_general(one, kernel, (((0,), (0,)), ((), ())), preferred_element_type=WIDE)
        o_ref[:, 64 * p : 64 * p + 64] = part.astype(LOW)


def place_lanes(place_ref, kernel, o_ref):
    for p in range(16):
        one = jnp.where(hot(place_ref[p : p + 1], kernel.shape[0]), 1.0, 0.0).astype(LOW)
        part = lax.dot_general(kernel, one, (((0,), (0,)), ((), ())), preferred_element_type=WIDE)
        o_ref[64 * p : 64 * p + 64] = part.astype(LOW)


def padded_kernel(rows, scratch, width):
    scratch[...] = jnp.zeros(scratch.shape, WIDE)
    for t in range(9):
        value = rows(t)
        scratch[width * t : width * t + value.shape[0]] = value
    return scratch[...].astype(LOW)


def build_small(entry_ref, one_ref, two_ref, norm_ref, head_ref, *refs):
    places = refs[:8]
    entry_one_o, entry_two_o, entry_turned_o, one_o, one_turned_o, two_o, two_turned_o, line_o = refs[8:16]
    par_refs, (small, large) = refs[16:26], refs[26:]
    entry_one = padded_kernel(lambda t: entry_ref[6 * t : 6 * t + 6, 0], small, 8)
    entry_two = padded_kernel(lambda t: entry_ref[6 * t : 6 * t + 6, 1], small, 8)
    exit_one = padded_kernel(lambda t: one_ref[t], small, 8)
    exit_two = padded_kernel(lambda t: two_ref[t], large, 16)
    place_rows(places[0], entry_one, entry_one_o)
    place_rows(places[1], entry_two, entry_two_o)
    place_lanes(places[2], entry_two, entry_turned_o)
    place_lanes(places[3], exit_one, one_o)
    place_rows(places[4], exit_one, one_turned_o)
    place_lanes(places[5], exit_two, two_o)
    place_rows(places[6], exit_two, two_turned_o)
    for norm, par_o in enumerate(par_refs):
        for spot in range(4):
            par_o[:, 64 * spot : 64 * spot + 64] = norm_ref[norm // 5, norm % 5]
    for spot in range(8):
        one = jnp.where(hot(places[7][spot : spot + 1], head_ref.shape[1]), 1.0, 0.0)
        line_o[spot : spot + 1] = exact_dot(head_ref[...], one, ((1,), (0,)))


def build_blocks(kernel_ref, *o_refs):
    for k, o_ref in enumerate(o_refs):
        tap = [kernel_ref[k, t].astype(LOW) for t in range(9)]
        zero = jnp.zeros((64, 64), LOW)
        for r in range(4):
            for c in range(4):
                parts = [
                    tap[3 * (r - q) + c - s] if 0 <= r - q < 3 and 0 <= c - s < 3 else zero
                    for q in range(2)
                    for s in range(2)
                ]
                row = (((r // 2) * 2 + c // 2) * 4 + (r % 2) * 2 + c % 2) * 64
                o_ref[row : row + 64] = jnp.concatenate(parts, axis=1)


def groups(count):
    head = [(0, 1)] if count % 8 else []
    return head + [(start, 8) for start in range(count % 8, count, 8)]


def lane_fold(value):
    value = value + pltpu.roll(value, 128, 1)
    return value + pltpu.roll(value, 64, 1)


def total_rows(value):
    return jnp.sum(value, axis=0, keepdims=True)


def edge_masks(odd, count):
    if not odd:
        return None, None
    lane = lax.broadcasted_iota(jnp.int32, (count, 1, 256), 2)
    spot = lax.broadcasted_iota(jnp.int32, (count, 1, 256), 0)
    low = (lane // 64) % 2 == 0
    columns = jnp.where((spot == 0) & low | (spot == count - 1) & ~low, 0.0, 1.0)
    row_low = lax.broadcasted_iota(jnp.int32, (1, 1, 256), 2) < 128

    def row(i):
        return jnp.where((i == 0) & row_low | (i == count - 1) & ~row_low, 0.0, 1.0)

    return columns, row


def masked(value, masks, i):
    columns, row = masks
    if columns is None:
        return value
    return value * (columns * row(i))


def norm_lines(st_ref, par_ref, cells):
    mean = st_ref[0:1, :]
    inv = lax.rsqrt(st_ref[1:2, :] / cells + NORM_EPS)
    return mean, inv, par_ref[0:1, :], par_ref[1:2, :]


def clear_border(ref, count):
    ref[0] = jnp.zeros(ref.shape[1:], ref.dtype)
    ref[count + 1] = jnp.zeros(ref.shape[1:], ref.dtype)
    ref[:, 0] = jnp.zeros((ref.shape[0],) + ref.shape[2:], ref.dtype)
    ref[:, count + 1] = jnp.zeros((ref.shape[0],) + ref.shape[2:], ref.dtype)


def activate(v_ref, count, st_ref, par_ref, a_ref, odd, cells):
    pad = 0 if odd else 1
    mean, inv, gain, shift = norm_lines(st_ref, par_ref, cells)
    scale = 0.5 * gain * inv
    offset = 0.5 * shift - mean * scale
    masks = edge_masks(odd, count)
    if pad:
        clear_border(a_ref, count)

    @pl.loop(0, count)
    def _(i):
        half = v_ref[i, :count] * scale + offset
        act = half + half * jnp.tanh(half)
        a_ref[i + pad, pad : pad + count] = masked(act, masks, i).astype(LOW)


def four_views(ref, start, size, count):
    n = ref.shape[2]
    return [
        ref[start + vi : start + vi + size, vj : vj + count].reshape(size * count * n, 256)
        for vi in range(2)
        for vj in range(2)
    ]


def column_stats(o_ref, count, st_ref, odd):
    n = o_ref.shape[2]
    row = jnp.sum(o_ref[count // 2, 1 : count - 1].reshape(-1, 256), 0, keepdims=True)
    shift = lane_fold(row) / (4 * n * (count - 2))
    masks = edge_masks(odd, count)

    def step(i, sums):
        gap = masked(o_ref[i, :count] - shift, masks, i)
        rows = gap.reshape(-1, 8, 256)
        return sums[0] + jnp.sum(rows, 0), sums[1] + jnp.sum(rows * rows, 0)

    zero = jnp.zeros((8, 256), WIDE)
    first, second = lax.fori_loop(0, count, step, (zero, zero))
    cells = n * (count - 1 if odd else count) ** 2 * 4
    first = lane_fold(total_rows(first)) / cells
    second = lane_fold(total_rows(second))
    st_ref[0:1, :] = shift + first
    st_ref[1:2, :] = second - first * first * cells


def mid_forward(odd, cells, st_ref, par_ref, held_ref, w_ref, state_ref, out_st_ref, far_ref, a_ref, sem):
    count = far_ref.shape[0]
    n = far_ref.shape[2]
    own = count + 1 if odd else count - 1
    v_ref, o_ref = (state_ref.at[0], state_ref.at[1]) if odd else (state_ref.at[1], state_ref.at[0])
    activate(v_ref, own, st_ref, par_ref, a_ref, odd, cells)
    copies = []
    for index, (start, size) in enumerate(groups(count)):
        left = jnp.concatenate(four_views(a_ref, start, size, count), axis=1)
        value = jnp.dot(left, w_ref[...], preferred_element_type=WIDE).reshape(size, count, n, 256)
        if not odd:
            value = value + o_ref[start : start + size, :count]
        o_ref[start : start + size, :count] = value
        copies.append(
            pltpu.make_async_copy(
                o_ref.at[start : start + size, :count], far_ref.at[start : start + size], sem.at[index]
            )
        )
        copies[-1].start()
    column_stats(o_ref, count, out_st_ref, not odd)
    for copy in copies:
        copy.wait()


def rolled(value, shift):
    shift = shift % 128
    return value if shift == 0 else pltpu.roll(value, shift, 1)


def window_left(x_ref, spot, width):
    count = x_ref.shape[0] // 2 - 1
    n = x_ref.shape[1]
    columns = 128 // width
    first = 2 * spot - 2
    value = rolled(x_ref[...].reshape(-1, 128), -width * first).reshape(count + 1, 2, n, 128)
    if first < 0 or first + 4 > columns:
        column = lax.broadcasted_iota(jnp.int32, (count + 1, 2, n, 128), 3) // width + first
        value = jnp.where((column >= 0) & (column < columns), value, jnp.zeros_like(value))
    return jnp.concatenate(
        [value[r // 2 : r // 2 + count, r % 2].reshape(count * n, 128) for r in range(4)], axis=1
    ).astype(LOW)


def window_forward(width, x_ref, w_ref, state_ref, st_ref, far_ref, sem):
    count, n = far_ref.shape[0], far_ref.shape[2]
    o_ref = state_ref.at[0]
    for spot in range(count):
        left = window_left(x_ref, spot, width)
        value = jnp.dot(left, w_ref[...], preferred_element_type=WIDE)
        o_ref[:, spot] = value.reshape(count, n, 256)
    copy = pltpu.make_async_copy(o_ref, far_ref, sem.at[0])
    copy.start()
    column_stats(o_ref, count, st_ref, True)
    copy.wait()


def to_rows(value_ref, step, items, store):
    count, n = value_ref.shape[0], value_ref.shape[2]
    room = 128 // items
    per = count // items
    sums = []
    for part in range(items):
        total = None
        for spot in range(part * per, part * per + per):
            moved = rolled(value_ref[:, spot].reshape(-1, 128), step * spot)
            total = moved if total is None else total + moved
        sums.append(total)
    lane = lax.broadcasted_iota(jnp.int32, (count * n, 128), 1) // room
    for item in range(items):
        value = sums[0]
        for part in range(1, items):
            value = jnp.where(lane == (item + part) % items, sums[part], value)
        store(item, rolled(value, -room * item).reshape(count, n, 128))


def exit_forward(cells, step, items, st_ref, par_ref, state_ref, w_ref, o_ref, a_ref, value_ref):
    count = value_ref.shape[0]
    n = value_ref.shape[2]
    activate(state_ref.at[0], count + 1, st_ref, par_ref, a_ref, True, cells)
    for start, size in groups(count):
        left = jnp.concatenate(four_views(a_ref, start, size, count), axis=1)
        value = jnp.dot(left, w_ref[...], preferred_element_type=WIDE)
        value_ref[start : start + size] = value.reshape(size, count, n, 128)

    def store(item, value):
        o_ref[item] = value

    to_rows(value_ref, step, items, store)


def activation_grads(g_ref, v_ref, count, st_ref, par_ref, a_ref, sum_ref, odd, cells):
    pad = 0 if odd else 1
    mean, inv, gain, shift = norm_lines(st_ref, par_ref, cells)
    offset = -mean * inv
    masks = edge_masks(odd, count)
    if pad:
        clear_border(a_ref, count)

    def step(i, sums):
        normed = v_ref[i, :count] * inv + offset
        half = normed * (0.5 * gain) + 0.5 * shift
        bend = jnp.tanh(half)
        a_ref[i + pad, pad : pad + count] = masked(half + half * bend, masks, i).astype(LOW)
        grad = masked(g_ref[i, :count] * ((1.0 + bend) * (1.0 + half * (1.0 - bend))), masks, i)
        g_ref[i, :count] = grad
        rows = grad.reshape(-1, 8, 256)
        other = (grad * normed).reshape(-1, 8, 256)
        return sums[0] + jnp.sum(rows, 0), sums[1] + jnp.sum(other, 0)

    zero = jnp.zeros((8, 256), WIDE)
    first, second = lax.fori_loop(0, count, step, (zero, zero))
    sum_ref[0:1, :] = lane_fold(total_rows(first))
    sum_ref[1:2, :] = lane_fold(total_rows(second))


def norm_input_grads(sum_ref, st_ref, par_ref, state_ref, count, low_ref, odd, cells, residual, keep):
    pad = 0 if odd else 1
    mean, inv, gain, shift = norm_lines(st_ref, par_ref, cells)
    scale = 0.5 * gain * inv
    slope = -scale * inv * sum_ref[1:2, :] / cells
    offset = -scale * sum_ref[0:1, :] / cells - slope * mean
    masks = edge_masks(odd, count)
    if pad:
        clear_border(low_ref, count)

    @pl.loop(0, count)
    def _(i):
        grad = masked(state_ref[0, i, :count] * scale + state_ref[1, i, :count] * slope + offset, masks, i)
        if residual:
            grad = grad + state_ref[2, i]
        if keep:
            state_ref[2, i] = grad
        low_ref[i + pad, pad : pad + count] = grad.astype(LOW)


def mid_backward(odd, residual, cells, *refs):
    sum_ref, st_ref, par_ref, held_ref, w_ref, in_st_ref, in_par_ref, in_v_far = refs[:8]
    state_ref, pair_ref, out_sum_ref, sem = refs[8:]
    count, n = in_v_far.shape[0], in_v_far.shape[2]
    own = count + 1 if odd else count - 1
    low_ref, a_ref = pair_ref.at[0], pair_ref.at[1]
    norm_input_grads(sum_ref, st_ref, par_ref, state_ref, own, low_ref, odd, cells, residual, odd)
    copy = pltpu.make_async_copy(in_v_far, state_ref.at[1, :count, :count], sem.at[0])
    copy.start()
    for start, size in groups(count):
        value = None
        for spot, left in enumerate(four_views(low_ref, start, size, count)):
            right = w_ref[256 * (3 - spot) : 256 * (4 - spot)]
            part = lax.dot_general(left, right, (((1,), (1,)), ((), ())), preferred_element_type=WIDE)
            value = part if value is None else value + part
        state_ref[0, start : start + size, :count] = value.reshape(size, count, n, 256)
    copy.wait()
    activation_grads(
        state_ref.at[0], state_ref.at[1], count, in_st_ref, in_par_ref, a_ref, out_sum_ref, not odd, cells
    )


def window_backward(width, arrays, cells, *refs):
    d_refs = refs[:arrays]
    w_ref, st_ref, par_ref, v_far, state_ref, a_ref, sum_ref, sem = refs[arrays:]
    count, n = v_far.shape[0], v_far.shape[2]
    copy = pltpu.make_async_copy(v_far, state_ref.at[1], sem.at[0])
    copy.start()
    for spot in range(count):
        left = jnp.concatenate([window_left(d_ref, spot, width) for d_ref in d_refs], axis=1)
        value = jnp.dot(left, w_ref[...], preferred_element_type=WIDE)
        state_ref[0, :, spot] = value.reshape(count, n, 256)
    copy.wait()
    activation_grads(state_ref.at[0], state_ref.at[1], count, st_ref, par_ref, a_ref, sum_ref, True, cells)


def entry_backward(cells, inputs, *refs):
    sum_ref, st_ref, par_ref, state_ref = refs[:4]
    low_ref = refs[5] if inputs else refs[4]
    count = low_ref.shape[0]
    norm_input_grads(sum_ref, st_ref, par_ref, state_ref, count, low_ref, True, cells, True, False)
    if inputs:
        w_ref, low_ref, o_ref, value_ref = refs[4:]
        count, n = value_ref.shape[0], value_ref.shape[2]
        for start, size in groups(count):
            left = jnp.concatenate(four_views(low_ref, start, size, count), axis=1)
            value = jnp.dot(left, w_ref[...], preferred_element_type=WIDE)
            value_ref[start : start + size] = value.reshape(size, count, n, 128)

        def store(item, value):
            o_ref[item] = value

        to_rows(value_ref, 16, 2, store)


def block_weight_grad(odd, spot, pair_ref, *refs):
    o_ref, acc_ref = refs[-2:]
    low_ref, a_ref = pair_ref.at[0], pair_ref.at[1]
    pad = 0 if odd else 1
    count = low_ref.shape[0] - (1 if odd else 2)
    n = low_ref.shape[2]
    for index, (start, size) in enumerate(groups(count)):
        grad = low_ref[start + pad : start + pad + size, pad : pad + count].reshape(size * count * n, 256)
        right = jnp.concatenate(four_views(a_ref, start, size, count), axis=1)
        part = lax.dot_general(grad, right, (((0,), (0,)), ((), ())), preferred_element_type=WIDE)
        if index == 0:
            acc_ref[...] = part
        else:
            acc_ref[...] += part
    for dy in range(3):
        for dx in range(3):
            total = None
            for q in range(2):
                for s in range(2):
                    r, c = dy + q, dx + s
                    lane = ((r // 2) * 2 + c // 2) * 256 + ((r % 2) * 2 + c % 2) * 64
                    part = acc_ref[(2 * q + s) * 64 : (2 * q + s) * 64 + 64, lane : lane + 64]
                    total = part if total is None else total + part
            total = total.T
            start = 288 * spot + 32 * (3 * dy + dx)
            o_ref[start : start + 32, :64] = total[:32]
            o_ref[start : start + 32, 64:] = total[32:]


def window_weight_grad(width, arrays, *refs):
    x_refs = refs[:arrays]
    b_ref, place_ref, o_ref, acc_ref = refs[arrays:]
    count, n = b_ref.shape[0], b_ref.shape[2]
    for spot in range(count):
        right = jnp.concatenate([window_left(x_ref, spot, width) for x_ref in x_refs], axis=1)
        left = b_ref[:, spot].reshape(count * n, 256)
        part = lax.dot_general(left, right, (((0,), (0,)), ((), ())), preferred_element_type=WIDE)
        if spot == 0:
            acc_ref[...] = part
        else:
            acc_ref[...] += part
    lane = lax.broadcasted_iota(jnp.int32, (64, 128), 1) // 32
    total = None
    for p in range(4):
        parts = []
        for array in range(arrays):
            held = jnp.zeros((64, 128), WIDE)
            for r in range(4):
                start = 512 * array + 128 * r
                value = rolled(acc_ref[64 * p : 64 * p + 64, start : start + 128], 32 * r)
                held = jnp.where(lane == r, value, held)
            parts.append(held)
        one = jnp.where(hot(place_ref[p : p + 1], 72 * arrays), 1.0, 0.0)
        part = exact_dot(one, jnp.concatenate(parts, axis=1), ((1,), (1,)))
        total = part if total is None else total + part
    o_ref[...] = total


def lane_ids(shape):
    return lax.broadcasted_iota(jnp.int32, shape, len(shape) - 1)


def flat_roll(value, shift):
    return rolled(value.reshape(-1, 128), shift).reshape(value.shape)


def valid_lanes(cells):
    held = jnp.where(lane_ids(cells.shape) % 4 == 3, cells, 0.0)
    return flat_roll(held, -1) + flat_roll(held, -2) + flat_roll(held, -3)


def pad_rows(x_ref, values):
    rows, n = values.shape[0], values.shape[1]
    x_ref[0:2] = jnp.zeros((2, n, 128), x_ref.dtype)
    x_ref[2 : 2 + rows] = values.astype(x_ref.dtype)
    x_ref[2 + rows :] = jnp.zeros((2, n, 128), x_ref.dtype)


def column_line(value):
    return jnp.sum(value.reshape(-1, 128), axis=0, keepdims=True)


def checks(shape):
    lane = lane_ids(shape)
    row = lax.broadcasted_iota(jnp.int32, shape, 0)
    return ((row + lane // 4) % 2 == 1) & (lane % 4 != 3)


def prepare(cells_ref, x_ref, logits_ref, sum_ref):
    cells = cells_ref[...]
    lane = lane_ids(cells.shape)
    channel = lane % 4 != 3
    valid = valid_lanes(cells)
    prob = ALPHA + (1.0 - 2.0 * ALPHA) * (cells / 256.0)
    log_in = jnp.log(prob)
    log_out = jnp.log(1.0 - prob)
    logits = jnp.where(channel, log_in - log_out, 0.0)
    jacobian = math.log(1.0 - 2.0 * ALPHA) - log_in - log_out
    logits_ref[...] = logits
    sum_ref[0:1] = column_line(valid)
    sum_ref[1:2] = column_line(valid * (HALF_LOG_TAU + LOG_LEVELS - jacobian))
    odd = checks(cells.shape)
    pad_rows(x_ref, jnp.where(odd, 1.0, logits))


def couple(line_ref, raw_ref, logits_ref, cells_ref, o_ref, bend_ref, sum_ref):
    logits = logits_ref[...]
    valid = valid_lanes(cells_ref[...])
    gain = line_ref[0:1].reshape(1, 1, 128)
    total = jnp.zeros((1, 128), WIDE)
    for q in range(2):
        raw = raw_ref[q] + line_ref[1 + q : 2 + q].reshape(1, 1, 128)
        own = logits_ref[pl.ds(q, raw.shape[0], 2)]
        cells = cells_ref[pl.ds(q, raw.shape[0], 2)]
        lane = lane_ids(raw.shape)
        odd = ((q + lane // 4) % 2 == 1) & (lane % 4 != 3)
        shift = flat_roll(raw, 4 if q == 0 else -4)
        bend = jnp.where(odd, jnp.tanh(raw), 0.0)
        scale = gain * bend
        coupled = jnp.where(odd, own * jnp.exp(scale) + shift, own)
        bend_ref[q] = bend
        total = total - column_line(valid_lanes(cells) * scale)
        o_ref[pl.ds(q, raw.shape[0], 2)] = jnp.where(lane % 4 == 3, cells, coupled)
    sum_ref[...] = total


def enter_two(coupled_ref, x_ref):
    value = coupled_ref[pl.ds(0, coupled_ref.shape[0] // 2, 2)]
    pad_rows(x_ref, jnp.where(lane_ids(value.shape) % 4 == 3, 0.0, value))


def losses(line_ref, count_ref, raw_ref, coupled_ref, scale_d_ref, shift_d_ref, grad_ref, sum_ref):
    half = coupled_ref.shape[0] // 2
    shape = (half, coupled_ref.shape[1], 128)
    channel = lane_ids(shape) % 4 != 3
    top = coupled_ref[pl.ds(0, half, 2)]
    low = coupled_ref[pl.ds(1, half, 2)]
    top_valid = valid_lanes(top)
    low_valid = valid_lanes(low)
    top = jnp.where(channel, top, 0.0)
    low = jnp.where(channel, low, 0.0)

    def rows(item):
        pair = jnp.stack([raw_ref[item], raw_ref[2 + item]], axis=1)
        return pair.reshape(shape) + line_ref[4 + item : 5 + item].reshape(1, 1, 128)

    gain = line_ref[3:4].reshape(1, 1, 128)
    unit = 1.0 / (LOG_TWO * jnp.sum(count_ref[0:1], axis=1, keepdims=True)).reshape(1, 1, 1)
    bend = jnp.tanh(rows(0))
    scale = gain * bend
    grow = jnp.exp(scale)
    latent = jnp.where(channel, low * grow + rows(1), 0.0)
    sum_ref[0:1] = column_line(top_valid * (0.5 * top * top) + low_valid * (0.5 * latent * latent - scale))
    moved = low_valid * unit * latent
    grad_scale = moved * low * grow - low_valid * unit
    raw_grad = grad_scale * gain * (1.0 - bend * bend)
    sum_ref[1:2] = column_line(grad_scale * bend)
    sum_ref[2:3] = column_line(raw_grad)
    sum_ref[3:4] = column_line(moved)
    pad_rows(scale_d_ref, raw_grad)
    pad_rows(shift_d_ref, moved)
    grad_ref[pl.ds(0, half, 2)] = top_valid * unit * top
    grad_ref[pl.ds(1, half, 2)] = moved * grow


def uncouple(mine_ref, line_ref, count_ref, entry_ref, grad_ref, logits_ref, bend_ref, cells_ref, d_ref, sum_ref):
    half = logits_ref.shape[0] // 2
    n = logits_ref.shape[1]
    own_part = pl.ds(pl.multiple_of(mine_ref[0], 8), n)
    gain = line_ref[0:1].reshape(1, 1, 128)
    unit = 1.0 / (LOG_TWO * jnp.sum(count_ref[0:1], axis=1, keepdims=True)).reshape(1, 1, 1)
    lines = [jnp.zeros((1, 128), WIDE)] * 3
    d_ref[0:2] = jnp.zeros((2, n, 128), d_ref.dtype)
    d_ref[2 * half + 2 :] = jnp.zeros((d_ref.shape[0] - 2 * half - 2, n, 128), d_ref.dtype)
    for q in range(2):
        grad = grad_ref[pl.ds(q, half, 2), own_part]
        if q == 0:
            grad = grad + jnp.stack([entry_ref[0, :, own_part], entry_ref[1, :, own_part]], axis=1).reshape(half, n, 128)
        own = logits_ref[pl.ds(q, half, 2)]
        valid = valid_lanes(cells_ref[pl.ds(q, half, 2)])
        bend = bend_ref[q]
        lane = lane_ids(grad.shape)
        odd = ((q + lane // 4) % 2 == 1) & (lane % 4 != 3)
        grad = jnp.where(odd, grad, 0.0)
        grad_scale = jnp.where(odd, grad * own * jnp.exp(gain * bend) - valid * unit, 0.0)
        raw_grad = grad_scale * gain * (1.0 - bend * bend)
        lines[0] = lines[0] + column_line(grad_scale * bend)
        lines[1] = lines[1] + column_line(raw_grad)
        lines[2] = lines[2] + column_line(grad)
        value = raw_grad + flat_roll(grad, -4 if q == 0 else 4)
        d_ref[pl.ds(2 + q, half, 2)] = value.astype(d_ref.dtype)
    for spot in range(3):
        sum_ref[spot : spot + 1] = lines[spot]


def call(kernel, outs, args, name, scratch=(), limit=8, far_in=(), far_out=(), sems=0, aliases=None, scalar_in=()):
    spaces = [
        pltpu.HBM if spot in far_in else pltpu.SMEM if spot in scalar_in else pltpu.VMEM
        for spot in range(len(args))
    ]
    out_spaces = [pltpu.HBM if spot in far_out else pltpu.VMEM for spot in range(len(outs))]
    held = [pltpu.VMEM(shape, dtype) for shape, dtype in scratch]
    args = [pltpu.with_memory_space_constraint(arg, space) if space is pltpu.HBM else arg for arg, space in zip(args, spaces)]
    if sems:
        held.append(pltpu.SemaphoreType.DMA(sems))
    return pl.pallas_call(
        kernel,
        out_shape=[space(shape, dtype) for space, (shape, dtype) in zip(out_spaces, outs)],
        in_specs=[pl.BlockSpec(memory_space=space) for space in spaces],
        out_specs=[pl.BlockSpec(memory_space=space) for space in out_spaces],
        scratch_shapes=held,
        compiler_params=pltpu.CompilerParams(vmem_limit_bytes=limit * 2**20),
        input_output_aliases=aliases or {},
        name=name,
    )(*args)


class Net:
    def __init__(self, name, blocks, n, width, group, total, pars, weights):
        self.name = name
        self.even = blocks
        self.odd = blocks + 1
        self.n = n
        self.width = width
        self.group = group
        self.cells = float(total)
        self.own = float(n * blocks * blocks * 4)
        self.pars = pars
        self.weights = weights
        self.far = []
        self.stats = []

    def shape(self, odd, padded=False):
        count = self.odd if odd else self.even
        pad = 2 if padded and not odd else 0
        return (count + pad, count + pad, self.n, 256)

    def keep(self, stats, far):
        self.far.append(far)
        self.stats.append(merge_stats(stats, self.own, self.group))

    def forward(self, x, entry, exit_weights, items):
        held = (2,) + self.shape(True)
        state, stats, far = call(
            functools.partial(window_forward, self.width),
            [(held, WIDE), ((2, 256), WIDE), (self.shape(True), WIDE)],
            [x, entry],
            self.name + "_entry",
            far_out=(2,),
            sems=(1,),
        )
        self.keep(stats, far)
        for index in range(4):
            odd = index % 2 == 0
            state, stats, far = call(
                functools.partial(mid_forward, odd, self.cells),
                [(held, WIDE), ((2, 256), WIDE), (self.shape(not odd), WIDE)],
                [self.stats[index], self.pars[index], state, self.weights[index]],
                self.name + "_forward",
                [(self.shape(odd, True), LOW)],
                far_out=(2,),
                sems=(len(groups(self.odd)),),
                aliases={2: 0},
            )
            self.keep(stats, far)
        return call(
            functools.partial(exit_forward, self.cells, 2 * self.width, items),
            [((items, self.even, self.n, 128), WIDE)],
            [self.stats[4], self.pars[4], state, exit_weights],
            self.name + "_exit",
            [(self.shape(True), LOW), ((self.even, self.even, self.n, 128), WIDE)],
        )[0]

    def backward(self, grads, exit_turned, exit_place, x, entry_turned, entry_place, packet, slots):
        arrays = len(grads)
        held = (3,) + self.shape(True)
        pair_shape = (2, self.even + 2, self.even + 2, self.n, 256)
        state, act, sums = call(
            functools.partial(window_backward, self.width, arrays, self.cells),
            [(held, WIDE), (self.shape(True), LOW), ((2, 256), WIDE)],
            list(grads) + [exit_turned, self.stats[4], self.pars[4], self.far[4]],
            self.name + "_exit_back",
            far_in=(arrays + 3,),
            sems=(1,),
        )
        exit_grad = call(
            functools.partial(window_weight_grad, self.width, arrays),
            [((72 * arrays, 64), WIDE)],
            list(grads) + [act, exit_place],
            self.name + "_exit_weights",
            [((256, 512 * arrays), WIDE)],
        )[0]
        results_of = {}
        sums, exit_grad, *done = lax.optimization_barrier(
            (group_sum(sums, self.group), exit_grad) + slots.get(4, lambda: ())()
        )
        results_of[4] = done
        norm_grads = [None] * 5
        block_grads = []
        norm_grads[4] = sums
        for index in reversed(range(4)):
            odd = index % 2 == 1
            state, pair, sums = call(
                functools.partial(mid_backward, odd, index == 1, self.cells),
                [(held, WIDE), (pair_shape, LOW), ((2, 256), WIDE)],
                [
                    sums,
                    self.stats[index + 1],
                    self.pars[index + 1],
                    state,
                    self.weights[index],
                    self.stats[index],
                    self.pars[index],
                    self.far[index],
                ],
                self.name + "_back",
                far_in=(7,),
                sems=(1,),
                aliases={3: 0},
            )
            spot = index % packet
            fresh = spot == packet - 1
            block = call(
                functools.partial(block_weight_grad, odd, spot),
                [((288 * packet, 128), WIDE)],
                [pair] + ([] if fresh else [block]),
                self.name + "_weights",
                [((256, 1024), WIDE)],
                aliases=None if fresh else {1: 0},
            )[0]
            sums, block, *done = lax.optimization_barrier((group_sum(sums, self.group), block) + slots.get(index, lambda: ())())
            results_of[index] = done
            norm_grads[index] = sums
            if spot == 0:
                block_grads.append(swap_terms(block, self.group))
        args = [sums, self.stats[0], self.pars[0], state]
        outs = [(self.shape(True), LOW)]
        scratch = []
        if entry_turned is not None:
            args.append(entry_turned)
            outs.append(((2, self.even, self.n, 128), WIDE))
            scratch.append(((self.even, self.even, self.n, 128), WIDE))
        results = call(
            functools.partial(entry_backward, self.cells, entry_turned is not None),
            outs,
            args,
            self.name + "_entry_back",
            scratch,
        )
        entry_grad = call(
            functools.partial(window_weight_grad, self.width, 1),
            [((72, 64), WIDE)],
            [x, results[0], entry_place],
            self.name + "_entry_weights",
            [((256, 512), WIDE)],
        )[0]
        return entry_grad, block_grads, exit_grad, norm_grads, results_of, (results[1] if entry_turned is not None else None)


def adam_blocks(spots, fresh, first, *refs):
    terms, refs = refs[:2], refs[2:]
    sources, refs = refs[:3], refs[3:]
    if not fresh:
        refs = refs[4:]
    targets, (held, out, out_low, in_sem, out_sem) = refs[:4], refs[4:]
    loads = []
    for k, spot in enumerate(spots):
        loads.append(
            [pltpu.make_async_copy(sources[j].at[spot], held.at[k, j], in_sem.at[k, j]) for j in range(3)]
        )
        for copy in loads[-1]:
            copy.start()
    stores = []
    for k, spot in enumerate(spots):
        for copy in loads[k]:
            copy.wait()
        for t in range(9):
            row = 288 * (first + k) + 32 * t
            packed = terms[0][row : row + 32] + terms[1][row : row + 32]
            grad = jnp.concatenate([packed[:, :64], packed[:, 64:]], axis=0)
            news = adamw(held[k, 0, t], held[k, 1, t], held[k, 2, t], grad, RATE_CONV)
            for j in range(3):
                out[k, j, t] = news[j]
            out_low[k, t] = news[3]
        copies = [pltpu.make_async_copy(out.at[k, j], targets[j].at[spot], out_sem.at[k, j]) for j in range(3)]
        copies.append(pltpu.make_async_copy(out_low.at[k], targets[3].at[spot], out_sem.at[k, 3]))
        for copy in copies:
            copy.start()
        stores += copies
    for copy in stores:
        copy.wait()


def step_blocks(spots, terms, first, sources, targets):
    count = len(spots)
    args = list(terms) + list(sources) + list(targets or [])
    shape = sources[0].shape
    head = 2
    return pl.pallas_call(
        functools.partial(adam_blocks, spots, targets is None, first),
        out_shape=[pltpu.HBM(shape, WIDE)] * 3 + [pltpu.HBM(shape, LOW)],
        in_specs=[pl.BlockSpec(memory_space=pltpu.VMEM)] * head
        + [pl.BlockSpec(memory_space=pltpu.HBM)] * (len(args) - head),
        out_specs=[pl.BlockSpec(memory_space=pltpu.HBM)] * 4,
        scratch_shapes=[
            pltpu.VMEM((count, 3) + shape[1:], WIDE),
            pltpu.VMEM((count, 3) + shape[1:], WIDE),
            pltpu.VMEM((count,) + shape[1:], LOW),
            pltpu.SemaphoreType.DMA((count, 3)),
            pltpu.SemaphoreType.DMA((count, 4)),
        ],
        input_output_aliases={} if targets is None else {head + 3 + j: j for j in range(4)},
        compiler_params=pltpu.CompilerParams(vmem_limit_bytes=12 * 2**20),
        name="step_blocks",
    )(*args[:head], *[pltpu.with_memory_space_constraint(arg, pltpu.HBM) for arg in args[head:]])


def adamw(master, first, second, grad, rate):
    first_new = BETA_ONE * first + (1.0 - BETA_ONE) * grad
    second_new = BETA_TWO * second + (1.0 - BETA_TWO) * grad * grad
    direction = (
        first_new
        / (1.0 - BETA_ONE**STEP)
        / (jnp.sqrt(second_new / (1.0 - BETA_TWO**STEP)) + ADAM_EPS)
    )
    master_new = master - rate * (direction + DECAY * master)
    return (master_new, first_new, second_new, master_new.astype(jnp.bfloat16))


def entry_view(array):
    return array.transpose(1, 2, 3, 0, 4).reshape(54, 2, 64)


def exit_view(array):
    return array.transpose(0, 1, 3, 2).reshape(9, array.shape[3], 64)


def pack_rows(*refs):
    o_ref = refs[-1]
    o_ref[...] = jnp.zeros(o_ref.shape, WIDE)
    row = 0
    for ref in refs[:-1]:
        o_ref[row : row + ref.shape[0], : ref.shape[1]] = ref[...]
        row += ref.shape[0]


def entry_grads(one_ref, one_other, two_ref, two_other, o_ref):
    one = one_ref[...] + one_other[...]
    two = two_ref[0:72, :64] + two_other[0:72, :64]
    for t in range(9):
        o_ref[6 * t : 6 * t + 6, 0] = one[8 * t : 8 * t + 6]
        o_ref[6 * t : 6 * t + 6, 1] = two[8 * t : 8 * t + 6]


def finish_kernel(*refs):
    one_ref, one_other, two_ref, two_other, count_ref = refs[:5]
    norm_sums, place_ref = refs[5:15], refs[15]
    exit_one, exit_two, norm, head = refs[16:19], refs[19:22], refs[22:25], refs[25:28]
    loss_o, valid_o = refs[28:30]
    exit_one_o, exit_two_o, norm_o, head_o = refs[30:34], refs[34:38], refs[38:42], refs[42:46]
    one = one_ref[...] + one_other[...]
    two = two_ref[...] + two_other[...]

    def store(outs, index, values):
        for o_ref, value in zip(outs, values):
            o_ref[index] = value

    for t in range(9):
        grad = one[8 * t : 8 * t + 6, :64]
        store(exit_one_o, t, adamw(exit_one[0][t], exit_one[1][t], exit_one[2][t], grad, RATE_CONV))
        grad = two[72 + 16 * t : 84 + 16 * t, :64]
        store(exit_two_o, t, adamw(exit_two[0][t], exit_two[1][t], exit_two[2][t], grad, RATE_CONV))
    for k in range(10):
        spot = (k // 5, k % 5)
        sums = norm_sums[k][...]
        grad = jnp.concatenate([sums[1:2, :64], sums[0:1, :64]], axis=0) * 0.5
        store(norm_o, spot, adamw(norm[0][spot], norm[1][spot], norm[2][spot], grad, RATE_SMALL))
    valid = jnp.sum(count_ref[0:1], axis=1, keepdims=True)
    constant = jnp.sum(count_ref[1:2], axis=1, keepdims=True)
    loss = jnp.sum(two[216:217], axis=1, keepdims=True) + jnp.sum(one[75:76], axis=1, keepdims=True)
    loss_o[...] = (loss + constant) / LOG_TWO
    valid_o[...] = valid

    def folded(line, spot):
        return exact_dot(line, jnp.where(hot(place_ref[spot : spot + 1], head[0].shape[1]), 1.0, 0.0), ((1,), (1,)))

    lane = lax.broadcasted_iota(jnp.int32, (1, 128), 1)
    raw, shift = one[73:74], one[74:75]
    grad = folded(one[72:73], 0) + folded(two[217:218], 3) + folded(two[218:219], 4) + folded(two[219:220], 5)
    grad = grad + folded(jnp.where((lane // 4) % 2 == 1, raw, 0.0), 1) + folded(jnp.where((lane // 4) % 2 == 0, raw, 0.0), 2)
    grad = grad + folded(jnp.where((lane // 4) % 2 == 0, shift, 0.0), 1) + folded(jnp.where((lane // 4) % 2 == 1, shift, 0.0), 2)
    for o_ref, value in zip(head_o, adamw(head[0][...], head[1][...], head[2][...], grad, RATE_SMALL)):
        o_ref[...] = value


def finish(packs, sums, place, exit_one, exit_two, norm, head):
    outs = [((1, 1), WIDE)] * 2
    for first in (exit_one[0], exit_two[0], norm[0], head[0]):
        outs += [(first.shape, WIDE)] * 3 + [(first.shape, LOW)]
    return call(
        finish_kernel, outs, packs + sums + [place] + exit_one + exit_two + norm + head, "finish"
    )


def body(
    pixels,
    valid,
    entry_conv,
    entry_first,
    entry_second,
    block_conv,
    block_first,
    block_second,
    exit_one,
    exit_one_first,
    exit_one_second,
    exit_two,
    exit_two_first,
    exit_two_second,
    norm_params,
    norm_first,
    norm_second,
    head_params,
    head_first,
    head_second,
):
    batch = pixels.shape[0] * lax.axis_size("batch")
    height = pixels.shape[1] * lax.axis_size("rows")
    group = group_bits(batch)
    small = group[:-1]
    last = group[-1]
    own = batch >> len(group)
    wide = 2 * own
    cells = jnp.concatenate([pixels, valid[..., None].astype(WIDE)], axis=3)
    cells = cells.reshape(pixels.shape[0], pixels.shape[1], 128).transpose(1, 0, 2)
    cells = distribute(cells, group)

    place = placements()
    small_places = [
        jnp.asarray(place[key])
        for key in (
            "entry_one",
            "entry_two",
            "entry_two_turned",
            "exit_one",
            "exit_one_turned",
            "exit_two",
            "exit_two_turned",
        )
    ]
    fold = [
        jnp.asarray(place[key + "_fold"])
        for key in ("entry_one", "entry_two", "exit_one_turned", "exit_two_turned")
    ]
    (
        entry_one_w,
        entry_two_w,
        entry_turned_w,
        exit_one_w,
        exit_one_turned_w,
        exit_two_w,
        exit_two_turned_w,
        head_lines,
        *par_lines,
    ) = call(
        build_small,
        [
            ((512, 256), LOW),
            ((512, 256), LOW),
            ((1024, 128), LOW),
            ((1024, 128), LOW),
            ((512, 256), LOW),
            ((1024, 128), LOW),
            ((1024, 256), LOW),
            ((8, 128), WIDE),
        ]
        + [((2, 256), WIDE)] * 10,
        [
            entry_view(entry_conv),
            exit_view(exit_one),
            exit_view(exit_two),
            norm_params,
            head_params[None],
        ]
        + small_places
        + [jnp.asarray(place["head"])],
        "build_small",
        [((72, 64), WIDE), ((144, 64), WIDE)],
    )
    blocks = call(build_blocks, [((1024, 256), LOW)] * 8, [block_conv.reshape(8, 9, 64, 64)], "build_blocks")
    weights = [[blocks[4 * j + k] for k in range(4)] for j in range(2)]
    pars = [[par_lines[5 * j + k] for k in range(5)] for j in range(2)]

    one = Net("one", height // 2, own, 4, group, batch * height * height, pars[0], weights[0])
    two = Net("two", height // 4, wide, 8, small, batch * (height // 2) ** 2, pars[1], weights[1])

    rows = height
    x_one, logits, first_sums = call(
        prepare,
        [((rows + 4, own, 128), WIDE), ((rows, own, 128), WIDE), ((2, 128), WIDE)],
        [cells],
        "prepare",
    )
    first_sums = group_sum(first_sums, group)
    mine, x_one = lax.optimization_barrier((side(last) * own, x_one))
    raw_one = one.forward(x_one, entry_one_w, exit_one_w, 2)
    coupled, bend_one, couple_sums = call(
        couple,
        [((rows, own, 128), WIDE), ((2, rows // 2, own, 128), WIDE), ((1, 128), WIDE)],
        [head_lines, raw_one, logits, cells],
        "couple",
    )
    coupled = joined(coupled, swap(coupled, last), mine, 1)
    x_two = call(enter_two, [((rows // 2 + 4, wide, 128), WIDE)], [coupled], "enter_two")[0]
    raw_two = two.forward(x_two, entry_two_w, exit_two_w, 4)
    scale_d, shift_d, grad_coupled, loss_sums = call(
        losses,
        [
            ((rows // 2 + 4, wide, 128), WIDE),
            ((rows // 2 + 4, wide, 128), WIDE),
            ((rows, wide, 128), WIDE),
            ((4, 128), WIDE),
        ],
        [
            head_lines,
            first_sums,
            raw_two,
            coupled,
        ],
        "losses",
    )
    entry_two, blocks_two, exit_two_part, norms_two, unused, grad_first = two.backward(
        [scale_d, shift_d], exit_two_turned_w, fold[3], x_two, entry_turned_w, fold[1], 4, {}
    )
    pack_two = call(
        pack_rows, [((224, 128), WIDE)], [entry_two, exit_two_part, loss_sums], "pack_two"
    )[0]
    pack_two = swap_terms(pack_two, small)
    sources = [part.reshape(8, 9, 64, 64) for part in (block_conv, block_first, block_second)]
    steps = {}

    def step(key, spots, terms, first):
        def run():
            steps[key] = tuple(step_blocks(spots, terms(), first, sources, steps.get(key - 1)))
            return steps[key]

        return run

    one_d, one_sums = call(
        uncouple,
        [((rows + 4, own, 128), WIDE), ((3, 128), WIDE)],
        [jnp.reshape(mine, (1,)), head_lines, first_sums, grad_first, grad_coupled, logits, bend_one, cells],
        "uncouple",
        scalar_in=(0,),
    )
    slots = {
        2: step(0, (4, 5), lambda: blocks_two[0], 0),
        1: step(1, (6, 7), lambda: blocks_two[0], 2),
    }
    entry_one, blocks_one, exit_one_part, norms_one, done, unused = one.backward(
        [one_d], exit_one_turned_w, fold[2], x_one, None, fold[0], 2, slots
    )
    pack_one = call(pack_rows, [((80, 128), WIDE)], [exit_one_part, one_sums, couple_sums], "pack_one")[0]
    pack_one = swap_terms(pack_one, group)
    entry_one = swap_terms(entry_one, group)
    stepped = step_blocks((2, 3), blocks_one[0], 0, sources, done[1])
    finished = finish(
        pack_one + pack_two,
        [first_sums] + norms_one + norms_two,
        jnp.asarray(place["head"]),
        [exit_view(part) for part in (exit_one, exit_one_first, exit_one_second)],
        [exit_view(part) for part in (exit_two, exit_two_first, exit_two_second)],
        [norm_params, norm_first, norm_second],
        [part[None] for part in (head_params, head_first, head_second)],
    )
    stepped = step_blocks((0, 1), blocks_one[1], 0, sources, stepped)
    entry_grad = call(
        entry_grads, [((54, 2, 64), WIDE)], entry_one + pack_two, "entry_grads"
    )[0]
    entry_steps = adamw(
        entry_view(entry_conv), entry_view(entry_first), entry_view(entry_second), entry_grad, RATE_CONV
    )
    entry_out = tuple(
        part.reshape(3, 3, 6, 2, 64).transpose(3, 0, 1, 2, 4) for part in entry_steps
    )
    one_out = tuple(part.reshape(3, 3, 6, 64).transpose(0, 1, 3, 2) for part in finished[2:6])
    two_out = tuple(part.reshape(3, 3, 12, 64).transpose(0, 1, 3, 2) for part in finished[6:10])
    return (
        (finished[0].reshape(()), finished[1].reshape(()))
        + entry_out
        + tuple(part.reshape(block_conv.shape) for part in stepped)
        + one_out
        + two_out
        + tuple(finished[10:14])
        + tuple(part.reshape(head_params.shape) for part in finished[14:18])
    )


def solution(mesh):
    placed = (P("batch", "rows", None, None), P("batch", "rows", None)) + (P(),) * 18
    return jax.shard_map(body, mesh=mesh, in_specs=placed, out_specs=(P(),) * 26, check_vma=False)
```

```python
import functools
import math

import jax
import jax.numpy as jnp
import numpy as np
from jax import lax
from jax.experimental import pallas as pl
from jax.experimental.pallas import tpu as pltpu
from jax.sharding import PartitionSpec as P

STEP = 10
ALPHA = 0.05
NORM_EPS = 1e-05
BETA_ONE = 0.9
BETA_TWO = 0.999
ADAM_EPS = 1e-08
DECAY = 0.01
RATE_CONV = 1.0
RATE_SMALL = 10.0
LOG_TWO = math.log(2.0)
HALF_LOG_TAU = 0.5 * math.log(2.0 * math.pi)
LOG_LEVELS = math.log(256.0)
IMAGES = 16
BITS = (("batch", 1), ("rows", 1), ("rows", 2), ("batch", 2), ("batch", 4), ("batch", 8), ("batch", 16), ("batch", 32))
LOW = jnp.bfloat16
WIDE = jnp.float32
COSTS = {
    "one_entry": 4.0,
    "one_forward": 3.7,
    "one_exit": 2.5,
    "one_exit_back": 5.7,
    "one_exit_weights": 2.6,
    "one_back": 5.4,
    "one_weights": 3.0,
    "one_entry_weights": 2.7,
    "two_entry": 2.7,
    "two_forward": 2.5,
    "two_exit": 1.4,
    "two_exit_back": 4.1,
    "two_exit_weights": 3.7,
    "two_back": 3.0,
    "two_weights": 1.9,
    "two_entry_back": 1.5,
    "two_entry_weights": 1.9,
    "build_small": 1.9,
    "build_blocks": 1.0,
    "finish": 1.2,
}


def axis_bits():
    return [bit for bit in BITS if bit[1] < lax.axis_size(bit[0])]


def group_bits(batch):
    bits = axis_bits()
    count = max(batch // IMAGES, 1).bit_length() - 1
    return bits[: min(count, len(bits))]


def swap(value, bit):
    axis, mask = bit
    return lax.ppermute(value, axis, [(i, i ^ mask) for i in range(lax.axis_size(axis))])


def side(bit):
    return (lax.axis_index(bit[0]) // bit[1]) % 2


def group_sum(value, bits):
    for bit in bits:
        value = jax.tree.map(lambda own: own + swap(own, bit), value)
    return value


def swap_terms(value, bits):
    value = group_sum(value, bits[:-1])
    return [value, swap(value, bits[-1])]


def joined(own, other, mine, dim):
    first = jnp.where(mine == 0, own, other)
    second = jnp.where(mine == 0, other, own)
    return jnp.concatenate([first, second], axis=dim)


def distribute(cells, group):
    for bit in sorted(axis_bits(), key=lambda b: (b[0] != "rows", b[1])):
        mine = side(bit)
        dim = 0 if bit[0] == "rows" else 1
        if bit in group:
            if bit[0] == "batch":
                continue
            half = cells.shape[1] // 2
            away = lax.dynamic_slice_in_dim(cells, (1 - mine) * half, half, 1)
            cells = lax.dynamic_slice_in_dim(cells, mine * half, half, 1)
        else:
            away = cells
        cells = joined(cells, swap(away, bit), mine, dim)
    return cells


def merge_stats(both, count, group):
    for bit in group:
        both = call(
            functools.partial(merge_pair, 0.5 * count), [((2, 256), WIDE)], [both, swap(both, bit)], "merge"
        )[0]
        count = 2 * count
    return both


def merge_pair(weight, own_ref, other_ref, o_ref):
    gap = own_ref[0:1] - other_ref[0:1]
    o_ref[0:1] = 0.5 * (own_ref[0:1] + other_ref[0:1])
    o_ref[1:2] = own_ref[1:2] + other_ref[1:2] + gap * gap * weight


def blockify(kernel):
    rows = np.stack([np.pad(kernel, ((q, 1 - q), (0, 0), (0, 0), (0, 0))) for q in range(2)], axis=3)
    return np.stack([np.pad(rows, ((0, 0), (s, 1 - s), (0, 0), (0, 0), (0, 0))) for s in range(2)], axis=4)


def turned(kernel):
    return np.flip(kernel, (0, 1)).transpose(0, 1, 3, 2)


def views(blocked):
    rest = blocked.shape[2:]
    split = blocked.reshape((2, 2, 2, 2) + rest)
    return split.transpose((0, 2, 1, 3) + tuple(range(4, 4 + len(rest)))).reshape((16,) + rest)


def mates(blocked):
    return np.flip(blocked.reshape(4, 2, 2, *blocked.shape[2:]), 2).reshape(blocked.shape)


def spread(values, axis):
    shape = values.shape
    cut = values.reshape(shape[:axis] + (2, 3) + shape[axis + 1 :])
    pad = [(0, 0)] * cut.ndim
    pad[axis + 1] = (0, 1)
    return np.pad(cut, pad).reshape(shape[:axis] + (8,) + shape[axis + 1 :])


def window_rows(weights):
    flat = weights.reshape(4, -1, 4)
    return np.pad(flat, ((0, 0), (0, 128 - flat.shape[1]), (0, 0))).reshape(512, 4)


def checker(odd):
    return ((np.arange(4)[:, None] + np.arange(4)[None, :]) % 2 == odd).reshape(4, 4, 1, 1)


def chosen(blocked, odd):
    both = np.where(checker(odd), blocked[:, :, :3], mates(blocked)[:, :, 3:])
    return window_rows(np.pad(both, ((0, 0), (0, 0), (0, 1), (0, 0))))


def numbered(channels, last):
    pad = 8 if channels == 6 else 16
    number = (pad * np.arange(9)[:, None] + np.arange(1, channels + 1)).reshape(3, 3, 1, channels)
    return number if last else number.transpose(0, 1, 3, 2)


@functools.cache
def placements():
    odd = (np.arange(2)[:, None] + np.arange(2)[None, :]) % 2 == 1
    found = {}
    blocked = blockify(numbered(6, False)).reshape(4, 4, 6, 4)
    found["entry_one"] = chosen(blocked, 0).T
    found["entry_two"] = window_rows(spread(blocked, 2)).T
    blocked = views(blockify(turned(numbered(6, False))))
    lanes = spread(blocked.reshape(16, 2, 2, 6), 3).reshape(16, 2, 16)
    lanes = np.pad(lanes, ((0, 0), (0, 0), (0, 48))).reshape(16, 128)
    found["entry_two_turned"] = lanes
    blocked = views(blockify(numbered(6, True))).reshape(16, 2, 2, 6)
    both = np.where(odd[None, :, :, None], blocked[..., :3], np.flip(blocked, 2)[..., 3:])
    lanes = np.pad(both, ((0, 0), (0, 0), (0, 0), (0, 1))).reshape(16, 2, 8)
    lanes = np.pad(lanes, ((0, 0), (0, 0), (0, 56))).reshape(16, 128)
    found["exit_one"] = lanes
    blocked = blockify(turned(numbered(6, True))).reshape(4, 4, 6, 4)
    found["exit_one_turned"] = chosen(blocked, 1).T
    blocked = views(blockify(numbered(12, True))).reshape(16, 2, 2, 2, 6)
    lanes = spread(blocked, 4).transpose(0, 1, 3, 2, 4).reshape(16, 4, 16)
    lanes = np.pad(lanes, ((0, 0), (0, 0), (0, 16))).reshape(16, 128)
    found["exit_two"] = lanes
    blocked = blockify(turned(numbered(12, True))).reshape(4, 4, 12, 4)
    pair = [window_rows(spread(blocked[:, :, 6 * s : 6 * s + 6], 2)) for s in range(2)]
    found["exit_two_turned"] = np.concatenate(pair).T
    for key in ("entry_one", "entry_two", "exit_one_turned", "exit_two_turned"):
        found[key + "_fold"] = found[key].reshape(4, -1, 128)[:, :, :32].reshape(4, -1)
    number = np.arange(1, 28)

    def line(values, lanes):
        cut = np.pad(values.reshape(-1, 3), ((0, 0), (0, 1))).reshape(-1)
        return np.tile(cut, 128 // lanes)

    pick = (np.arange(128) // 4) % 2
    scale, shift = line(number[9:12], 4), line(number[12:15], 4)
    lines = [
        line(number[0:3], 4),
        np.where(pick == 1, scale, shift),
        np.where(pick == 0, scale, shift),
        line(number[3:9], 8),
        line(number[15:21], 8),
        line(number[21:27], 8),
        np.zeros(128, int),
        np.zeros(128, int),
    ]
    found["head"] = np.stack(lines)
    return {key: value.astype(np.int32) for key, value in found.items()}


def exact_dot(left, right, dims):
    return lax.dot_general(
        left, right, (dims, ((), ())), precision=lax.Precision.HIGHEST, preferred_element_type=WIDE
    )


def hot(line, count):
    return lax.broadcasted_iota(jnp.int32, (count, line.shape[1]), 0) + 1 == line


def place_rows(place_ref, kernel, o_ref):
    for p in range(4):
        one = jnp.where(hot(place_ref[p : p + 1], kernel.shape[0]), 1.0, 0.0).astype(LOW)
        part = lax.dot_general(one, kernel, (((0,), (0,)), ((), ())), preferred_element_type=WIDE)
        o_ref[:, 64 * p : 64 * p + 64] = part.astype(LOW)


def place_lanes(place_ref, kernel, o_ref):
    for p in range(16):
        one = jnp.where(hot(place_ref[p : p + 1], kernel.shape[0]), 1.0, 0.0).astype(LOW)
        part = lax.dot_general(kernel, one, (((0,), (0,)), ((), ())), preferred_element_type=WIDE)
        o_ref[64 * p : 64 * p + 64] = part.astype(LOW)


def padded_kernel(rows, scratch, width):
    scratch[...] = jnp.zeros(scratch.shape, WIDE)
    for t in range(9):
        value = rows(t)
        scratch[width * t : width * t + value.shape[0]] = value
    return scratch[...].astype(LOW)


def build_small(entry_ref, one_ref, two_ref, norm_ref, head_ref, *refs):
    places = refs[:8]
    entry_one_o, entry_two_o, entry_turned_o, one_o, one_turned_o, two_o, two_turned_o, line_o = refs[8:16]
    par_refs, (small, large) = refs[16:26], refs[26:]
    entry_one = padded_kernel(lambda t: entry_ref[6 * t : 6 * t + 6, 0], small, 8)
    entry_two = padded_kernel(lambda t: entry_ref[6 * t : 6 * t + 6, 1], small, 8)
    exit_one = padded_kernel(lambda t: one_ref[t], small, 8)
    exit_two = padded_kernel(lambda t: two_ref[t], large, 16)
    place_rows(places[0], entry_one, entry_one_o)
    place_rows(places[1], entry_two, entry_two_o)
    place_lanes(places[2], entry_two, entry_turned_o)
    place_lanes(places[3], exit_one, one_o)
    place_rows(places[4], exit_one, one_turned_o)
    place_lanes(places[5], exit_two, two_o)
    place_rows(places[6], exit_two, two_turned_o)
    for norm, par_o in enumerate(par_refs):
        for spot in range(4):
            par_o[:, 64 * spot : 64 * spot + 64] = norm_ref[norm // 5, norm % 5]
    for spot in range(8):
        one = jnp.where(hot(places[7][spot : spot + 1], head_ref.shape[1]), 1.0, 0.0)
        line_o[spot : spot + 1] = exact_dot(head_ref[...], one, ((1,), (0,)))


def build_blocks(kernel_ref, *o_refs):
    count = kernel_ref.shape[0]
    for k, o_ref in enumerate(o_refs):
        if k < count:
            tap = [kernel_ref[k, t].astype(LOW) for t in range(9)]
        else:
            tap = [kernel_ref[k - count, 8 - t].T.astype(LOW) for t in range(9)]
        zero = jnp.zeros((64, 64), LOW)
        for r in range(4):
            for c in range(4):
                parts = [
                    tap[3 * (r - q) + c - s] if 0 <= r - q < 3 and 0 <= c - s < 3 else zero
                    for q in range(2)
                    for s in range(2)
                ]
                row = (((r // 2) * 2 + c // 2) * 4 + (r % 2) * 2 + c % 2) * 64
                o_ref[row : row + 64] = jnp.concatenate(parts, axis=1)


def groups(count):
    head = [(0, 1)] if count % 8 else []
    return head + [(start, 8) for start in range(count % 8, count, 8)]


def runs(count):
    return [list(range(start, min(start + 4, count))) for start in range(0, count, 4)]


def lane_fold(value):
    value = value + pltpu.roll(value, 128, 1)
    return value + pltpu.roll(value, 64, 1)


def total_rows(value):
    return jnp.sum(value, axis=0, keepdims=True)


def edge_masks(odd, count, by_row=True):
    if not odd:
        return lambda k, value: value
    lane = lax.broadcasted_iota(jnp.int32, (count, 1, 256), 2)
    spot = lax.broadcasted_iota(jnp.int32, (count, 1, 256), 0)
    low_column = (lane // 64) % 2 == 0
    low_row = lane < 128
    along, across = (low_column, low_row) if by_row else (low_row, low_column)
    line = jnp.where((spot == 0) & along | (spot == count - 1) & ~along, 0.0, 1.0)
    first = jnp.where(across, 0.0, line)
    last = jnp.where(across, line, 0.0)

    def apply(k, value):
        if k == 0 or k == count - 1:
            return value * (first if k == 0 else last)
        return jnp.concatenate([value[:1] * line[:1], value[1:-1], value[-1:] * line[-1:]], axis=0)

    return apply


def norm_lines(st_ref, par_ref, cells):
    mean = st_ref[0:1, :]
    inv = lax.rsqrt(st_ref[1:2, :] / cells + NORM_EPS)
    return mean, inv, par_ref[0:1, :], par_ref[1:2, :]


def clear_border(ref, count):
    ref[0] = jnp.zeros(ref.shape[1:], ref.dtype)
    ref[count + 1] = jnp.zeros(ref.shape[1:], ref.dtype)
    ref[:, 0] = jnp.zeros((ref.shape[0],) + ref.shape[2:], ref.dtype)
    ref[:, count + 1] = jnp.zeros((ref.shape[0],) + ref.shape[2:], ref.dtype)


class Activation:
    def __init__(self, v_ref, count, st_ref, par_ref, a_ref, odd, cells):
        mean, inv, gain, shift = norm_lines(st_ref, par_ref, cells)
        self.scale = 0.5 * gain * inv
        self.offset = 0.5 * shift - mean * self.scale
        self.inside = edge_masks(odd, count)
        self.pad = 0 if odd else 1
        self.v_ref, self.a_ref, self.count = v_ref, a_ref, count
        if self.pad:
            clear_border(a_ref, count)

    def row(self, i):
        half = self.v_ref[i, : self.count] * self.scale + self.offset
        act = self.inside(i, half * (1.0 + jnp.tanh(half)))
        self.a_ref[i + self.pad, self.pad : self.pad + self.count] = act.astype(LOW)


def staged(own, count, odd, size, before, work, after):
    done = 0
    last = range(0)
    for start in range(0, count, size):
        rows = range(start, min(start + size, count))
        ready = min(own, rows[-1] + 3 if odd else rows[-1] + 2)
        for i in range(done, ready):
            before(i)
        done = ready
        work(rows[0], len(rows))
        for k in last:
            after(k)
        last = rows
    for i in range(done, own):
        before(i)
    for k in last:
        after(k)


def four_views(ref, start, size, count):
    n = ref.shape[2]
    return [
        ref[start + vi : start + vi + size, vj : vj + count].reshape(size * count * n, 256)
        for vi in range(2)
        for vj in range(2)
    ]


class Spread:
    def __init__(self, o_ref, count, odd, by_row):
        self.o_ref, self.count, self.odd, self.by_row = o_ref, count, odd, by_row
        self.inside = edge_masks(odd, count, by_row)
        self.near = None
        self.first = self.second = jnp.zeros((8, 256), WIDE)

    def add(self, k):
        count, n = self.count, self.o_ref.shape[2]
        value = self.o_ref[k, :count] if self.by_row else self.o_ref[:count, k]
        if self.near is None:
            line = self.o_ref[1, 1 : count - 1] if self.by_row else self.o_ref[1 : count - 1, 1]
            line = jnp.sum(line.reshape(-1, 256), 0, keepdims=True)
            self.near = lane_fold(line) / (4 * n * (count - 2))
        rows = self.inside(k, value - self.near).reshape(-1, 8, 256)
        self.first = self.first + jnp.sum(rows, 0)
        self.second = self.second + jnp.sum(rows * rows, 0)

    def store(self, st_ref):
        side_cells = self.count - 1 if self.odd else self.count
        cells = self.o_ref.shape[2] * side_cells**2 * 4
        first = lane_fold(total_rows(self.first)) / cells
        second = lane_fold(total_rows(self.second))
        st_ref[0:1, :] = self.near + first
        st_ref[1:2, :] = second - first * first * cells


def mid_forward(odd, cells, st_ref, par_ref, held_ref, w_ref, state_ref, out_st_ref, far_ref, a_ref, sem):
    count = far_ref.shape[0]
    n = far_ref.shape[2]
    own = count + 1 if odd else count - 1
    v_ref, o_ref = (state_ref.at[0], state_ref.at[1]) if odd else (state_ref.at[1], state_ref.at[0])
    activation = Activation(v_ref, own, st_ref, par_ref, a_ref, odd, cells)
    spread = Spread(o_ref, count, not odd, True)
    copies = []

    def work(k, size):
        left = jnp.concatenate(four_views(a_ref, k, size, count), axis=1)
        value = jnp.dot(left, w_ref[...], preferred_element_type=WIDE).reshape(size, count, n, 256)
        o_ref[k : k + size, :count] = value if odd else value + o_ref[k : k + size, :count]
        copies.append(
            pltpu.make_async_copy(o_ref.at[k : k + size, :count], far_ref.at[k : k + size], sem.at[k])
        )
        copies[-1].start()

    def after(k):
        if k > 0 or count == 1:
            spread.add(k)
        if k == 1:
            spread.add(0)

    staged(own, count, odd, 1, activation.row, work, after)
    spread.store(out_st_ref)
    for copy in copies:
        copy.wait()


def rolled(value, shift):
    shift = shift % 128
    return value if shift == 0 else pltpu.roll(value, shift, 1)


def window_left(x_ref, spot, width):
    count = x_ref.shape[0] // 2 - 1
    n = x_ref.shape[1]
    columns = 128 // width
    first = 2 * spot - 2
    value = rolled(x_ref[...].reshape(-1, 128), -width * first).reshape(count + 1, 2, n, 128)
    if first < 0 or first + 4 > columns:
        column = lax.broadcasted_iota(jnp.int32, (count + 1, 2, n, 128), 3) // width + first
        value = jnp.where((column >= 0) & (column < columns), value, jnp.zeros_like(value))
    return jnp.concatenate(
        [value[r // 2 : r // 2 + count, r % 2].reshape(count * n, 128) for r in range(4)], axis=1
    ).astype(LOW)


def window_forward(width, x_ref, w_ref, state_ref, st_ref, far_ref, sem):
    count, n = far_ref.shape[0], far_ref.shape[2]
    o_ref = state_ref.at[0]
    spread = Spread(o_ref, count, True, False)
    done = []
    for spots in runs(count):
        left = jnp.concatenate([window_left(x_ref, spot, width) for spot in spots], axis=0)
        value = jnp.dot(left, w_ref[...], preferred_element_type=WIDE).reshape(len(spots), count, n, 256)
        for k, spot in enumerate(spots):
            o_ref[:, spot] = value[k]
        for spot in done:
            spread.add(spot)
        done = spots
    copy = pltpu.make_async_copy(o_ref, far_ref, sem.at[0])
    copy.start()
    for spot in done:
        spread.add(spot)
    spread.store(st_ref)
    copy.wait()


def to_rows(value_ref, step, items, store):
    count, n = value_ref.shape[0], value_ref.shape[2]
    room = 128 // items
    per = count // items
    sums = []
    for part in range(items):
        total = None
        for spot in range(part * per, part * per + per):
            moved = rolled(value_ref[:, spot].reshape(-1, 128), step * spot)
            total = moved if total is None else total + moved
        sums.append(total)
    lane = lax.broadcasted_iota(jnp.int32, (count * n, 128), 1) // room
    for item in range(items):
        value = sums[0]
        for part in range(1, items):
            value = jnp.where(lane == (item + part) % items, sums[part], value)
        store(item, rolled(value, -room * item).reshape(count, n, 128))


def exit_forward(cells, step, items, st_ref, par_ref, state_ref, w_ref, o_ref, a_ref, value_ref):
    count = value_ref.shape[0]
    n = value_ref.shape[2]
    activation = Activation(state_ref.at[0], count + 1, st_ref, par_ref, a_ref, True, cells)

    def work(k, size):
        left = jnp.concatenate(four_views(a_ref, k, size, count), axis=1)
        value = jnp.dot(left, w_ref[...], preferred_element_type=WIDE)
        value_ref[k : k + size] = value.reshape(size, count, n, 128)

    staged(count + 1, count, True, 1, activation.row, work, lambda k: None)

    def store(item, value):
        o_ref[item] = value

    to_rows(value_ref, step, items, store)


class ActivationGrads:
    def __init__(self, g_ref, v_ref, count, st_ref, par_ref, a_ref, odd, cells, by_row):
        mean, inv, self.gain, self.shift = norm_lines(st_ref, par_ref, cells)
        self.scale = 0.5 * self.gain * inv
        self.offset = 0.5 * self.shift - mean * self.scale
        self.inside = edge_masks(odd, count, by_row)
        self.pad = 0 if odd else 1
        self.g_ref, self.v_ref, self.a_ref = g_ref, v_ref, a_ref
        self.count, self.by_row = count, by_row
        self.first = self.second = jnp.zeros((8, 256), WIDE)
        if self.pad:
            clear_border(a_ref, count)

    def add(self, k):
        here = (k, slice(0, self.count)) if self.by_row else (slice(0, self.count), k)
        low, high = self.pad, self.pad + self.count
        there = (k + self.pad, slice(low, high)) if self.by_row else (slice(low, high), k + self.pad)
        half = self.v_ref[here] * self.scale + self.offset
        bend = jnp.tanh(half)
        rise = 1.0 + bend
        act = half * rise
        self.a_ref[there] = self.inside(k, act).astype(LOW)
        grad = self.inside(k, self.g_ref[here] * (rise + act * (1.0 - bend)))
        self.g_ref[here] = grad
        self.first = self.first + jnp.sum(grad.reshape(-1, 8, 256), 0)
        self.second = self.second + jnp.sum((grad * half).reshape(-1, 8, 256), 0)

    def store(self, sum_ref):
        first = lane_fold(total_rows(self.first))
        second = lane_fold(total_rows(self.second))
        sum_ref[0:1, :] = first
        sum_ref[1:2, :] = (2.0 * second - self.shift * first) / self.gain


class NormInputGrads:
    def __init__(self, sum_ref, st_ref, par_ref, state_ref, spot, count, low_ref, odd, cells, residual, keep):
        mean, inv, gain, shift = norm_lines(st_ref, par_ref, cells)
        self.scale = 0.5 * gain * inv
        self.slope = -self.scale * inv * sum_ref[1:2, :] / cells
        self.offset = -self.scale * sum_ref[0:1, :] / cells - self.slope * mean
        self.inside = edge_masks(odd, count)
        self.pad = 0 if odd else 1
        self.state_ref, self.low_ref, self.spot, self.count = state_ref, low_ref, spot, count
        self.residual, self.keep = residual, keep
        if self.pad:
            clear_border(low_ref, count)

    def row(self, i):
        state_ref, count = self.state_ref, self.count
        grad = state_ref[0, i, :count] * self.scale + state_ref[self.spot, i, :count] * self.slope + self.offset
        grad = self.inside(i, grad)
        if self.residual:
            grad = grad + state_ref[2, i]
        if self.keep:
            state_ref[2, i] = grad
        self.low_ref[i + self.pad, self.pad : self.pad + count] = grad.astype(LOW)


def pieces(count):
    edges = [count * k // 4 for k in range(5)]
    return list(zip(edges[:-1], edges[1:]))


def mid_backward(odd, residual, cells, *refs):
    sum_ref, st_ref, par_ref, held_ref, w_ref, in_st_ref, in_par_ref, in_v_far = refs[:8]
    state_ref, pair_ref, out_sum_ref, sem = refs[8:]
    count, n = in_v_far.shape[0], in_v_far.shape[2]
    own = count + 1 if odd else count - 1
    low_ref, a_ref = pair_ref.at[0], pair_ref.at[1]
    spot, next_spot = (1, 3) if odd else (3, 1)
    copies = {}
    for k, (low, high) in enumerate(pieces(count)):
        copies[low] = pltpu.make_async_copy(
            in_v_far.at[low:high], state_ref.at[next_spot, low:high, :count], sem.at[k]
        )
        copies[low].start()
    inputs = NormInputGrads(sum_ref, st_ref, par_ref, state_ref, spot, own, low_ref, odd, cells, residual, odd)
    outputs = ActivationGrads(
        state_ref.at[0], state_ref.at[next_spot], count, in_st_ref, in_par_ref, a_ref, not odd, cells, True
    )

    def work(k, size):
        left = jnp.concatenate(four_views(low_ref, k, size, count), axis=1)
        value = jnp.dot(left, w_ref[...], preferred_element_type=WIDE)
        state_ref[0, k : k + size, :count] = value.reshape(size, count, n, 256)

    def after(k):
        if k in copies:
            copies[k].wait()
        outputs.add(k)

    staged(own, count, odd, 17, inputs.row, work, after)
    outputs.store(out_sum_ref)


def window_backward(width, arrays, cells, *refs):
    d_refs = refs[:arrays]
    w_ref, st_ref, par_ref, v_far, state_ref, a_ref, sum_ref, sem = refs[arrays:]
    count, n = v_far.shape[0], v_far.shape[2]
    copy = pltpu.make_async_copy(v_far, state_ref.at[1], sem.at[0])
    copy.start()
    outputs = ActivationGrads(
        state_ref.at[0], state_ref.at[1], count, st_ref, par_ref, a_ref, True, cells, False
    )
    done = []
    for index, spots in enumerate(runs(count)):
        left = jnp.concatenate(
            [
                jnp.concatenate([window_left(d_ref, spot, width) for d_ref in d_refs], axis=1)
                for spot in spots
            ],
            axis=0,
        )
        value = jnp.dot(left, w_ref[...], preferred_element_type=WIDE).reshape(len(spots), count, n, 256)
        for k, spot in enumerate(spots):
            state_ref[0, :, spot] = value[k]
        if index == 1:
            copy.wait()
        for spot in done:
            outputs.add(spot)
        done = spots
    for spot in done:
        outputs.add(spot)
    outputs.store(sum_ref)


def entry_backward(cells, inputs, *refs):
    sum_ref, st_ref, par_ref, state_ref = refs[:4]
    low_ref = refs[5] if inputs else refs[4]
    count = low_ref.shape[0]
    grads = NormInputGrads(sum_ref, st_ref, par_ref, state_ref, 1, count, low_ref, True, cells, True, False)
    for i in range(count):
        grads.row(i)
    if inputs:
        w_ref, low_ref, o_ref, value_ref = refs[4:]
        count, n = value_ref.shape[0], value_ref.shape[2]
        for start, size in groups(count):
            left = jnp.concatenate(four_views(low_ref, start, size, count), axis=1)
            value = jnp.dot(left, w_ref[...], preferred_element_type=WIDE)
            value_ref[start : start + size] = value.reshape(size, count, n, 128)

        def store(item, value):
            o_ref[item] = value

        to_rows(value_ref, 16, 2, store)


def block_weight_grad(odd, spot, pair_ref, *refs):
    o_ref, acc_ref = refs[-2:]
    low_ref, a_ref = pair_ref.at[0], pair_ref.at[1]
    pad = 0 if odd else 1
    count = low_ref.shape[0] - (1 if odd else 2)
    n = low_ref.shape[2]
    for index, (start, size) in enumerate(groups(count)):
        grad = low_ref[start + pad : start + pad + size, pad : pad + count].reshape(size * count * n, 256)
        right = jnp.concatenate(four_views(a_ref, start, size, count), axis=1)
        part = lax.dot_general(grad, right, (((0,), (0,)), ((), ())), preferred_element_type=WIDE)
        if index == 0:
            acc_ref[...] = part
        else:
            acc_ref[...] += part
    for dy in range(3):
        for dx in range(3):
            total = None
            for q in range(2):
                for s in range(2):
                    r, c = dy + q, dx + s
                    lane = ((r // 2) * 2 + c // 2) * 256 + ((r % 2) * 2 + c % 2) * 64
                    part = acc_ref[(2 * q + s) * 64 : (2 * q + s) * 64 + 64, lane : lane + 64]
                    total = part if total is None else total + part
            total = total.T
            start = 288 * spot + 32 * (3 * dy + dx)
            o_ref[start : start + 32, :64] = total[:32]
            o_ref[start : start + 32, 64:] = total[32:]


def window_weight_grad(width, arrays, *refs):
    x_refs = refs[:arrays]
    b_ref, place_ref, o_ref, acc_ref = refs[arrays:]
    count, n = b_ref.shape[0], b_ref.shape[2]
    for spots in runs(count):
        right = jnp.concatenate(
            [
                jnp.concatenate([window_left(x_ref, spot, width) for x_ref in x_refs], axis=1)
                for spot in spots
            ],
            axis=0,
        )
        left = jnp.concatenate([b_ref[:, spot].reshape(count * n, 256) for spot in spots], axis=0)
        part = lax.dot_general(left, right, (((0,), (0,)), ((), ())), preferred_element_type=WIDE)
        if spots[0] == 0:
            acc_ref[...] = part
        else:
            acc_ref[...] += part
    lane = lax.broadcasted_iota(jnp.int32, (64, 128), 1) // 32
    total = None
    for p in range(4):
        parts = []
        for array in range(arrays):
            held = jnp.zeros((64, 128), WIDE)
            for r in range(4):
                start = 512 * array + 128 * r
                value = rolled(acc_ref[64 * p : 64 * p + 64, start : start + 128], 32 * r)
                held = jnp.where(lane == r, value, held)
            parts.append(held)
        one = jnp.where(hot(place_ref[p : p + 1], 72 * arrays), 1.0, 0.0)
        part = exact_dot(one, jnp.concatenate(parts, axis=1), ((1,), (1,)))
        total = part if total is None else total + part
    o_ref[...] = total


def lane_ids(shape):
    return lax.broadcasted_iota(jnp.int32, shape, len(shape) - 1)


def flat_roll(value, shift):
    return rolled(value.reshape(-1, 128), shift).reshape(value.shape)


def valid_lanes(cells):
    held = jnp.where(lane_ids(cells.shape) % 4 == 3, cells, 0.0)
    return flat_roll(held, -1) + flat_roll(held, -2) + flat_roll(held, -3)


def pad_rows(x_ref, values):
    rows, n = values.shape[0], values.shape[1]
    x_ref[0:2] = jnp.zeros((2, n, 128), x_ref.dtype)
    x_ref[2 : 2 + rows] = values.astype(x_ref.dtype)
    x_ref[2 + rows :] = jnp.zeros((2, n, 128), x_ref.dtype)


def column_line(value):
    return jnp.sum(value.reshape(-1, 128), axis=0, keepdims=True)


def checks(shape):
    lane = lane_ids(shape)
    row = lax.broadcasted_iota(jnp.int32, shape, 0)
    return ((row + lane // 4) % 2 == 1) & (lane % 4 != 3)


def prepare(cells_ref, x_ref, logits_ref, sum_ref):
    cells = cells_ref[...]
    lane = lane_ids(cells.shape)
    channel = lane % 4 != 3
    valid = valid_lanes(cells)
    prob = ALPHA + (1.0 - 2.0 * ALPHA) * (cells / 256.0)
    log_in = jnp.log(prob)
    log_out = jnp.log(1.0 - prob)
    logits = jnp.where(channel, log_in - log_out, 0.0)
    jacobian = math.log(1.0 - 2.0 * ALPHA) - log_in - log_out
    logits_ref[...] = logits
    sum_ref[0:1] = column_line(valid)
    sum_ref[1:2] = column_line(valid * (HALF_LOG_TAU + LOG_LEVELS - jacobian))
    odd = checks(cells.shape)
    pad_rows(x_ref, jnp.where(odd, 1.0, logits))


def couple(line_ref, raw_ref, logits_ref, cells_ref, o_ref, bend_ref, sum_ref):
    logits = logits_ref[...]
    valid = valid_lanes(cells_ref[...])
    gain = line_ref[0:1].reshape(1, 1, 128)
    total = jnp.zeros((1, 128), WIDE)
    for q in range(2):
        raw = raw_ref[q] + line_ref[1 + q : 2 + q].reshape(1, 1, 128)
        own = logits_ref[pl.ds(q, raw.shape[0], 2)]
        cells = cells_ref[pl.ds(q, raw.shape[0], 2)]
        lane = lane_ids(raw.shape)
        odd = ((q + lane // 4) % 2 == 1) & (lane % 4 != 3)
        shift = flat_roll(raw, 4 if q == 0 else -4)
        bend = jnp.where(odd, jnp.tanh(raw), 0.0)
        scale = gain * bend
        coupled = jnp.where(odd, own * jnp.exp(scale) + shift, own)
        bend_ref[q] = bend
        total = total - column_line(valid_lanes(cells) * scale)
        o_ref[pl.ds(q, raw.shape[0], 2)] = jnp.where(lane % 4 == 3, cells, coupled)
    sum_ref[...] = total


def enter_two(coupled_ref, x_ref):
    value = coupled_ref[pl.ds(0, coupled_ref.shape[0] // 2, 2)]
    pad_rows(x_ref, jnp.where(lane_ids(value.shape) % 4 == 3, 0.0, value))


def losses(line_ref, count_ref, raw_ref, coupled_ref, scale_d_ref, shift_d_ref, grad_ref, sum_ref):
    half = coupled_ref.shape[0] // 2
    shape = (half, coupled_ref.shape[1], 128)
    channel = lane_ids(shape) % 4 != 3
    top = coupled_ref[pl.ds(0, half, 2)]
    low = coupled_ref[pl.ds(1, half, 2)]
    top_valid = valid_lanes(top)
    low_valid = valid_lanes(low)
    top = jnp.where(channel, top, 0.0)
    low = jnp.where(channel, low, 0.0)

    def rows(item):
        pair = jnp.stack([raw_ref[item], raw_ref[2 + item]], axis=1)
        return pair.reshape(shape) + line_ref[4 + item : 5 + item].reshape(1, 1, 128)

    gain = line_ref[3:4].reshape(1, 1, 128)
    unit = 1.0 / (LOG_TWO * jnp.sum(count_ref[0:1], axis=1, keepdims=True)).reshape(1, 1, 1)
    bend = jnp.tanh(rows(0))
    scale = gain * bend
    grow = jnp.exp(scale)
    latent = jnp.where(channel, low * grow + rows(1), 0.0)
    sum_ref[0:1] = column_line(top_valid * (0.5 * top * top) + low_valid * (0.5 * latent * latent - scale))
    moved = low_valid * unit * latent
    grad_scale = moved * low * grow - low_valid * unit
    raw_grad = grad_scale * gain * (1.0 - bend * bend)
    sum_ref[1:2] = column_line(grad_scale * bend)
    sum_ref[2:3] = column_line(raw_grad)
    sum_ref[3:4] = column_line(moved)
    pad_rows(scale_d_ref, raw_grad)
    pad_rows(shift_d_ref, moved)
    grad_ref[pl.ds(0, half, 2)] = top_valid * unit * top
    grad_ref[pl.ds(1, half, 2)] = moved * grow


def uncouple(mine_ref, line_ref, count_ref, entry_ref, grad_ref, logits_ref, bend_ref, cells_ref, d_ref, sum_ref):
    half = logits_ref.shape[0] // 2
    n = logits_ref.shape[1]
    own_part = pl.ds(pl.multiple_of(mine_ref[0], 8), n)
    gain = line_ref[0:1].reshape(1, 1, 128)
    unit = 1.0 / (LOG_TWO * jnp.sum(count_ref[0:1], axis=1, keepdims=True)).reshape(1, 1, 1)
    lines = [jnp.zeros((1, 128), WIDE)] * 3
    d_ref[0:2] = jnp.zeros((2, n, 128), d_ref.dtype)
    d_ref[2 * half + 2 :] = jnp.zeros((d_ref.shape[0] - 2 * half - 2, n, 128), d_ref.dtype)
    for q in range(2):
        grad = grad_ref[pl.ds(q, half, 2), own_part]
        if q == 0:
            grad = grad + jnp.stack([entry_ref[0, :, own_part], entry_ref[1, :, own_part]], axis=1).reshape(half, n, 128)
        own = logits_ref[pl.ds(q, half, 2)]
        valid = valid_lanes(cells_ref[pl.ds(q, half, 2)])
        bend = bend_ref[q]
        lane = lane_ids(grad.shape)
        odd = ((q + lane // 4) % 2 == 1) & (lane % 4 != 3)
        grad = jnp.where(odd, grad, 0.0)
        grad_scale = jnp.where(odd, grad * own * jnp.exp(gain * bend) - valid * unit, 0.0)
        raw_grad = grad_scale * gain * (1.0 - bend * bend)
        lines[0] = lines[0] + column_line(grad_scale * bend)
        lines[1] = lines[1] + column_line(raw_grad)
        lines[2] = lines[2] + column_line(grad)
        value = raw_grad + flat_roll(grad, -4 if q == 0 else 4)
        d_ref[pl.ds(2 + q, half, 2)] = value.astype(d_ref.dtype)
    for spot in range(3):
        sum_ref[spot : spot + 1] = lines[spot]


def call(kernel, outs, args, name, scratch=(), limit=16, far_in=(), far_out=(), sems=0, aliases=None, scalar_in=()):
    spaces = [
        pltpu.HBM if spot in far_in else pltpu.SMEM if spot in scalar_in else pltpu.VMEM
        for spot in range(len(args))
    ]
    out_spaces = [pltpu.HBM if spot in far_out else pltpu.VMEM for spot in range(len(outs))]
    held = [pltpu.VMEM(shape, dtype) for shape, dtype in scratch]
    args = [pltpu.with_memory_space_constraint(arg, space) if space is pltpu.HBM else arg for arg, space in zip(args, spaces)]
    if sems:
        held.append(pltpu.SemaphoreType.DMA(sems))
    return pl.pallas_call(
        kernel,
        out_shape=[space(shape, dtype) for space, (shape, dtype) in zip(out_spaces, outs)],
        in_specs=[pl.BlockSpec(memory_space=space) for space in spaces],
        out_specs=[pl.BlockSpec(memory_space=space) for space in out_spaces],
        scratch_shapes=held,
        compiler_params=pltpu.CompilerParams(vmem_limit_bytes=limit * 2**20),
        input_output_aliases=aliases or {},
        cost_estimate=pl.CostEstimate(
            flops=int(1e+09 * COSTS.get(name, 0.5)), bytes_accessed=0, transcendentals=0
        ),
        name=name,
    )(*args)


class Net:
    def __init__(self, name, blocks, n, width, group, total, pars, weights, turned_weights):
        self.name = name
        self.even = blocks
        self.odd = blocks + 1
        self.n = n
        self.width = width
        self.group = group
        self.cells = float(total)
        self.own = float(n * blocks * blocks * 4)
        self.pars = pars
        self.weights = weights
        self.turned_weights = turned_weights
        self.far = []
        self.stats = []

    def shape(self, odd, padded=False):
        count = self.odd if odd else self.even
        pad = 2 if padded and not odd else 0
        return (count + pad, count + pad, self.n, 256)

    def keep(self, stats, far):
        self.far.append(far)
        self.stats.append(merge_stats(stats, self.own, self.group))

    def forward(self, x, entry, exit_weights, items):
        held = (2,) + self.shape(True)
        state, stats, far = call(
            functools.partial(window_forward, self.width),
            [(held, WIDE), ((2, 256), WIDE), (self.shape(True), WIDE)],
            [x, entry],
            self.name + "_entry",
            far_out=(2,),
            sems=(1,),
        )
        self.keep(stats, far)
        for index in range(4):
            odd = index % 2 == 0
            state, stats, far = call(
                functools.partial(mid_forward, odd, self.cells),
                [(held, WIDE), ((2, 256), WIDE), (self.shape(not odd), WIDE)],
                [self.stats[index], self.pars[index], state, self.weights[index]],
                self.name + "_forward",
                [(self.shape(odd, True), LOW)],
                far_out=(2,),
                sems=(self.odd,),
                aliases={2: 0},
            )
            self.keep(stats, far)
        return call(
            functools.partial(exit_forward, self.cells, 2 * self.width, items),
            [((items, self.even, self.n, 128), WIDE)],
            [self.stats[4], self.pars[4], state, exit_weights],
            self.name + "_exit",
            [(self.shape(True), LOW), ((self.even, self.even, self.n, 128), WIDE)],
        )[0]

    def backward(self, grads, exit_turned, exit_place, x, entry_turned, entry_place, packets, slots):
        arrays = len(grads)
        held = (4,) + self.shape(True)
        pair_shape = (2, self.even + 2, self.even + 2, self.n, 256)
        state, act, sums = call(
            functools.partial(window_backward, self.width, arrays, self.cells),
            [(held, WIDE), (self.shape(True), LOW), ((2, 256), WIDE)],
            list(grads) + [exit_turned, self.stats[4], self.pars[4], self.far[4]],
            self.name + "_exit_back",
            far_in=(arrays + 3,),
            sems=(1,),
        )
        exit_grad = call(
            functools.partial(window_weight_grad, self.width, arrays),
            [((72 * arrays, 64), WIDE)],
            list(grads) + [act, exit_place],
            self.name + "_exit_weights",
            [((256, 512 * arrays), WIDE)],
        )[0]
        results_of = {}
        sums, exit_grad, *done = lax.optimization_barrier(
            (group_sum(sums, self.group), exit_grad) + slots.get(4, lambda *held: ())(None, exit_grad)
        )
        results_of[4] = done
        norm_grads = [None] * 5
        block_grads = []
        norm_grads[4] = sums
        for index in reversed(range(4)):
            odd = index % 2 == 1
            state, pair, sums = call(
                functools.partial(mid_backward, odd, index == 1, self.cells),
                [(held, WIDE), (pair_shape, LOW), ((2, 256), WIDE)],
                [
                    sums,
                    self.stats[index + 1],
                    self.pars[index + 1],
                    state,
                    self.turned_weights[index],
                    self.stats[index],
                    self.pars[index],
                    self.far[index],
                ],
                self.name + "_back",
                far_in=(7,),
                sems=(4,),
                aliases={3: 0},
            )
            packet = next(held for held in packets if index in held)
            spot = packet.index(index)
            fresh = index == packet[-1]
            block = call(
                functools.partial(block_weight_grad, odd, spot),
                [((288 * len(packet), 128), WIDE)],
                [pair] + ([] if fresh else [block]),
                self.name + "_weights",
                [((256, 1024), WIDE)],
                aliases=None if fresh else {1: 0},
            )[0]
            sums, block, *done = lax.optimization_barrier((group_sum(sums, self.group), block) + slots.get(index, lambda *held: ())(block_grads, exit_grad))
            results_of[index] = done
            norm_grads[index] = sums
            if index == packet[0]:
                block_grads.append(swap_terms(block, self.group))
        args = [sums, self.stats[0], self.pars[0], state]
        outs = [(self.shape(True), LOW)]
        scratch = []
        if entry_turned is not None:
            args.append(entry_turned)
            outs.append(((2, self.even, self.n, 128), WIDE))
            scratch.append(((self.even, self.even, self.n, 128), WIDE))
        results = call(
            functools.partial(entry_backward, self.cells, entry_turned is not None),
            outs,
            args,
            self.name + "_entry_back",
            scratch,
        )

        def entry_grad(token):
            low, unused = lax.optimization_barrier((results[0], token))
            return call(
                functools.partial(window_weight_grad, self.width, 1),
                [((72, 64), WIDE)],
                [x, low, entry_place],
                self.name + "_entry_weights",
                [((256, 512), WIDE)],
            )[0]

        return entry_grad, block_grads, exit_grad, norm_grads, results_of, (results[1] if entry_turned is not None else None)


def adam_blocks(spots, fresh, first, *refs):
    terms, refs = refs[:2], refs[2:]
    sources, refs = refs[:3], refs[3:]
    if not fresh:
        refs = refs[4:]
    targets, (held, out, out_low, in_sem, out_sem) = refs[:4], refs[4:]
    loads = []
    for k, spot in enumerate(spots):
        loads.append(
            [pltpu.make_async_copy(sources[j].at[spot], held.at[k, j], in_sem.at[k, j]) for j in range(3)]
        )
        for copy in loads[-1]:
            copy.start()
    stores = []
    for k, spot in enumerate(spots):
        for copy in loads[k]:
            copy.wait()
        for t in range(9):
            row = 288 * (first + k) + 32 * t
            packed = terms[0][row : row + 32] + terms[1][row : row + 32]
            grad = jnp.concatenate([packed[:, :64], packed[:, 64:]], axis=0)
            news = adamw(held[k, 0, t], held[k, 1, t], held[k, 2, t], grad, RATE_CONV)
            for j in range(3):
                out[k, j, t] = news[j]
            out_low[k, t] = news[3]
        copies = [pltpu.make_async_copy(out.at[k, j], targets[j].at[spot], out_sem.at[k, j]) for j in range(3)]
        copies.append(pltpu.make_async_copy(out_low.at[k], targets[3].at[spot], out_sem.at[k, 3]))
        for copy in copies:
            copy.start()
        stores += copies
    for copy in stores:
        copy.wait()


def step_blocks(spots, terms, first, sources, targets):
    count = len(spots)
    args = list(terms) + list(sources) + list(targets or [])
    shape = sources[0].shape
    head = 2
    return pl.pallas_call(
        functools.partial(adam_blocks, spots, targets is None, first),
        out_shape=[pltpu.HBM(shape, WIDE)] * 3 + [pltpu.HBM(shape, LOW)],
        in_specs=[pl.BlockSpec(memory_space=pltpu.VMEM)] * head
        + [pl.BlockSpec(memory_space=pltpu.HBM)] * (len(args) - head),
        out_specs=[pl.BlockSpec(memory_space=pltpu.HBM)] * 4,
        scratch_shapes=[
            pltpu.VMEM((count, 3) + shape[1:], WIDE),
            pltpu.VMEM((count, 3) + shape[1:], WIDE),
            pltpu.VMEM((count,) + shape[1:], LOW),
            pltpu.SemaphoreType.DMA((count, 3)),
            pltpu.SemaphoreType.DMA((count, 4)),
        ],
        input_output_aliases={} if targets is None else {head + 3 + j: j for j in range(4)},
        compiler_params=pltpu.CompilerParams(vmem_limit_bytes=12 * 2**20),
        cost_estimate=pl.CostEstimate(flops=int(1e+09 * (1 + count)), bytes_accessed=0, transcendentals=0),
        name="step_blocks",
    )(*args[:head], *[pltpu.with_memory_space_constraint(arg, pltpu.HBM) for arg in args[head:]])


def adamw(master, first, second, grad, rate):
    first_new = BETA_ONE * first + (1.0 - BETA_ONE) * grad
    second_new = BETA_TWO * second + (1.0 - BETA_TWO) * grad * grad
    direction = (
        first_new
        / (1.0 - BETA_ONE**STEP)
        / (jnp.sqrt(second_new / (1.0 - BETA_TWO**STEP)) + ADAM_EPS)
    )
    master_new = master - rate * (direction + DECAY * master)
    return (master_new, first_new, second_new, master_new.astype(jnp.bfloat16))


def entry_view(array):
    return array.transpose(1, 2, 3, 0, 4).reshape(54, 2, 64)


def exit_view(array):
    return array.transpose(0, 1, 3, 2).reshape(9, array.shape[3], 64)


def pack_rows(*refs):
    o_ref = refs[-1]
    o_ref[...] = jnp.zeros(o_ref.shape, WIDE)
    row = 0
    for ref in refs[:-1]:
        o_ref[row : row + ref.shape[0], : ref.shape[1]] = ref[...]
        row += ref.shape[0]


def entry_grads(one_ref, one_other, two_ref, two_other, o_ref):
    one = one_ref[...] + one_other[...]
    two = two_ref[0:72, :64] + two_other[0:72, :64]
    for t in range(9):
        o_ref[6 * t : 6 * t + 6, 0] = one[8 * t : 8 * t + 6]
        o_ref[6 * t : 6 * t + 6, 1] = two[8 * t : 8 * t + 6]


def finish_kernel(*refs):
    one_ref, one_other, two_ref, two_other, count_ref = refs[:5]
    norm_sums, place_ref = refs[5:15], refs[15]
    exit_one, exit_two, norm, head = refs[16:19], refs[19:22], refs[22:25], refs[25:28]
    far, near, sem = refs[28:46], refs[46:64], refs[64]
    loss_o, valid_o = near[0:2]
    exit_one_o, exit_two_o, norm_o, head_o = near[2:6], near[6:10], near[10:14], near[14:18]
    one = one_ref[...] + one_other[...]
    two = two_ref[...] + two_other[...]

    def store(outs, index, values):
        for o_ref, value in zip(outs, values):
            o_ref[index] = value

    for t in range(9):
        grad = one[8 * t : 8 * t + 6, :64]
        store(exit_one_o, t, adamw(exit_one[0][t], exit_one[1][t], exit_one[2][t], grad, RATE_CONV))
        grad = two[72 + 16 * t : 84 + 16 * t, :64]
        store(exit_two_o, t, adamw(exit_two[0][t], exit_two[1][t], exit_two[2][t], grad, RATE_CONV))
    for k in range(10):
        spot = (k // 5, k % 5)
        sums = norm_sums[k][...]
        grad = jnp.concatenate([sums[1:2, :64], sums[0:1, :64]], axis=0) * 0.5
        store(norm_o, spot, adamw(norm[0][spot], norm[1][spot], norm[2][spot], grad, RATE_SMALL))
    valid = jnp.sum(count_ref[0:1], axis=1, keepdims=True)
    constant = jnp.sum(count_ref[1:2], axis=1, keepdims=True)
    loss = jnp.sum(two[216:217], axis=1, keepdims=True) + jnp.sum(one[75:76], axis=1, keepdims=True)
    loss_o[...] = (loss + constant) / LOG_TWO
    valid_o[...] = valid

    def folded(line, spot):
        return exact_dot(line, jnp.where(hot(place_ref[spot : spot + 1], head[0].shape[1]), 1.0, 0.0), ((1,), (1,)))

    lane = lax.broadcasted_iota(jnp.int32, (1, 128), 1)
    raw, shift = one[73:74], one[74:75]
    grad = folded(one[72:73], 0) + folded(two[217:218], 3) + folded(two[218:219], 4) + folded(two[219:220], 5)
    grad = grad + folded(jnp.where((lane // 4) % 2 == 1, raw, 0.0), 1) + folded(jnp.where((lane // 4) % 2 == 0, raw, 0.0), 2)
    grad = grad + folded(jnp.where((lane // 4) % 2 == 0, shift, 0.0), 1) + folded(jnp.where((lane // 4) % 2 == 1, shift, 0.0), 2)
    for o_ref, value in zip(head_o, adamw(head[0][...], head[1][...], head[2][...], grad, RATE_SMALL)):
        o_ref[...] = value
    copies = [pltpu.make_async_copy(near[k], far[k], sem.at[k]) for k in range(18)]
    for copy in copies:
        copy.start()
    for copy in copies:
        copy.wait()


def finish(packs, sums, place, exit_one, exit_two, norm, head):
    outs = [((1, 1), WIDE)] * 2
    for first in (exit_one[0], exit_two[0], norm[0], head[0]):
        outs += [(first.shape, WIDE)] * 3 + [(first.shape, LOW)]
    return call(
        finish_kernel,
        outs,
        packs + sums + [place] + exit_one + exit_two + norm + head,
        "finish",
        outs,
        far_out=tuple(range(18)),
        sems=(18,),
    )


def body(
    pixels,
    valid,
    entry_conv,
    entry_first,
    entry_second,
    block_conv,
    block_first,
    block_second,
    exit_one,
    exit_one_first,
    exit_one_second,
    exit_two,
    exit_two_first,
    exit_two_second,
    norm_params,
    norm_first,
    norm_second,
    head_params,
    head_first,
    head_second,
):
    batch = pixels.shape[0] * lax.axis_size("batch")
    height = pixels.shape[1] * lax.axis_size("rows")
    group = group_bits(batch)
    small = group[:-1]
    last = group[-1]
    own = batch >> len(group)
    wide = 2 * own
    cells = jnp.concatenate([pixels, valid[..., None].astype(WIDE)], axis=3)
    cells = cells.reshape(pixels.shape[0], pixels.shape[1], 128).transpose(1, 0, 2)
    cells = distribute(cells, group)

    place = placements()
    small_places = [
        jnp.asarray(place[key])
        for key in (
            "entry_one",
            "entry_two",
            "entry_two_turned",
            "exit_one",
            "exit_one_turned",
            "exit_two",
            "exit_two_turned",
        )
    ]
    fold = [
        jnp.asarray(place[key + "_fold"])
        for key in ("entry_one", "entry_two", "exit_one_turned", "exit_two_turned")
    ]
    (
        entry_one_w,
        entry_two_w,
        entry_turned_w,
        exit_one_w,
        exit_one_turned_w,
        exit_two_w,
        exit_two_turned_w,
        head_lines,
        *par_lines,
    ) = call(
        build_small,
        [
            ((512, 256), LOW),
            ((512, 256), LOW),
            ((1024, 128), LOW),
            ((1024, 128), LOW),
            ((512, 256), LOW),
            ((1024, 128), LOW),
            ((1024, 256), LOW),
            ((8, 128), WIDE),
        ]
        + [((2, 256), WIDE)] * 10,
        [
            entry_view(entry_conv),
            exit_view(exit_one),
            exit_view(exit_two),
            norm_params,
            head_params[None],
        ]
        + small_places
        + [jnp.asarray(place["head"])],
        "build_small",
        [((72, 64), WIDE), ((144, 64), WIDE)],
    )
    blocks = call(build_blocks, [((1024, 256), LOW)] * 16, [block_conv.reshape(8, 9, 64, 64)], "build_blocks")
    weights = [[blocks[4 * j + k] for k in range(4)] for j in range(2)]
    turned_w = [[blocks[8 + 4 * j + k] for k in range(4)] for j in range(2)]
    pars = [[par_lines[5 * j + k] for k in range(5)] for j in range(2)]

    one = Net("one", height // 2, own, 4, group, batch * height * height, pars[0], weights[0], turned_w[0])
    two = Net("two", height // 4, wide, 8, small, batch * (height // 2) ** 2, pars[1], weights[1], turned_w[1])

    rows = height
    x_one, logits, first_sums = call(
        prepare,
        [((rows + 4, own, 128), WIDE), ((rows, own, 128), WIDE), ((2, 128), WIDE)],
        [cells],
        "prepare",
    )
    first_sums = group_sum(first_sums, group)
    mine, x_one = lax.optimization_barrier((side(last) * own, x_one))
    raw_one = one.forward(x_one, entry_one_w, exit_one_w, 2)
    coupled, bend_one, couple_sums = call(
        couple,
        [((rows, own, 128), WIDE), ((2, rows // 2, own, 128), WIDE), ((1, 128), WIDE)],
        [head_lines, raw_one, logits, cells],
        "couple",
    )
    coupled = joined(coupled, swap(coupled, last), mine, 1)
    x_two = call(enter_two, [((rows // 2 + 4, wide, 128), WIDE)], [coupled], "enter_two")[0]
    raw_two = two.forward(x_two, entry_two_w, exit_two_w, 4)
    scale_d, shift_d, grad_coupled, loss_sums = call(
        losses,
        [
            ((rows // 2 + 4, wide, 128), WIDE),
            ((rows // 2 + 4, wide, 128), WIDE),
            ((rows, wide, 128), WIDE),
            ((4, 128), WIDE),
        ],
        [
            head_lines,
            first_sums,
            raw_two,
            coupled,
        ],
        "losses",
    )
    entry_two, blocks_two, exit_two_part, norms_two, unused, grad_first = two.backward(
        [scale_d, shift_d], exit_two_turned_w, fold[3], x_two, entry_turned_w, fold[1], [[0, 1, 2, 3]], {}
    )
    def send_two(held, exit_grad):
        rows = call(pack_rows, [((224, 128), WIDE)], [entry_two(exit_grad), exit_two_part, loss_sums], "pack_two")[0]
        return tuple(swap_terms(rows, small))

    def send_one(held, exit_grad):
        rows = call(pack_rows, [((80, 128), WIDE)], [exit_grad, one_sums, couple_sums], "pack_one")[0]
        return tuple(swap_terms(rows, group))

    sources = [part.reshape(8, 9, 64, 64) for part in (block_conv, block_first, block_second)]
    steps = {}

    def step(key, spots, terms, first):
        def run(held, exit_grad):
            steps[key] = tuple(step_blocks(spots, terms(held), first, sources, steps.get(key - 1)))
            return steps[key]

        return run

    one_d, one_sums = call(
        uncouple,
        [((rows + 4, own, 128), WIDE), ((3, 128), WIDE)],
        [jnp.reshape(mine, (1,)), head_lines, first_sums, grad_first, grad_coupled, logits, bend_one, cells],
        "uncouple",
        scalar_in=(0,),
    )
    slots = {
        4: send_two,
        3: send_one,
        2: step(0, (4, 5), lambda held: blocks_two[0], 0),
        0: step(1, (6, 7), lambda held: blocks_two[0], 2),
    }
    entry_one, blocks_one, exit_one_part, norms_one, done, unused = one.backward(
        [one_d], exit_one_turned_w, fold[2], x_one, None, fold[0], [[1, 2, 3], [0]], slots
    )
    entry_one, *blocks_done = lax.optimization_barrier((entry_one(first_sums), *blocks_one[0]))
    entry_one = swap_terms(entry_one, group)
    pack_two, pack_one = list(done[4]), list(done[3])
    stepped = step_blocks((1, 2, 3), blocks_done, 0, sources, done[0])
    finished = finish(
        pack_one + pack_two,
        [first_sums] + norms_one + norms_two,
        jnp.asarray(place["head"]),
        [exit_view(part) for part in (exit_one, exit_one_first, exit_one_second)],
        [exit_view(part) for part in (exit_two, exit_two_first, exit_two_second)],
        [norm_params, norm_first, norm_second],
        [part[None] for part in (head_params, head_first, head_second)],
    )
    stepped = step_blocks((0,), blocks_one[1], 0, sources, stepped)
    entry_grad = call(
        entry_grads, [((54, 2, 64), WIDE)], entry_one + pack_two, "entry_grads"
    )[0]
    entry_steps = adamw(
        entry_view(entry_conv), entry_view(entry_first), entry_view(entry_second), entry_grad, RATE_CONV
    )
    entry_out = tuple(
        part.reshape(3, 3, 6, 2, 64).transpose(3, 0, 1, 2, 4) for part in entry_steps
    )
    one_out = tuple(part.reshape(3, 3, 6, 64).transpose(0, 1, 3, 2) for part in finished[2:6])
    two_out = tuple(part.reshape(3, 3, 12, 64).transpose(0, 1, 3, 2) for part in finished[6:10])
    return (
        (finished[0].reshape(()), finished[1].reshape(()))
        + entry_out
        + tuple(part.reshape(block_conv.shape) for part in stepped)
        + one_out
        + two_out
        + tuple(finished[10:14])
        + tuple(part.reshape(head_params.shape) for part in finished[14:18])
    )


def solution(mesh):
    placed = (P("batch", "rows", None, None), P("batch", "rows", None)) + (P(),) * 18
    return jax.shard_map(body, mesh=mesh, in_specs=placed, out_specs=(P(),) * 26, check_vma=False)
```

```python
import functools
import math

import jax
import jax.numpy as jnp
import numpy as np
from jax import lax
from jax.experimental import pallas as pl
from jax.experimental.pallas import tpu as pltpu
from jax.sharding import PartitionSpec as P

STEP = 10
ALPHA = 0.05
NORM_EPS = 1e-05
BETA_ONE = 0.9
BETA_TWO = 0.999
ADAM_EPS = 1e-08
DECAY = 0.01
RATE_CONV = 1.0
RATE_SMALL = 10.0
LOG_TWO = math.log(2.0)
HALF_LOG_TAU = 0.5 * math.log(2.0 * math.pi)
LOG_LEVELS = math.log(256.0)
IMAGES = 16
BITS = (("batch", 1), ("batch", 2), ("rows", 1), ("rows", 2), ("batch", 4), ("batch", 8), ("batch", 16), ("batch", 32))
LOW = jnp.bfloat16
WIDE = jnp.float32
COSTS = {
    "one_entry": 4.0,
    "one_forward": 3.7,
    "one_exit": 2.5,
    "one_exit_back": 5.7,
    "one_exit_weights": 2.6,
    "one_back": 5.4,
    "one_weights": 3.0,
    "one_entry_weights": 2.7,
    "two_entry": 2.7,
    "two_forward": 2.5,
    "two_exit": 1.4,
    "two_exit_back": 4.1,
    "two_exit_weights": 3.7,
    "two_back": 3.0,
    "two_weights": 1.9,
    "two_entry_back": 1.5,
    "two_entry_weights": 1.9,
    "build_small": 1.9,
    "build_blocks": 1.0,
    "finish": 1.2,
}


def axis_bits():
    return [bit for bit in BITS if bit[1] < lax.axis_size(bit[0])]


def group_bits(batch):
    bits = axis_bits()
    count = max(batch // IMAGES, 1).bit_length() - 1
    return bits[: min(count, len(bits))]


def swap(value, bit):
    axis, mask = bit
    return lax.ppermute(value, axis, [(i, i ^ mask) for i in range(lax.axis_size(axis))])


def side(bit):
    return (lax.axis_index(bit[0]) // bit[1]) % 2


def group_sum(value, bits):
    for bit in bits:
        value = jax.tree.map(lambda own: own + swap(own, bit), value)
    return value


def travel(sums, bits, work):
    held = sums
    if len(bits) > 1:
        held = sums + swap(sums, bits[0])
        bits = bits[1:]
    results = work(held)
    return lax.optimization_barrier((group_sum(held, bits),) + tuple(results))


def tied(values, token):
    return lax.optimization_barrier((tuple(values), token))[0]


def swap_terms(value, bits):
    value = group_sum(value, bits[:-1])
    return [value, swap(value, bits[-1])]


def joined(own, other, mine, dim):
    first = jnp.where(mine == 0, own, other)
    second = jnp.where(mine == 0, other, own)
    return jnp.concatenate([first, second], axis=dim)


def chosen_part(label, parts):
    found = []
    for k in range(len(parts)):
        value = parts[k]
        for own in range(1, len(parts)):
            value = jnp.where(label == own, parts[k ^ own], value)
        found.append(value)
    return found


def split_parts(label_ref, cells_ref, *o_refs):
    count = cells_ref.shape[1] // len(o_refs)
    parts = [cells_ref[:, count * k : count * k + count] for k in range(len(o_refs))]
    for o_ref, value in zip(o_refs, chosen_part(label_ref[0], parts)):
        o_ref[...] = value


def lay_parts(dim, label_ref, *refs):
    o_ref = refs[-1]
    parts = [ref[...] for ref in refs[:-1]]
    size = parts[0].shape[dim]
    for k, value in enumerate(chosen_part(label_ref[0], parts)):
        if dim == 0:
            o_ref[size * k : size * k + size] = value
        else:
            o_ref[:, size * k : size * k + size] = value


def distribute(cells, group, beside):
    bands = lax.axis_size("rows")
    rows, images = cells.shape[:2]
    row = lax.axis_index("rows")
    mask = sum(bit[1] for bit in group if bit[0] == "rows")
    share = images // (mask + 1)
    pieces = call(
        split_parts,
        [((rows, share, 128), WIDE)] * (mask + 1),
        [jnp.reshape(row & mask, (1,)), cells],
        "split_parts",
        scalar_in=(0,),
    )
    came = [pieces[0]] + [swap(pieces[k & mask], ("rows", k)) for k in range(1, bands)]
    came, beside = lax.optimization_barrier((came, beside))
    cells = call(
        functools.partial(lay_parts, 0),
        [((bands * rows, share, 128), WIDE)],
        [jnp.reshape(row, (1,))] + came,
        "lay_bands",
        scalar_in=(0,),
    )[0]
    others = [bit[1] for bit in axis_bits() if bit[0] == "batch" and bit not in group]
    if not others:
        return cells, beside
    low = others[0]
    came = [cells] + [swap(cells, ("batch", k * low)) for k in range(1, 2 ** len(others))]
    cells = call(
        functools.partial(lay_parts, 1),
        [((bands * rows, share * len(came), 128), WIDE)],
        [jnp.reshape(lax.axis_index("batch") // low, (1,))] + came,
        "lay_images",
        scalar_in=(0,),
    )[0]
    return cells, beside


def merge_stats(both, count, group):
    for bit in group:
        both = call(
            functools.partial(merge_pair, 0.5 * count), [((2, 256), WIDE)], [both, swap(both, bit)], "merge"
        )[0]
        count = 2 * count
    return both


def merge_pair(weight, own_ref, other_ref, o_ref):
    gap = own_ref[0:1] - other_ref[0:1]
    o_ref[0:1] = 0.5 * (own_ref[0:1] + other_ref[0:1])
    o_ref[1:2] = own_ref[1:2] + other_ref[1:2] + gap * gap * weight


def blockify(kernel):
    rows = np.stack([np.pad(kernel, ((q, 1 - q), (0, 0), (0, 0), (0, 0))) for q in range(2)], axis=3)
    return np.stack([np.pad(rows, ((0, 0), (s, 1 - s), (0, 0), (0, 0), (0, 0))) for s in range(2)], axis=4)


def turned(kernel):
    return np.flip(kernel, (0, 1)).transpose(0, 1, 3, 2)


def views(blocked):
    rest = blocked.shape[2:]
    split = blocked.reshape((2, 2, 2, 2) + rest)
    return split.transpose((0, 2, 1, 3) + tuple(range(4, 4 + len(rest)))).reshape((16,) + rest)


def mates(blocked):
    return np.flip(blocked.reshape(4, 2, 2, *blocked.shape[2:]), 2).reshape(blocked.shape)


def spread(values, axis):
    shape = values.shape
    cut = values.reshape(shape[:axis] + (2, 3) + shape[axis + 1 :])
    pad = [(0, 0)] * cut.ndim
    pad[axis + 1] = (0, 1)
    return np.pad(cut, pad).reshape(shape[:axis] + (8,) + shape[axis + 1 :])


def window_rows(weights):
    flat = weights.reshape(4, -1, 4)
    return np.pad(flat, ((0, 0), (0, 128 - flat.shape[1]), (0, 0))).reshape(512, 4)


def checker(odd):
    return ((np.arange(4)[:, None] + np.arange(4)[None, :]) % 2 == odd).reshape(4, 4, 1, 1)


def chosen(blocked, odd):
    both = np.where(checker(odd), blocked[:, :, :3], mates(blocked)[:, :, 3:])
    return window_rows(np.pad(both, ((0, 0), (0, 0), (0, 1), (0, 0))))


def numbered(channels, last):
    pad = 8 if channels == 6 else 16
    number = (pad * np.arange(9)[:, None] + np.arange(1, channels + 1)).reshape(3, 3, 1, channels)
    return number if last else number.transpose(0, 1, 3, 2)


@functools.cache
def placements():
    odd = (np.arange(2)[:, None] + np.arange(2)[None, :]) % 2 == 1
    found = {}
    blocked = blockify(numbered(6, False)).reshape(4, 4, 6, 4)
    found["entry_one"] = chosen(blocked, 0).T
    found["entry_two"] = window_rows(spread(blocked, 2)).T
    blocked = views(blockify(turned(numbered(6, False))))
    lanes = spread(blocked.reshape(16, 2, 2, 6), 3).reshape(16, 2, 16)
    lanes = np.pad(lanes, ((0, 0), (0, 0), (0, 48))).reshape(16, 128)
    found["entry_two_turned"] = lanes
    blocked = views(blockify(numbered(6, True))).reshape(16, 2, 2, 6)
    both = np.where(odd[None, :, :, None], blocked[..., :3], np.flip(blocked, 2)[..., 3:])
    lanes = np.pad(both, ((0, 0), (0, 0), (0, 0), (0, 1))).reshape(16, 2, 8)
    lanes = np.pad(lanes, ((0, 0), (0, 0), (0, 56))).reshape(16, 128)
    found["exit_one"] = lanes
    blocked = blockify(turned(numbered(6, True))).reshape(4, 4, 6, 4)
    found["exit_one_turned"] = chosen(blocked, 1).T
    blocked = views(blockify(numbered(12, True))).reshape(16, 2, 2, 2, 6)
    lanes = spread(blocked, 4).transpose(0, 1, 3, 2, 4).reshape(16, 4, 16)
    lanes = np.pad(lanes, ((0, 0), (0, 0), (0, 16))).reshape(16, 128)
    found["exit_two"] = lanes
    blocked = blockify(turned(numbered(12, True))).reshape(4, 4, 12, 4)
    pair = [window_rows(spread(blocked[:, :, 6 * s : 6 * s + 6], 2)) for s in range(2)]
    found["exit_two_turned"] = np.concatenate(pair).T
    for key in ("entry_one", "entry_two", "exit_one_turned", "exit_two_turned"):
        found[key + "_fold"] = found[key].reshape(4, -1, 128)[:, :, :32].reshape(4, -1)
    number = np.arange(1, 28)

    def line(values, lanes):
        cut = np.pad(values.reshape(-1, 3), ((0, 0), (0, 1))).reshape(-1)
        return np.tile(cut, 128 // lanes)

    pick = (np.arange(128) // 4) % 2
    scale, shift = line(number[9:12], 4), line(number[12:15], 4)
    lines = [
        line(number[0:3], 4),
        np.where(pick == 1, scale, shift),
        np.where(pick == 0, scale, shift),
        line(number[3:9], 8),
        line(number[15:21], 8),
        line(number[21:27], 8),
        np.zeros(128, int),
        np.zeros(128, int),
    ]
    found["head"] = np.stack(lines)
    return {key: value.astype(np.int32) for key, value in found.items()}


def exact_dot(left, right, dims):
    return lax.dot_general(
        left, right, (dims, ((), ())), precision=lax.Precision.HIGHEST, preferred_element_type=WIDE
    )


def hot(line, count):
    return lax.broadcasted_iota(jnp.int32, (count, line.shape[1]), 0) + 1 == line


def place_rows(place_ref, kernel, o_ref):
    for p in range(4):
        one = jnp.where(hot(place_ref[p : p + 1], kernel.shape[0]), 1.0, 0.0).astype(LOW)
        part = lax.dot_general(one, kernel, (((0,), (0,)), ((), ())), preferred_element_type=WIDE)
        o_ref[:, 64 * p : 64 * p + 64] = part.astype(LOW)


def place_lanes(place_ref, kernel, o_ref):
    for p in range(16):
        one = jnp.where(hot(place_ref[p : p + 1], kernel.shape[0]), 1.0, 0.0).astype(LOW)
        part = lax.dot_general(kernel, one, (((0,), (0,)), ((), ())), preferred_element_type=WIDE)
        o_ref[64 * p : 64 * p + 64] = part.astype(LOW)


def padded_kernel(rows, scratch, width):
    scratch[...] = jnp.zeros(scratch.shape, WIDE)
    for t in range(9):
        value = rows(t)
        scratch[width * t : width * t + value.shape[0]] = value
    return scratch[...].astype(LOW)


def build_small(entry_ref, one_ref, two_ref, norm_ref, head_ref, *refs):
    places = refs[:8]
    entry_one_o, entry_two_o, entry_turned_o, one_o, one_turned_o, two_o, two_turned_o, line_o = refs[8:16]
    par_refs, (small, large) = refs[16:26], refs[26:]
    entry_one = padded_kernel(lambda t: entry_ref[6 * t : 6 * t + 6, 0], small, 8)
    entry_two = padded_kernel(lambda t: entry_ref[6 * t : 6 * t + 6, 1], small, 8)
    exit_one = padded_kernel(lambda t: one_ref[t], small, 8)
    exit_two = padded_kernel(lambda t: two_ref[t], large, 16)
    place_rows(places[0], entry_one, entry_one_o)
    place_rows(places[1], entry_two, entry_two_o)
    place_lanes(places[2], entry_two, entry_turned_o)
    place_lanes(places[3], exit_one, one_o)
    place_rows(places[4], exit_one, one_turned_o)
    place_lanes(places[5], exit_two, two_o)
    place_rows(places[6], exit_two, two_turned_o)
    for norm, par_o in enumerate(par_refs):
        for spot in range(4):
            par_o[:, 64 * spot : 64 * spot + 64] = norm_ref[norm // 5, norm % 5]
    for spot in range(8):
        one = jnp.where(hot(places[7][spot : spot + 1], head_ref.shape[1]), 1.0, 0.0)
        line_o[spot : spot + 1] = exact_dot(head_ref[...], one, ((1,), (0,)))


def build_blocks(kernel_ref, *o_refs):
    count = kernel_ref.shape[0]
    for k, o_ref in enumerate(o_refs):
        if k < count:
            tap = [kernel_ref[k, t].astype(LOW) for t in range(9)]
        else:
            tap = [kernel_ref[k - count, 8 - t].T.astype(LOW) for t in range(9)]
        zero = jnp.zeros((64, 64), LOW)
        for r in range(4):
            for c in range(4):
                parts = [
                    tap[3 * (r - q) + c - s] if 0 <= r - q < 3 and 0 <= c - s < 3 else zero
                    for q in range(2)
                    for s in range(2)
                ]
                row = (((r // 2) * 2 + c // 2) * 4 + (r % 2) * 2 + c % 2) * 64
                o_ref[row : row + 64] = jnp.concatenate(parts, axis=1)


def groups(count):
    head = [(0, 1)] if count % 8 else []
    return head + [(start, 8) for start in range(count % 8, count, 8)]


def runs(count):
    return [list(range(start, min(start + 4, count))) for start in range(0, count, 4)]


def lane_fold(value):
    value = value + pltpu.roll(value, 128, 1)
    return value + pltpu.roll(value, 64, 1)


def total_rows(value):
    return jnp.sum(value, axis=0, keepdims=True)


def edge_masks(odd, count, by_row=True):
    if not odd:
        return lambda k, value: value
    lane = lax.broadcasted_iota(jnp.int32, (count, 1, 256), 2)
    spot = lax.broadcasted_iota(jnp.int32, (count, 1, 256), 0)
    low_column = (lane // 64) % 2 == 0
    low_row = lane < 128
    along, across = (low_column, low_row) if by_row else (low_row, low_column)
    line = jnp.where((spot == 0) & along | (spot == count - 1) & ~along, 0.0, 1.0)
    first = jnp.where(across, 0.0, line)
    last = jnp.where(across, line, 0.0)

    def apply(k, value):
        if k == 0 or k == count - 1:
            return value * (first if k == 0 else last)
        return jnp.concatenate([value[:1] * line[:1], value[1:-1], value[-1:] * line[-1:]], axis=0)

    return apply


def norm_lines(st_ref, par_ref, cells):
    mean = st_ref[0:1, :]
    inv = lax.rsqrt(st_ref[1:2, :] / cells + NORM_EPS)
    return mean, inv, par_ref[0:1, :], par_ref[1:2, :]


def clear_border(ref, count):
    ref[0] = jnp.zeros(ref.shape[1:], ref.dtype)
    ref[count + 1] = jnp.zeros(ref.shape[1:], ref.dtype)
    ref[:, 0] = jnp.zeros((ref.shape[0],) + ref.shape[2:], ref.dtype)
    ref[:, count + 1] = jnp.zeros((ref.shape[0],) + ref.shape[2:], ref.dtype)


class Activation:
    def __init__(self, v_ref, count, st_ref, par_ref, a_ref, odd, cells):
        mean, inv, gain, shift = norm_lines(st_ref, par_ref, cells)
        self.scale = 0.5 * gain * inv
        self.offset = 0.5 * shift - mean * self.scale
        self.inside = edge_masks(odd, count)
        self.pad = 0 if odd else 1
        self.v_ref, self.a_ref, self.count = v_ref, a_ref, count
        if self.pad:
            clear_border(a_ref, count)

    def row(self, i):
        half = self.v_ref[i, : self.count] * self.scale + self.offset
        act = self.inside(i, half * (1.0 + jnp.tanh(half)))
        self.a_ref[i + self.pad, self.pad : self.pad + self.count] = act.astype(LOW)


def staged(own, count, odd, size, before, work, after):
    done = 0
    last = range(0)
    for start in range(0, count, size):
        rows = range(start, min(start + size, count))
        ready = min(own, rows[-1] + 3 if odd else rows[-1] + 2)
        for i in range(done, ready):
            before(i)
        done = ready
        work(rows[0], len(rows))
        for k in last:
            after(k)
        last = rows
    for i in range(done, own):
        before(i)
    for k in last:
        after(k)


def four_views(ref, start, size, count):
    n = ref.shape[2]
    return [
        ref[start + vi : start + vi + size, vj : vj + count].reshape(size * count * n, 256)
        for vi in range(2)
        for vj in range(2)
    ]


class Spread:
    def __init__(self, o_ref, count, odd, by_row):
        self.o_ref, self.count, self.odd, self.by_row = o_ref, count, odd, by_row
        self.inside = edge_masks(odd, count, by_row)
        self.near = None
        self.first = self.second = jnp.zeros((8, 256), WIDE)

    def add(self, k):
        count, n = self.count, self.o_ref.shape[2]
        value = self.o_ref[k, :count] if self.by_row else self.o_ref[:count, k]
        if self.near is None:
            line = self.o_ref[1, 1 : count - 1] if self.by_row else self.o_ref[1 : count - 1, 1]
            line = jnp.sum(line.reshape(-1, 256), 0, keepdims=True)
            self.near = lane_fold(line) / (4 * n * (count - 2))
        rows = self.inside(k, value - self.near).reshape(-1, 8, 256)
        self.first = self.first + jnp.sum(rows, 0)
        self.second = self.second + jnp.sum(rows * rows, 0)

    def store(self, st_ref):
        side_cells = self.count - 1 if self.odd else self.count
        cells = self.o_ref.shape[2] * side_cells**2 * 4
        first = lane_fold(total_rows(self.first)) / cells
        second = lane_fold(total_rows(self.second))
        st_ref[0:1, :] = self.near + first
        st_ref[1:2, :] = second - first * first * cells


def mid_forward(odd, cells, st_ref, par_ref, held_ref, w_ref, state_ref, out_st_ref, far_ref, a_ref, sem):
    count = far_ref.shape[0]
    n = far_ref.shape[2]
    own = count + 1 if odd else count - 1
    v_ref, o_ref = (state_ref.at[0], state_ref.at[1]) if odd else (state_ref.at[1], state_ref.at[0])
    activation = Activation(v_ref, own, st_ref, par_ref, a_ref, odd, cells)
    spread = Spread(o_ref, count, not odd, True)
    copies = []

    def work(k, size):
        left = jnp.concatenate(four_views(a_ref, k, size, count), axis=1)
        value = jnp.dot(left, w_ref[...], preferred_element_type=WIDE).reshape(size, count, n, 256)
        o_ref[k : k + size, :count] = value if odd else value + o_ref[k : k + size, :count]
        copies.append(
            pltpu.make_async_copy(o_ref.at[k : k + size, :count], far_ref.at[k : k + size], sem.at[k])
        )
        copies[-1].start()

    def after(k):
        if k > 0 or count == 1:
            spread.add(k)
        if k == 1:
            spread.add(0)

    staged(own, count, odd, 1, activation.row, work, after)
    spread.store(out_st_ref)
    for copy in copies:
        copy.wait()


def rolled(value, shift):
    shift = shift % 128
    return value if shift == 0 else pltpu.roll(value, shift, 1)


def window_left(x_ref, spot, width):
    count = x_ref.shape[0] // 2 - 1
    n = x_ref.shape[1]
    columns = 128 // width
    first = 2 * spot - 2
    value = rolled(x_ref[...].reshape(-1, 128), -width * first).reshape(count + 1, 2, n, 128)
    if first < 0 or first + 4 > columns:
        column = lax.broadcasted_iota(jnp.int32, (count + 1, 2, n, 128), 3) // width + first
        value = jnp.where((column >= 0) & (column < columns), value, jnp.zeros_like(value))
    return jnp.concatenate(
        [value[r // 2 : r // 2 + count, r % 2].reshape(count * n, 128) for r in range(4)], axis=1
    ).astype(LOW)


def window_forward(width, x_ref, w_ref, state_ref, st_ref, far_ref, sem):
    count, n = far_ref.shape[0], far_ref.shape[2]
    o_ref = state_ref.at[0]
    spread = Spread(o_ref, count, True, False)
    done = []
    for spots in runs(count):
        left = jnp.concatenate([window_left(x_ref, spot, width) for spot in spots], axis=0)
        value = jnp.dot(left, w_ref[...], preferred_element_type=WIDE).reshape(len(spots), count, n, 256)
        for k, spot in enumerate(spots):
            o_ref[:, spot] = value[k]
        for spot in done:
            spread.add(spot)
        done = spots
    copy = pltpu.make_async_copy(o_ref, far_ref, sem.at[0])
    copy.start()
    for spot in done:
        spread.add(spot)
    spread.store(st_ref)
    copy.wait()


def to_rows(value_ref, step, items, store):
    count, n = value_ref.shape[0], value_ref.shape[2]
    room = 128 // items
    per = count // items
    sums = []
    for part in range(items):
        total = None
        for spot in range(part * per, part * per + per):
            moved = rolled(value_ref[:, spot].reshape(-1, 128), step * spot)
            total = moved if total is None else total + moved
        sums.append(total)
    lane = lax.broadcasted_iota(jnp.int32, (count * n, 128), 1) // room
    for item in range(items):
        value = sums[0]
        for part in range(1, items):
            value = jnp.where(lane == (item + part) % items, sums[part], value)
        store(item, rolled(value, -room * item).reshape(count, n, 128))


def exit_forward(cells, step, items, st_ref, par_ref, state_ref, w_ref, o_ref, a_ref, value_ref):
    count = value_ref.shape[0]
    n = value_ref.shape[2]
    activation = Activation(state_ref.at[0], count + 1, st_ref, par_ref, a_ref, True, cells)

    def work(k, size):
        left = jnp.concatenate(four_views(a_ref, k, size, count), axis=1)
        value = jnp.dot(left, w_ref[...], preferred_element_type=WIDE)
        value_ref[k : k + size] = value.reshape(size, count, n, 128)

    staged(count + 1, count, True, 1, activation.row, work, lambda k: None)

    def store(item, value):
        o_ref[item] = value

    to_rows(value_ref, step, items, store)


class ActivationGrads:
    def __init__(self, g_ref, v_ref, count, st_ref, par_ref, a_ref, odd, cells, by_row):
        mean, inv, self.gain, self.shift = norm_lines(st_ref, par_ref, cells)
        self.scale = 0.5 * self.gain * inv
        self.offset = 0.5 * self.shift - mean * self.scale
        self.inside = edge_masks(odd, count, by_row)
        self.pad = 0 if odd else 1
        self.g_ref, self.v_ref, self.a_ref = g_ref, v_ref, a_ref
        self.count, self.by_row = count, by_row
        self.first = self.second = jnp.zeros((8, 256), WIDE)
        if self.pad:
            clear_border(a_ref, count)

    def add(self, k):
        here = (k, slice(0, self.count)) if self.by_row else (slice(0, self.count), k)
        low, high = self.pad, self.pad + self.count
        there = (k + self.pad, slice(low, high)) if self.by_row else (slice(low, high), k + self.pad)
        half = self.v_ref[here] * self.scale + self.offset
        bend = jnp.tanh(half)
        rise = 1.0 + bend
        act = half * rise
        self.a_ref[there] = self.inside(k, act).astype(LOW)
        grad = self.inside(k, self.g_ref[here] * (rise + act * (1.0 - bend)))
        self.g_ref[here] = grad
        self.first = self.first + jnp.sum(grad.reshape(-1, 8, 256), 0)
        self.second = self.second + jnp.sum((grad * half).reshape(-1, 8, 256), 0)

    def store(self, sum_ref):
        first = lane_fold(total_rows(self.first))
        second = lane_fold(total_rows(self.second))
        sum_ref[0:1, :] = first
        sum_ref[1:2, :] = (2.0 * second - self.shift * first) / self.gain


class NormInputGrads:
    def __init__(self, sum_ref, st_ref, par_ref, state_ref, spot, count, low_ref, odd, cells, residual, keep):
        mean, inv, gain, shift = norm_lines(st_ref, par_ref, cells)
        self.scale = 0.5 * gain * inv
        self.slope = -self.scale * inv * sum_ref[1:2, :] / cells
        self.offset = -self.scale * sum_ref[0:1, :] / cells - self.slope * mean
        self.inside = edge_masks(odd, count)
        self.pad = 0 if odd else 1
        self.state_ref, self.low_ref, self.spot, self.count = state_ref, low_ref, spot, count
        self.residual, self.keep = residual, keep
        if self.pad:
            clear_border(low_ref, count)

    def row(self, i):
        state_ref, count = self.state_ref, self.count
        grad = state_ref[0, i, :count] * self.scale + state_ref[self.spot, i, :count] * self.slope + self.offset
        grad = self.inside(i, grad)
        if self.residual:
            grad = grad + state_ref[2, i]
        if self.keep:
            state_ref[2, i] = grad
        self.low_ref[i + self.pad, self.pad : self.pad + count] = grad.astype(LOW)


def pieces(count):
    edges = [count * k // 4 for k in range(5)]
    return list(zip(edges[:-1], edges[1:]))


def mid_backward(odd, residual, cells, *refs):
    sum_ref, st_ref, par_ref, held_ref, w_ref, in_st_ref, in_par_ref, in_v_far = refs[:8]
    state_ref, pair_ref, out_sum_ref, sem = refs[8:]
    count, n = in_v_far.shape[0], in_v_far.shape[2]
    own = count + 1 if odd else count - 1
    low_ref, a_ref = pair_ref.at[0], pair_ref.at[1]
    spot, next_spot = (1, 3) if odd else (3, 1)
    copies = {}
    for k, (low, high) in enumerate(pieces(count)):
        copies[low] = pltpu.make_async_copy(
            in_v_far.at[low:high], state_ref.at[next_spot, low:high, :count], sem.at[k]
        )
        copies[low].start()
    inputs = NormInputGrads(sum_ref, st_ref, par_ref, state_ref, spot, own, low_ref, odd, cells, residual, odd)
    outputs = ActivationGrads(
        state_ref.at[0], state_ref.at[next_spot], count, in_st_ref, in_par_ref, a_ref, not odd, cells, True
    )

    def work(k, size):
        left = jnp.concatenate(four_views(low_ref, k, size, count), axis=1)
        value = jnp.dot(left, w_ref[...], preferred_element_type=WIDE)
        state_ref[0, k : k + size, :count] = value.reshape(size, count, n, 256)

    def after(k):
        if k in copies:
            copies[k].wait()
        outputs.add(k)

    staged(own, count, odd, 17, inputs.row, work, after)
    outputs.store(out_sum_ref)


def window_backward(width, arrays, cells, *refs):
    d_refs = refs[:arrays]
    w_ref, st_ref, par_ref, v_far, state_ref, a_ref, sum_ref, sem = refs[arrays:]
    count, n = v_far.shape[0], v_far.shape[2]
    copy = pltpu.make_async_copy(v_far, state_ref.at[1], sem.at[0])
    copy.start()
    outputs = ActivationGrads(
        state_ref.at[0], state_ref.at[1], count, st_ref, par_ref, a_ref, True, cells, False
    )
    done = []
    for index, spots in enumerate(runs(count)):
        left = jnp.concatenate(
            [
                jnp.concatenate([window_left(d_ref, spot, width) for d_ref in d_refs], axis=1)
                for spot in spots
            ],
            axis=0,
        )
        value = jnp.dot(left, w_ref[...], preferred_element_type=WIDE).reshape(len(spots), count, n, 256)
        for k, spot in enumerate(spots):
            state_ref[0, :, spot] = value[k]
        if index == 1:
            copy.wait()
        for spot in done:
            outputs.add(spot)
        done = spots
    for spot in done:
        outputs.add(spot)
    outputs.store(sum_ref)


def entry_backward(cells, inputs, *refs):
    sum_ref, st_ref, par_ref, state_ref = refs[:4]
    low_ref = refs[5] if inputs else refs[4]
    count = low_ref.shape[0]
    grads = NormInputGrads(sum_ref, st_ref, par_ref, state_ref, 1, count, low_ref, True, cells, True, False)
    for i in range(count):
        grads.row(i)
    if inputs:
        w_ref, low_ref, o_ref, value_ref = refs[4:]
        count, n = value_ref.shape[0], value_ref.shape[2]
        for start, size in groups(count):
            left = jnp.concatenate(four_views(low_ref, start, size, count), axis=1)
            value = jnp.dot(left, w_ref[...], preferred_element_type=WIDE)
            value_ref[start : start + size] = value.reshape(size, count, n, 128)

        def store(item, value):
            o_ref[item] = value

        to_rows(value_ref, 16, 2, store)


def block_weight_grad(odd, spot, pair_ref, *refs):
    o_ref, acc_ref = refs[-2:]
    low_ref, a_ref = pair_ref.at[0], pair_ref.at[1]
    pad = 0 if odd else 1
    count = low_ref.shape[0] - (1 if odd else 2)
    n = low_ref.shape[2]
    for index, (start, size) in enumerate(groups(count)):
        grad = low_ref[start + pad : start + pad + size, pad : pad + count].reshape(size * count * n, 256)
        right = jnp.concatenate(four_views(a_ref, start, size, count), axis=1)
        part = lax.dot_general(grad, right, (((0,), (0,)), ((), ())), preferred_element_type=WIDE)
        if index == 0:
            acc_ref[...] = part
        else:
            acc_ref[...] += part
    for dy in range(3):
        for dx in range(3):
            total = None
            for q in range(2):
                for s in range(2):
                    r, c = dy + q, dx + s
                    lane = ((r // 2) * 2 + c // 2) * 256 + ((r % 2) * 2 + c % 2) * 64
                    part = acc_ref[(2 * q + s) * 64 : (2 * q + s) * 64 + 64, lane : lane + 64]
                    total = part if total is None else total + part
            total = total.T
            start = 288 * spot + 32 * (3 * dy + dx)
            o_ref[start : start + 32, :64] = total[:32]
            o_ref[start : start + 32, 64:] = total[32:]


def window_weight_grad(width, arrays, *refs):
    x_refs = refs[:arrays]
    b_ref, place_ref, o_ref, acc_ref = refs[arrays:]
    count, n = b_ref.shape[0], b_ref.shape[2]
    for spots in runs(count):
        right = jnp.concatenate(
            [
                jnp.concatenate([window_left(x_ref, spot, width) for x_ref in x_refs], axis=1)
                for spot in spots
            ],
            axis=0,
        )
        left = jnp.concatenate([b_ref[:, spot].reshape(count * n, 256) for spot in spots], axis=0)
        part = lax.dot_general(left, right, (((0,), (0,)), ((), ())), preferred_element_type=WIDE)
        if spots[0] == 0:
            acc_ref[...] = part
        else:
            acc_ref[...] += part
    lane = lax.broadcasted_iota(jnp.int32, (64, 128), 1) // 32
    total = None
    for p in range(4):
        parts = []
        for array in range(arrays):
            held = jnp.zeros((64, 128), WIDE)
            for r in range(4):
                start = 512 * array + 128 * r
                value = rolled(acc_ref[64 * p : 64 * p + 64, start : start + 128], 32 * r)
                held = jnp.where(lane == r, value, held)
            parts.append(held)
        one = jnp.where(hot(place_ref[p : p + 1], 72 * arrays), 1.0, 0.0)
        part = exact_dot(one, jnp.concatenate(parts, axis=1), ((1,), (1,)))
        total = part if total is None else total + part
    o_ref[...] = total


def lane_ids(shape):
    return lax.broadcasted_iota(jnp.int32, shape, len(shape) - 1)


def flat_roll(value, shift):
    return rolled(value.reshape(-1, 128), shift).reshape(value.shape)


def valid_lanes(cells):
    held = jnp.where(lane_ids(cells.shape) % 4 == 3, cells, 0.0)
    return flat_roll(held, -1) + flat_roll(held, -2) + flat_roll(held, -3)


def pad_rows(x_ref, values):
    rows, n = values.shape[0], values.shape[1]
    x_ref[0:2] = jnp.zeros((2, n, 128), x_ref.dtype)
    x_ref[2 : 2 + rows] = values.astype(x_ref.dtype)
    x_ref[2 + rows :] = jnp.zeros((2, n, 128), x_ref.dtype)


def column_line(value):
    return jnp.sum(value.reshape(-1, 128), axis=0, keepdims=True)


def checks(shape):
    lane = lane_ids(shape)
    row = lax.broadcasted_iota(jnp.int32, shape, 0)
    return ((row + lane // 4) % 2 == 1) & (lane % 4 != 3)


def prepare(cells_ref, x_ref, logits_ref, sum_ref):
    cells = cells_ref[...]
    lane = lane_ids(cells.shape)
    channel = lane % 4 != 3
    valid = valid_lanes(cells)
    prob = ALPHA + (1.0 - 2.0 * ALPHA) * (cells / 256.0)
    log_in = jnp.log(prob)
    log_out = jnp.log(1.0 - prob)
    logits = jnp.where(channel, log_in - log_out, 0.0)
    jacobian = math.log(1.0 - 2.0 * ALPHA) - log_in - log_out
    logits_ref[...] = logits
    sum_ref[0:1] = column_line(valid)
    sum_ref[1:2] = column_line(valid * (HALF_LOG_TAU + LOG_LEVELS - jacobian))
    odd = checks(cells.shape)
    pad_rows(x_ref, jnp.where(odd, 1.0, logits))


def couple(line_ref, raw_ref, logits_ref, cells_ref, o_ref, bend_ref, sum_ref):
    logits = logits_ref[...]
    valid = valid_lanes(cells_ref[...])
    gain = line_ref[0:1].reshape(1, 1, 128)
    total = jnp.zeros((1, 128), WIDE)
    for q in range(2):
        raw = raw_ref[q] + line_ref[1 + q : 2 + q].reshape(1, 1, 128)
        own = logits_ref[pl.ds(q, raw.shape[0], 2)]
        cells = cells_ref[pl.ds(q, raw.shape[0], 2)]
        lane = lane_ids(raw.shape)
        odd = ((q + lane // 4) % 2 == 1) & (lane % 4 != 3)
        shift = flat_roll(raw, 4 if q == 0 else -4)
        bend = jnp.where(odd, jnp.tanh(raw), 0.0)
        scale = gain * bend
        coupled = jnp.where(odd, own * jnp.exp(scale) + shift, own)
        bend_ref[q] = bend
        total = total - column_line(valid_lanes(cells) * scale)
        o_ref[pl.ds(q, raw.shape[0], 2)] = jnp.where(lane % 4 == 3, cells, coupled)
    sum_ref[...] = total


def enter_two(coupled_ref, x_ref):
    value = coupled_ref[pl.ds(0, coupled_ref.shape[0] // 2, 2)]
    pad_rows(x_ref, jnp.where(lane_ids(value.shape) % 4 == 3, 0.0, value))


def losses(line_ref, count_ref, raw_ref, coupled_ref, scale_d_ref, shift_d_ref, grad_ref, sum_ref):
    half = coupled_ref.shape[0] // 2
    shape = (half, coupled_ref.shape[1], 128)
    channel = lane_ids(shape) % 4 != 3
    top = coupled_ref[pl.ds(0, half, 2)]
    low = coupled_ref[pl.ds(1, half, 2)]
    top_valid = valid_lanes(top)
    low_valid = valid_lanes(low)
    top = jnp.where(channel, top, 0.0)
    low = jnp.where(channel, low, 0.0)

    def rows(item):
        pair = jnp.stack([raw_ref[item], raw_ref[2 + item]], axis=1)
        return pair.reshape(shape) + line_ref[4 + item : 5 + item].reshape(1, 1, 128)

    gain = line_ref[3:4].reshape(1, 1, 128)
    unit = 1.0 / (LOG_TWO * jnp.sum(count_ref[0:1], axis=1, keepdims=True)).reshape(1, 1, 1)
    bend = jnp.tanh(rows(0))
    scale = gain * bend
    grow = jnp.exp(scale)
    latent = jnp.where(channel, low * grow + rows(1), 0.0)
    sum_ref[0:1] = column_line(top_valid * (0.5 * top * top) + low_valid * (0.5 * latent * latent - scale))
    moved = low_valid * unit * latent
    grad_scale = moved * low * grow - low_valid * unit
    raw_grad = grad_scale * gain * (1.0 - bend * bend)
    sum_ref[1:2] = column_line(grad_scale * bend)
    sum_ref[2:3] = column_line(raw_grad)
    sum_ref[3:4] = column_line(moved)
    pad_rows(scale_d_ref, raw_grad)
    pad_rows(shift_d_ref, moved)
    grad_ref[pl.ds(0, half, 2)] = top_valid * unit * top
    grad_ref[pl.ds(1, half, 2)] = moved * grow


def uncouple(mine_ref, line_ref, count_ref, entry_ref, grad_ref, logits_ref, bend_ref, cells_ref, d_ref, sum_ref):
    half = logits_ref.shape[0] // 2
    n = logits_ref.shape[1]
    own_part = pl.ds(pl.multiple_of(mine_ref[0], 8), n)
    gain = line_ref[0:1].reshape(1, 1, 128)
    unit = 1.0 / (LOG_TWO * jnp.sum(count_ref[0:1], axis=1, keepdims=True)).reshape(1, 1, 1)
    lines = [jnp.zeros((1, 128), WIDE)] * 3
    d_ref[0:2] = jnp.zeros((2, n, 128), d_ref.dtype)
    d_ref[2 * half + 2 :] = jnp.zeros((d_ref.shape[0] - 2 * half - 2, n, 128), d_ref.dtype)
    for q in range(2):
        grad = grad_ref[pl.ds(q, half, 2), own_part]
        if q == 0:
            grad = grad + jnp.stack([entry_ref[0, :, own_part], entry_ref[1, :, own_part]], axis=1).reshape(half, n, 128)
        own = logits_ref[pl.ds(q, half, 2)]
        valid = valid_lanes(cells_ref[pl.ds(q, half, 2)])
        bend = bend_ref[q]
        lane = lane_ids(grad.shape)
        odd = ((q + lane // 4) % 2 == 1) & (lane % 4 != 3)
        grad = jnp.where(odd, grad, 0.0)
        grad_scale = jnp.where(odd, grad * own * jnp.exp(gain * bend) - valid * unit, 0.0)
        raw_grad = grad_scale * gain * (1.0 - bend * bend)
        lines[0] = lines[0] + column_line(grad_scale * bend)
        lines[1] = lines[1] + column_line(raw_grad)
        lines[2] = lines[2] + column_line(grad)
        value = raw_grad + flat_roll(grad, -4 if q == 0 else 4)
        d_ref[pl.ds(2 + q, half, 2)] = value.astype(d_ref.dtype)
    for spot in range(3):
        sum_ref[spot : spot + 1] = lines[spot]


def call(kernel, outs, args, name, scratch=(), limit=16, far_in=(), far_out=(), sems=0, aliases=None, scalar_in=()):
    spaces = [
        pltpu.HBM if spot in far_in else pltpu.SMEM if spot in scalar_in else pltpu.VMEM
        for spot in range(len(args))
    ]
    out_spaces = [pltpu.HBM if spot in far_out else pltpu.VMEM for spot in range(len(outs))]
    held = [pltpu.VMEM(shape, dtype) for shape, dtype in scratch]
    args = [pltpu.with_memory_space_constraint(arg, space) if space is pltpu.HBM else arg for arg, space in zip(args, spaces)]
    if sems:
        held.append(pltpu.SemaphoreType.DMA(sems))
    return pl.pallas_call(
        kernel,
        out_shape=[space(shape, dtype) for space, (shape, dtype) in zip(out_spaces, outs)],
        in_specs=[pl.BlockSpec(memory_space=space) for space in spaces],
        out_specs=[pl.BlockSpec(memory_space=space) for space in out_spaces],
        scratch_shapes=held,
        compiler_params=pltpu.CompilerParams(vmem_limit_bytes=limit * 2**20),
        input_output_aliases=aliases or {},
        cost_estimate=pl.CostEstimate(
            flops=int(1e+09 * COSTS.get(name, 0.5)), bytes_accessed=0, transcendentals=0
        ),
        name=name,
    )(*args)


class Net:
    def __init__(self, name, blocks, n, width, group, total, pars, weights, turned_weights):
        self.name = name
        self.even = blocks
        self.odd = blocks + 1
        self.n = n
        self.width = width
        self.group = group
        self.cells = float(total)
        self.own = float(n * blocks * blocks * 4)
        self.pars = pars
        self.weights = weights
        self.turned_weights = turned_weights
        self.far = []
        self.stats = []

    def shape(self, odd, padded=False):
        count = self.odd if odd else self.even
        pad = 2 if padded and not odd else 0
        return (count + pad, count + pad, self.n, 256)

    def keep(self, stats, far):
        self.far.append(far)
        self.stats.append(merge_stats(stats, self.own, self.group))

    def forward(self, x, entry, exit_weights, items):
        held = (2,) + self.shape(True)
        state, stats, far = call(
            functools.partial(window_forward, self.width),
            [(held, WIDE), ((2, 256), WIDE), (self.shape(True), WIDE)],
            [x, entry],
            self.name + "_entry",
            far_out=(2,),
            sems=(1,),
        )
        self.keep(stats, far)
        for index in range(4):
            odd = index % 2 == 0
            state, stats, far = call(
                functools.partial(mid_forward, odd, self.cells),
                [(held, WIDE), ((2, 256), WIDE), (self.shape(not odd), WIDE)],
                [self.stats[index], self.pars[index], state, self.weights[index]],
                self.name + "_forward",
                [(self.shape(odd, True), LOW)],
                far_out=(2,),
                sems=(self.odd,),
                aliases={2: 0},
            )
            self.keep(stats, far)
        return call(
            functools.partial(exit_forward, self.cells, 2 * self.width, items),
            [((items, self.even, self.n, 128), WIDE)],
            [self.stats[4], self.pars[4], state, exit_weights],
            self.name + "_exit",
            [(self.shape(True), LOW), ((self.even, self.even, self.n, 128), WIDE)],
        )[0]

    def backward(self, grads, exit_turned, exit_place, x, entry_turned, entry_place, packets, slots):
        arrays = len(grads)
        held = (4,) + self.shape(True)
        pair_shape = (2, self.even + 2, self.even + 2, self.n, 256)
        state, act, sums = call(
            functools.partial(window_backward, self.width, arrays, self.cells),
            [(held, WIDE), (self.shape(True), LOW), ((2, 256), WIDE)],
            list(grads) + [exit_turned, self.stats[4], self.pars[4], self.far[4]],
            self.name + "_exit_back",
            far_in=(arrays + 3,),
            sems=(1,),
        )
        results_of = {}

        def exit_work(token):
            (held,) = tied([act], token)
            grad = call(
                functools.partial(window_weight_grad, self.width, arrays),
                [((72 * arrays, 64), WIDE)],
                list(grads) + [held, exit_place],
                self.name + "_exit_weights",
                [((256, 512 * arrays), WIDE)],
            )[0]
            return (grad,) + slots.get(4, lambda *held: ())(None, grad, token)

        sums, exit_grad, *done = travel(sums, self.group, exit_work)
        results_of[4] = done
        norm_grads = [None] * 5
        block_grads = []
        norm_grads[4] = sums
        for index in reversed(range(4)):
            odd = index % 2 == 1
            state, pair, sums = call(
                functools.partial(mid_backward, odd, index == 1, self.cells),
                [(held, WIDE), (pair_shape, LOW), ((2, 256), WIDE)],
                [
                    sums,
                    self.stats[index + 1],
                    self.pars[index + 1],
                    state,
                    self.turned_weights[index],
                    self.stats[index],
                    self.pars[index],
                    self.far[index],
                ],
                self.name + "_back",
                far_in=(7,),
                sems=(4,),
                aliases={3: 0},
            )
            packet = next(held for held in packets if index in held)
            spot = packet.index(index)
            fresh = index == packet[-1]

            def block_work(token):
                (held,) = tied([pair], token)
                grad = call(
                    functools.partial(block_weight_grad, odd, spot),
                    [((288 * len(packet), 128), WIDE)],
                    [held] + ([] if fresh else [block]),
                    self.name + "_weights",
                    [((256, 1024), WIDE)],
                    aliases=None if fresh else {1: 0},
                )[0]
                return (grad,) + slots.get(index, lambda *held: ())(block_grads, exit_grad, token)

            sums, block, *done = travel(sums, self.group, block_work)
            results_of[index] = done
            norm_grads[index] = sums
            if index == packet[0]:
                block_grads.append(swap_terms(block, self.group))
        args = [sums, self.stats[0], self.pars[0], state]
        outs = [(self.shape(True), LOW)]
        scratch = []
        if entry_turned is not None:
            args.append(entry_turned)
            outs.append(((2, self.even, self.n, 128), WIDE))
            scratch.append(((self.even, self.even, self.n, 128), WIDE))
        results = call(
            functools.partial(entry_backward, self.cells, entry_turned is not None),
            outs,
            args,
            self.name + "_entry_back",
            scratch,
        )

        def entry_grad(token):
            low, unused = lax.optimization_barrier((results[0], token))
            return call(
                functools.partial(window_weight_grad, self.width, 1),
                [((72, 64), WIDE)],
                [x, low, entry_place],
                self.name + "_entry_weights",
                [((256, 512), WIDE)],
            )[0]

        return entry_grad, block_grads, exit_grad, norm_grads, results_of, (results[1] if entry_turned is not None else None)


def adam_blocks(spots, fresh, places, *refs):
    count = 2 * (1 + max(place[0] for place in places))
    terms, refs = refs[:count], refs[count:]
    sources, refs = refs[:3], refs[3:]
    if not fresh:
        refs = refs[4:]
    targets, (held, out, out_low, in_sem, out_sem) = refs[:4], refs[4:]
    loads = []
    for k, spot in enumerate(spots):
        loads.append(
            [pltpu.make_async_copy(sources[j].at[spot], held.at[k, j], in_sem.at[k, j]) for j in range(3)]
        )
        for copy in loads[-1]:
            copy.start()
    stores = []
    for k, spot in enumerate(spots):
        for copy in loads[k]:
            copy.wait()
        for t in range(9):
            pair, row = 2 * places[k][0], 288 * places[k][1] + 32 * t
            packed = terms[pair][row : row + 32] + terms[pair + 1][row : row + 32]
            grad = jnp.concatenate([packed[:, :64], packed[:, 64:]], axis=0)
            news = adamw(held[k, 0, t], held[k, 1, t], held[k, 2, t], grad, RATE_CONV)
            for j in range(3):
                out[k, j, t] = news[j]
            out_low[k, t] = news[3]
        copies = [pltpu.make_async_copy(out.at[k, j], targets[j].at[spot], out_sem.at[k, j]) for j in range(3)]
        copies.append(pltpu.make_async_copy(out_low.at[k], targets[3].at[spot], out_sem.at[k, 3]))
        for copy in copies:
            copy.start()
        stores += copies
    for copy in stores:
        copy.wait()


def step_blocks(spots, pairs, places, sources, targets):
    count = len(spots)
    terms = [term for pair in pairs for term in pair]
    args = terms + list(sources) + list(targets or [])
    shape = sources[0].shape
    head = len(terms)
    return pl.pallas_call(
        functools.partial(adam_blocks, spots, targets is None, places),
        out_shape=[pltpu.HBM(shape, WIDE)] * 3 + [pltpu.HBM(shape, LOW)],
        in_specs=[pl.BlockSpec(memory_space=pltpu.VMEM)] * head
        + [pl.BlockSpec(memory_space=pltpu.HBM)] * (len(args) - head),
        out_specs=[pl.BlockSpec(memory_space=pltpu.HBM)] * 4,
        scratch_shapes=[
            pltpu.VMEM((count, 3) + shape[1:], WIDE),
            pltpu.VMEM((count, 3) + shape[1:], WIDE),
            pltpu.VMEM((count,) + shape[1:], LOW),
            pltpu.SemaphoreType.DMA((count, 3)),
            pltpu.SemaphoreType.DMA((count, 4)),
        ],
        input_output_aliases={} if targets is None else {head + 3 + j: j for j in range(4)},
        compiler_params=pltpu.CompilerParams(vmem_limit_bytes=12 * 2**20),
        cost_estimate=pl.CostEstimate(flops=int(1e+09 * (1 + count)), bytes_accessed=0, transcendentals=0),
        name="step_blocks",
    )(*args[:head], *[pltpu.with_memory_space_constraint(arg, pltpu.HBM) for arg in args[head:]])


def adamw(master, first, second, grad, rate):
    first_new = BETA_ONE * first + (1.0 - BETA_ONE) * grad
    second_new = BETA_TWO * second + (1.0 - BETA_TWO) * grad * grad
    direction = (
        first_new
        / (1.0 - BETA_ONE**STEP)
        / (jnp.sqrt(second_new / (1.0 - BETA_TWO**STEP)) + ADAM_EPS)
    )
    master_new = master - rate * (direction + DECAY * master)
    return (master_new, first_new, second_new, master_new.astype(jnp.bfloat16))


def entry_view(array):
    return array.transpose(1, 2, 3, 0, 4).reshape(54, 2, 64)


def exit_view(array):
    return array.transpose(0, 1, 3, 2).reshape(9, array.shape[3], 64)


def pack_rows(*refs):
    o_ref = refs[-1]
    o_ref[...] = jnp.zeros(o_ref.shape, WIDE)
    row = 0
    for ref in refs[:-1]:
        o_ref[row : row + ref.shape[0], : ref.shape[1]] = ref[...]
        row += ref.shape[0]


def entry_grads(one_ref, one_other, two_ref, two_other, o_ref):
    one = one_ref[...] + one_other[...]
    two = two_ref[0:72, :64] + two_other[0:72, :64]
    for t in range(9):
        o_ref[6 * t : 6 * t + 6, 0] = one[8 * t : 8 * t + 6]
        o_ref[6 * t : 6 * t + 6, 1] = two[8 * t : 8 * t + 6]


def finish_kernel(*refs):
    one_ref, one_other, two_ref, two_other, count_ref = refs[:5]
    norm_sums, place_ref = refs[5:15], refs[15]
    exit_one, exit_two, norm, head = refs[16:19], refs[19:22], refs[22:25], refs[25:28]
    far, near, sem = refs[28:46], refs[46:64], refs[64]
    loss_o, valid_o = near[0:2]
    exit_one_o, exit_two_o, norm_o, head_o = near[2:6], near[6:10], near[10:14], near[14:18]
    one = one_ref[...] + one_other[...]
    two = two_ref[...] + two_other[...]

    def store(outs, index, values):
        for o_ref, value in zip(outs, values):
            o_ref[index] = value

    for t in range(9):
        grad = one[8 * t : 8 * t + 6, :64]
        store(exit_one_o, t, adamw(exit_one[0][t], exit_one[1][t], exit_one[2][t], grad, RATE_CONV))
        grad = two[72 + 16 * t : 84 + 16 * t, :64]
        store(exit_two_o, t, adamw(exit_two[0][t], exit_two[1][t], exit_two[2][t], grad, RATE_CONV))
    for k in range(10):
        spot = (k // 5, k % 5)
        sums = norm_sums[k][...]
        grad = jnp.concatenate([sums[1:2, :64], sums[0:1, :64]], axis=0) * 0.5
        store(norm_o, spot, adamw(norm[0][spot], norm[1][spot], norm[2][spot], grad, RATE_SMALL))
    valid = jnp.sum(count_ref[0:1], axis=1, keepdims=True)
    constant = jnp.sum(count_ref[1:2], axis=1, keepdims=True)
    loss = jnp.sum(two[216:217], axis=1, keepdims=True) + jnp.sum(one[75:76], axis=1, keepdims=True)
    loss_o[...] = (loss + constant) / LOG_TWO
    valid_o[...] = valid

    def folded(line, spot):
        return exact_dot(line, jnp.where(hot(place_ref[spot : spot + 1], head[0].shape[1]), 1.0, 0.0), ((1,), (1,)))

    lane = lax.broadcasted_iota(jnp.int32, (1, 128), 1)
    raw, shift = one[73:74], one[74:75]
    grad = folded(one[72:73], 0) + folded(two[217:218], 3) + folded(two[218:219], 4) + folded(two[219:220], 5)
    grad = grad + folded(jnp.where((lane // 4) % 2 == 1, raw, 0.0), 1) + folded(jnp.where((lane // 4) % 2 == 0, raw, 0.0), 2)
    grad = grad + folded(jnp.where((lane // 4) % 2 == 0, shift, 0.0), 1) + folded(jnp.where((lane // 4) % 2 == 1, shift, 0.0), 2)
    for o_ref, value in zip(head_o, adamw(head[0][...], head[1][...], head[2][...], grad, RATE_SMALL)):
        o_ref[...] = value
    copies = [pltpu.make_async_copy(near[k], far[k], sem.at[k]) for k in range(18)]
    for copy in copies:
        copy.start()
    for copy in copies:
        copy.wait()


def finish(packs, sums, place, exit_one, exit_two, norm, head):
    outs = [((1, 1), WIDE)] * 2
    for first in (exit_one[0], exit_two[0], norm[0], head[0]):
        outs += [(first.shape, WIDE)] * 3 + [(first.shape, LOW)]
    return call(
        finish_kernel,
        outs,
        packs + sums + [place] + exit_one + exit_two + norm + head,
        "finish",
        outs,
        far_out=tuple(range(18)),
        sems=(18,),
    )


def body(
    pixels,
    valid,
    entry_conv,
    entry_first,
    entry_second,
    block_conv,
    block_first,
    block_second,
    exit_one,
    exit_one_first,
    exit_one_second,
    exit_two,
    exit_two_first,
    exit_two_second,
    norm_params,
    norm_first,
    norm_second,
    head_params,
    head_first,
    head_second,
):
    batch = pixels.shape[0] * lax.axis_size("batch")
    height = pixels.shape[1] * lax.axis_size("rows")
    group = group_bits(batch)
    small = group[:-1]
    last = group[-1]
    own = batch >> len(group)
    wide = 2 * own
    cells = jnp.concatenate([pixels, valid[..., None].astype(WIDE)], axis=3)
    cells = cells.reshape(pixels.shape[0], pixels.shape[1], 128).transpose(1, 0, 2)

    place = placements()
    small_places = [
        jnp.asarray(place[key])
        for key in (
            "entry_one",
            "entry_two",
            "entry_two_turned",
            "exit_one",
            "exit_one_turned",
            "exit_two",
            "exit_two_turned",
        )
    ]
    fold = [
        jnp.asarray(place[key + "_fold"])
        for key in ("entry_one", "entry_two", "exit_one_turned", "exit_two_turned")
    ]
    small_built = call(
        build_small,
        [
            ((512, 256), LOW),
            ((512, 256), LOW),
            ((1024, 128), LOW),
            ((1024, 128), LOW),
            ((512, 256), LOW),
            ((1024, 128), LOW),
            ((1024, 256), LOW),
            ((8, 128), WIDE),
        ]
        + [((2, 256), WIDE)] * 10,
        [
            entry_view(entry_conv),
            exit_view(exit_one),
            exit_view(exit_two),
            norm_params,
            head_params[None],
        ]
        + small_places
        + [jnp.asarray(place["head"])],
        "build_small",
        [((72, 64), WIDE), ((144, 64), WIDE)],
    )
    cells, small_built = distribute(cells, group, small_built)
    (
        entry_one_w,
        entry_two_w,
        entry_turned_w,
        exit_one_w,
        exit_one_turned_w,
        exit_two_w,
        exit_two_turned_w,
        head_lines,
        *par_lines,
    ) = small_built
    blocks = call(build_blocks, [((1024, 256), LOW)] * 16, [block_conv.reshape(8, 9, 64, 64)], "build_blocks")
    weights = [[blocks[4 * j + k] for k in range(4)] for j in range(2)]
    turned_w = [[blocks[8 + 4 * j + k] for k in range(4)] for j in range(2)]
    pars = [[par_lines[5 * j + k] for k in range(5)] for j in range(2)]

    one = Net("one", height // 2, own, 4, group, batch * height * height, pars[0], weights[0], turned_w[0])
    two = Net("two", height // 4, wide, 8, small, batch * (height // 2) ** 2, pars[1], weights[1], turned_w[1])

    rows = height
    x_one, logits, first_sums = call(
        prepare,
        [((rows + 4, own, 128), WIDE), ((rows, own, 128), WIDE), ((2, 128), WIDE)],
        [cells],
        "prepare",
    )
    first_sums = group_sum(first_sums, group)
    mine, x_one = lax.optimization_barrier((side(last) * own, x_one))
    raw_one = one.forward(x_one, entry_one_w, exit_one_w, 2)
    coupled, bend_one, couple_sums = call(
        couple,
        [((rows, own, 128), WIDE), ((2, rows // 2, own, 128), WIDE), ((1, 128), WIDE)],
        [head_lines, raw_one, logits, cells],
        "couple",
    )
    coupled = joined(coupled, swap(coupled, last), mine, 1)
    x_two = call(enter_two, [((rows // 2 + 4, wide, 128), WIDE)], [coupled], "enter_two")[0]
    raw_two = two.forward(x_two, entry_two_w, exit_two_w, 4)
    scale_d, shift_d, grad_coupled, loss_sums = call(
        losses,
        [
            ((rows // 2 + 4, wide, 128), WIDE),
            ((rows // 2 + 4, wide, 128), WIDE),
            ((rows, wide, 128), WIDE),
            ((4, 128), WIDE),
        ],
        [
            head_lines,
            first_sums,
            raw_two,
            coupled,
        ],
        "losses",
    )
    entry_two, blocks_two, exit_two_part, norms_two, unused, grad_first = two.backward(
        [scale_d, shift_d], exit_two_turned_w, fold[3], x_two, entry_turned_w, fold[1], [[0, 1, 2, 3]], {}
    )
    def send_two(held, exit_grad, token):
        rows = call(pack_rows, [((224, 128), WIDE)], [entry_two(token), exit_two_part, loss_sums], "pack_two")[0]
        return tuple(swap_terms(rows, small))

    def send_one(held, exit_grad, token):
        rows = call(pack_rows, [((80, 128), WIDE)], [exit_grad, one_sums, couple_sums], "pack_one")[0]
        return tuple(swap_terms(rows, group))

    sources = [part.reshape(8, 9, 64, 64) for part in (block_conv, block_first, block_second)]
    steps = {}

    def step(key, spots, terms, firsts):
        def run(held, exit_grad, token):
            steps[key] = tuple(
                step_blocks(spots, [tied(terms, token)], [(0, k) for k in firsts], sources, steps.get(key - 1))
            )
            return steps[key]

        return run

    one_d, one_sums = call(
        uncouple,
        [((rows + 4, own, 128), WIDE), ((3, 128), WIDE)],
        [jnp.reshape(mine, (1,)), head_lines, first_sums, grad_first, grad_coupled, logits, bend_one, cells],
        "uncouple",
        scalar_in=(0,),
    )
    slots = {
        4: send_two,
        3: send_one,
        2: step(0, (4, 5), blocks_two[0], (0, 1)),
        0: step(1, (6, 7), blocks_two[0], (2, 3)),
    }
    entry_one, blocks_one, exit_one_part, norms_one, done, unused = one.backward(
        [one_d], exit_one_turned_w, fold[2], x_one, None, fold[0], [[1, 2, 3], [0]], slots
    )
    entry_one, *blocks_done = lax.optimization_barrier((entry_one(first_sums), *blocks_one[0]))
    entry_one = swap_terms(entry_one, group)
    pack_two, pack_one = list(done[4]), list(done[3])
    stepped = step_blocks(
        (1, 2, 3), [blocks_done], [(0, 0), (0, 1), (0, 2)], sources, done[0]
    )
    finished = finish(
        pack_one + pack_two,
        [first_sums] + norms_one + norms_two,
        jnp.asarray(place["head"]),
        [exit_view(part) for part in (exit_one, exit_one_first, exit_one_second)],
        [exit_view(part) for part in (exit_two, exit_two_first, exit_two_second)],
        [norm_params, norm_first, norm_second],
        [part[None] for part in (head_params, head_first, head_second)],
    )
    stepped = step_blocks((0,), [blocks_one[1]], [(0, 0)], sources, stepped)
    entry_grad = call(
        entry_grads, [((54, 2, 64), WIDE)], entry_one + pack_two, "entry_grads"
    )[0]
    entry_steps = adamw(
        entry_view(entry_conv), entry_view(entry_first), entry_view(entry_second), entry_grad, RATE_CONV
    )
    entry_out = tuple(
        part.reshape(3, 3, 6, 2, 64).transpose(3, 0, 1, 2, 4) for part in entry_steps
    )
    one_out = tuple(part.reshape(3, 3, 6, 64).transpose(0, 1, 3, 2) for part in finished[2:6])
    two_out = tuple(part.reshape(3, 3, 12, 64).transpose(0, 1, 3, 2) for part in finished[6:10])
    return (
        (finished[0].reshape(()), finished[1].reshape(()))
        + entry_out
        + tuple(part.reshape(block_conv.shape) for part in stepped)
        + one_out
        + two_out
        + tuple(finished[10:14])
        + tuple(part.reshape(head_params.shape) for part in finished[14:18])
    )


def solution(mesh):
    placed = (P("batch", "rows", None, None), P("batch", "rows", None)) + (P(),) * 18
    return jax.shard_map(body, mesh=mesh, in_specs=placed, out_specs=(P(),) * 26, check_vma=False)
```

```python
import functools
import math

import jax
import jax.numpy as jnp
import numpy as np
from jax import lax
from jax.experimental import pallas as pl
from jax.experimental.pallas import tpu as pltpu
from jax.sharding import PartitionSpec as P

STEP = 10
ALPHA = 0.05
NORM_EPS = 1e-05
BETA_ONE = 0.9
BETA_TWO = 0.999
ADAM_EPS = 1e-08
DECAY = 0.01
RATE_CONV = 1.0
RATE_SMALL = 10.0
LOG_TWO = math.log(2.0)
HALF_LOG_TAU = 0.5 * math.log(2.0 * math.pi)
LOG_LEVELS = math.log(256.0)
IMAGES = 16
BITS = (("batch", 1), ("batch", 2), ("rows", 1), ("rows", 2), ("batch", 4), ("batch", 8), ("batch", 16), ("batch", 32))
LOW = jnp.bfloat16
WIDE = jnp.float32
COSTS = {
    "one_entry": 4.0,
    "one_forward": 3.7,
    "one_exit": 2.5,
    "one_exit_back": 5.7,
    "one_exit_weights": 2.6,
    "one_back": 5.4,
    "one_weights": 3.0,
    "one_entry_weights": 2.7,
    "two_entry": 2.7,
    "two_forward": 2.5,
    "two_exit": 1.4,
    "two_exit_back": 4.1,
    "two_exit_weights": 3.7,
    "two_back": 3.0,
    "two_weights": 1.9,
    "two_entry_back": 1.5,
    "two_entry_weights": 1.9,
    "build_small": 1.9,
    "build_blocks": 1.0,
    "finish": 1.2,
}


def axis_bits():
    return [bit for bit in BITS if bit[1] < lax.axis_size(bit[0])]


def group_bits(batch):
    bits = axis_bits()
    count = max(batch // IMAGES, 1).bit_length() - 1
    return bits[: min(count, len(bits))]


def swap(value, bit):
    axis, mask = bit
    return lax.ppermute(value, axis, [(i, i ^ mask) for i in range(lax.axis_size(axis))])


def side(bit):
    return (lax.axis_index(bit[0]) // bit[1]) % 2


def group_sum(value, bits):
    for bit in bits:
        value = jax.tree.map(lambda own: own + swap(own, bit), value)
    return value


def travel(sums, bits, work):
    held = sums
    if len(bits) > 1:
        held = sums + swap(sums, bits[0])
        bits = bits[1:]
    results = work(held)
    return lax.optimization_barrier((group_sum(held, bits),) + tuple(results))


def tied(values, token):
    return lax.optimization_barrier((tuple(values), token))[0]


def swap_terms(value, bits):
    value = group_sum(value, bits[:-1])
    return [value, swap(value, bits[-1])]


def joined(own, other, mine, dim):
    first = jnp.where(mine == 0, own, other)
    second = jnp.where(mine == 0, other, own)
    return jnp.concatenate([first, second], axis=dim)


def chosen_part(label, parts):
    found = []
    for k in range(len(parts)):
        value = parts[k]
        for own in range(1, len(parts)):
            value = jnp.where(label == own, parts[k ^ own], value)
        found.append(value)
    return found


def split_parts(label_ref, cells_ref, *o_refs):
    count = cells_ref.shape[1] // len(o_refs)
    parts = [cells_ref[:, count * k : count * k + count] for k in range(len(o_refs))]
    for o_ref, value in zip(o_refs, chosen_part(label_ref[0], parts)):
        o_ref[...] = value


def lay_parts(dim, label_ref, *refs):
    o_ref = refs[-1]
    parts = [ref[...] for ref in refs[:-1]]
    size = parts[0].shape[dim]
    for k, value in enumerate(chosen_part(label_ref[0], parts)):
        if dim == 0:
            o_ref[size * k : size * k + size] = value
        else:
            o_ref[:, size * k : size * k + size] = value


def distribute(cells, group, beside):
    bands = lax.axis_size("rows")
    rows, images = cells.shape[:2]
    row = lax.axis_index("rows")
    mask = sum(bit[1] for bit in group if bit[0] == "rows")
    share = images // (mask + 1)
    pieces = call(
        split_parts,
        [((rows, share, 128), WIDE)] * (mask + 1),
        [jnp.reshape(row & mask, (1,)), cells],
        "split_parts",
        scalar_in=(0,),
    )
    came = [pieces[0]] + [swap(pieces[k & mask], ("rows", k)) for k in range(1, bands)]
    came, beside = lax.optimization_barrier((came, beside))
    cells = call(
        functools.partial(lay_parts, 0),
        [((bands * rows, share, 128), WIDE)],
        [jnp.reshape(row, (1,))] + came,
        "lay_bands",
        scalar_in=(0,),
    )[0]
    others = [bit[1] for bit in axis_bits() if bit[0] == "batch" and bit not in group]
    if not others:
        return cells, beside
    low = others[0]
    came = [cells] + [swap(cells, ("batch", k * low)) for k in range(1, 2 ** len(others))]
    cells = call(
        functools.partial(lay_parts, 1),
        [((bands * rows, share * len(came), 128), WIDE)],
        [jnp.reshape(lax.axis_index("batch") // low, (1,))] + came,
        "lay_images",
        scalar_in=(0,),
    )[0]
    return cells, beside


def merge_stats(both, count, group):
    for bit in group:
        both = call(
            functools.partial(merge_pair, 0.5 * count), [((2, 256), WIDE)], [both, swap(both, bit)], "merge"
        )[0]
        count = 2 * count
    return both


def merge_pair(weight, own_ref, other_ref, o_ref):
    gap = own_ref[0:1] - other_ref[0:1]
    o_ref[0:1] = 0.5 * (own_ref[0:1] + other_ref[0:1])
    o_ref[1:2] = own_ref[1:2] + other_ref[1:2] + gap * gap * weight


def blockify(kernel):
    rows = np.stack([np.pad(kernel, ((q, 1 - q), (0, 0), (0, 0), (0, 0))) for q in range(2)], axis=3)
    return np.stack([np.pad(rows, ((0, 0), (s, 1 - s), (0, 0), (0, 0), (0, 0))) for s in range(2)], axis=4)


def turned(kernel):
    return np.flip(kernel, (0, 1)).transpose(0, 1, 3, 2)


def views(blocked):
    rest = blocked.shape[2:]
    split = blocked.reshape((2, 2, 2, 2) + rest)
    return split.transpose((0, 2, 1, 3) + tuple(range(4, 4 + len(rest)))).reshape((16,) + rest)


def mates(blocked):
    return np.flip(blocked.reshape(4, 2, 2, *blocked.shape[2:]), 2).reshape(blocked.shape)


def spread(values, axis):
    shape = values.shape
    cut = values.reshape(shape[:axis] + (2, 3) + shape[axis + 1 :])
    pad = [(0, 0)] * cut.ndim
    pad[axis + 1] = (0, 1)
    return np.pad(cut, pad).reshape(shape[:axis] + (8,) + shape[axis + 1 :])


def window_rows(weights):
    flat = weights.reshape(4, -1, 4)
    return np.pad(flat, ((0, 0), (0, 128 - flat.shape[1]), (0, 0))).reshape(512, 4)


def checker(odd):
    return ((np.arange(4)[:, None] + np.arange(4)[None, :]) % 2 == odd).reshape(4, 4, 1, 1)


def chosen(blocked, odd):
    both = np.where(checker(odd), blocked[:, :, :3], mates(blocked)[:, :, 3:])
    return window_rows(np.pad(both, ((0, 0), (0, 0), (0, 1), (0, 0))))


def numbered(channels, last):
    pad = 8 if channels == 6 else 16
    number = (pad * np.arange(9)[:, None] + np.arange(1, channels + 1)).reshape(3, 3, 1, channels)
    return number if last else number.transpose(0, 1, 3, 2)


@functools.cache
def placements():
    odd = (np.arange(2)[:, None] + np.arange(2)[None, :]) % 2 == 1
    found = {}
    blocked = blockify(numbered(6, False)).reshape(4, 4, 6, 4)
    found["entry_one"] = chosen(blocked, 0).T
    found["entry_two"] = window_rows(spread(blocked, 2)).T
    blocked = views(blockify(turned(numbered(6, False))))
    lanes = spread(blocked.reshape(16, 2, 2, 6), 3).reshape(16, 2, 16)
    lanes = np.pad(lanes, ((0, 0), (0, 0), (0, 48))).reshape(16, 128)
    found["entry_two_turned"] = lanes
    blocked = views(blockify(numbered(6, True))).reshape(16, 2, 2, 6)
    both = np.where(odd[None, :, :, None], blocked[..., :3], np.flip(blocked, 2)[..., 3:])
    lanes = np.pad(both, ((0, 0), (0, 0), (0, 0), (0, 1))).reshape(16, 2, 8)
    lanes = np.pad(lanes, ((0, 0), (0, 0), (0, 56))).reshape(16, 128)
    found["exit_one"] = lanes
    blocked = blockify(turned(numbered(6, True))).reshape(4, 4, 6, 4)
    found["exit_one_turned"] = chosen(blocked, 1).T
    blocked = views(blockify(numbered(12, True))).reshape(16, 2, 2, 2, 6)
    lanes = spread(blocked, 4).transpose(0, 1, 3, 2, 4).reshape(16, 4, 16)
    lanes = np.pad(lanes, ((0, 0), (0, 0), (0, 16))).reshape(16, 128)
    found["exit_two"] = lanes
    blocked = blockify(turned(numbered(12, True))).reshape(4, 4, 12, 4)
    pair = [window_rows(spread(blocked[:, :, 6 * s : 6 * s + 6], 2)) for s in range(2)]
    found["exit_two_turned"] = np.concatenate(pair).T
    for key in ("entry_one", "entry_two", "exit_one_turned", "exit_two_turned"):
        found[key + "_fold"] = found[key].reshape(4, -1, 128)[:, :, :32].reshape(4, -1)
    number = np.arange(1, 28)

    def line(values, lanes):
        cut = np.pad(values.reshape(-1, 3), ((0, 0), (0, 1))).reshape(-1)
        return np.tile(cut, 128 // lanes)

    pick = (np.arange(128) // 4) % 2
    scale, shift = line(number[9:12], 4), line(number[12:15], 4)
    lines = [
        line(number[0:3], 4),
        np.where(pick == 1, scale, shift),
        np.where(pick == 0, scale, shift),
        line(number[3:9], 8),
        line(number[15:21], 8),
        line(number[21:27], 8),
        np.zeros(128, int),
        np.zeros(128, int),
    ]
    found["head"] = np.stack(lines)
    return {key: value.astype(np.int32) for key, value in found.items()}


def exact_dot(left, right, dims):
    return lax.dot_general(
        left, right, (dims, ((), ())), precision=lax.Precision.HIGHEST, preferred_element_type=WIDE
    )


def hot(line, count):
    return lax.broadcasted_iota(jnp.int32, (count, line.shape[1]), 0) + 1 == line


def place_rows(place_ref, kernel, o_ref):
    for p in range(4):
        one = jnp.where(hot(place_ref[p : p + 1], kernel.shape[0]), 1.0, 0.0).astype(LOW)
        part = lax.dot_general(one, kernel, (((0,), (0,)), ((), ())), preferred_element_type=WIDE)
        o_ref[:, 64 * p : 64 * p + 64] = part.astype(LOW)


def place_lanes(place_ref, kernel, o_ref):
    for p in range(16):
        one = jnp.where(hot(place_ref[p : p + 1], kernel.shape[0]), 1.0, 0.0).astype(LOW)
        part = lax.dot_general(kernel, one, (((0,), (0,)), ((), ())), preferred_element_type=WIDE)
        o_ref[64 * p : 64 * p + 64] = part.astype(LOW)


def padded_kernel(rows, scratch, width):
    scratch[...] = jnp.zeros(scratch.shape, WIDE)
    for t in range(9):
        value = rows(t)
        scratch[width * t : width * t + value.shape[0]] = value
    return scratch[...].astype(LOW)


def build_small(entry_ref, one_ref, two_ref, norm_ref, head_ref, *refs):
    places = refs[:8]
    entry_one_o, entry_two_o, entry_turned_o, one_o, one_turned_o, two_o, two_turned_o, line_o = refs[8:16]
    par_refs, (small, large) = refs[16:26], refs[26:]
    entry_one = padded_kernel(lambda t: entry_ref[6 * t : 6 * t + 6, 0], small, 8)
    entry_two = padded_kernel(lambda t: entry_ref[6 * t : 6 * t + 6, 1], small, 8)
    exit_one = padded_kernel(lambda t: one_ref[t], small, 8)
    exit_two = padded_kernel(lambda t: two_ref[t], large, 16)
    place_rows(places[0], entry_one, entry_one_o)
    place_rows(places[1], entry_two, entry_two_o)
    place_lanes(places[2], entry_two, entry_turned_o)
    place_lanes(places[3], exit_one, one_o)
    place_rows(places[4], exit_one, one_turned_o)
    place_lanes(places[5], exit_two, two_o)
    place_rows(places[6], exit_two, two_turned_o)
    for norm, par_o in enumerate(par_refs):
        for spot in range(4):
            par_o[:, 64 * spot : 64 * spot + 64] = norm_ref[norm // 5, norm % 5]
    for spot in range(8):
        one = jnp.where(hot(places[7][spot : spot + 1], head_ref.shape[1]), 1.0, 0.0)
        line_o[spot : spot + 1] = exact_dot(head_ref[...], one, ((1,), (0,)))


def build_blocks(kernel_ref, *o_refs):
    count = kernel_ref.shape[0]
    for k, o_ref in enumerate(o_refs):
        if k < count:
            tap = [kernel_ref[k, t].astype(LOW) for t in range(9)]
        else:
            tap = [kernel_ref[k - count, 8 - t].T.astype(LOW) for t in range(9)]
        zero = jnp.zeros((64, 64), LOW)
        for r in range(4):
            for c in range(4):
                parts = [
                    tap[3 * (r - q) + c - s] if 0 <= r - q < 3 and 0 <= c - s < 3 else zero
                    for q in range(2)
                    for s in range(2)
                ]
                row = (((r // 2) * 2 + c // 2) * 4 + (r % 2) * 2 + c % 2) * 64
                o_ref[row : row + 64] = jnp.concatenate(parts, axis=1)


def groups(count):
    head = [(0, 1)] if count % 8 else []
    return head + [(start, 8) for start in range(count % 8, count, 8)]


def runs(count):
    return [list(range(start, min(start + 4, count))) for start in range(0, count, 4)]


def lane_fold(value):
    value = value + pltpu.roll(value, 128, 1)
    return value + pltpu.roll(value, 64, 1)


def total_rows(value):
    return jnp.sum(value, axis=0, keepdims=True)


def edge_masks(odd, count, by_row=True):
    if not odd:
        return lambda k, value: value
    lane = lax.broadcasted_iota(jnp.int32, (count, 1, 256), 2)
    spot = lax.broadcasted_iota(jnp.int32, (count, 1, 256), 0)
    low_column = (lane // 64) % 2 == 0
    low_row = lane < 128
    along, across = (low_column, low_row) if by_row else (low_row, low_column)
    line = jnp.where((spot == 0) & along | (spot == count - 1) & ~along, 0.0, 1.0)
    first = jnp.where(across, 0.0, line)
    last = jnp.where(across, line, 0.0)

    def apply(k, value):
        if k == 0 or k == count - 1:
            return value * (first if k == 0 else last)
        return jnp.concatenate([value[:1] * line[:1], value[1:-1], value[-1:] * line[-1:]], axis=0)

    return apply


def norm_lines(st_ref, par_ref, cells):
    mean = st_ref[0:1, :]
    inv = lax.rsqrt(st_ref[1:2, :] / cells + NORM_EPS)
    return mean, inv, par_ref[0:1, :], par_ref[1:2, :]


def clear_border(ref, count):
    ref[0] = jnp.zeros(ref.shape[1:], ref.dtype)
    ref[count + 1] = jnp.zeros(ref.shape[1:], ref.dtype)
    ref[:, 0] = jnp.zeros((ref.shape[0],) + ref.shape[2:], ref.dtype)
    ref[:, count + 1] = jnp.zeros((ref.shape[0],) + ref.shape[2:], ref.dtype)


class Activation:
    def __init__(self, v_ref, count, st_ref, par_ref, a_ref, odd, cells):
        mean, inv, gain, shift = norm_lines(st_ref, par_ref, cells)
        self.scale = 0.5 * gain * inv
        self.offset = 0.5 * shift - mean * self.scale
        self.inside = edge_masks(odd, count)
        self.pad = 0 if odd else 1
        self.v_ref, self.a_ref, self.count = v_ref, a_ref, count
        if self.pad:
            clear_border(a_ref, count)

    def row(self, i):
        half = self.v_ref[i, : self.count] * self.scale + self.offset
        act = self.inside(i, half * (1.0 + jnp.tanh(half)))
        self.a_ref[i + self.pad, self.pad : self.pad + self.count] = act.astype(LOW)


def staged(own, count, odd, size, before, work, after):
    done = 0
    last = range(0)
    for start in range(0, count, size):
        rows = range(start, min(start + size, count))
        ready = min(own, rows[-1] + 3 if odd else rows[-1] + 2)
        for i in range(done, ready):
            before(i)
        done = ready
        work(rows[0], len(rows))
        for k in last:
            after(k)
        last = rows
    for i in range(done, own):
        before(i)
    for k in last:
        after(k)


def four_views(ref, start, size, count):
    n = ref.shape[2]
    return [
        ref[start + vi : start + vi + size, vj : vj + count].reshape(size * count * n, 256)
        for vi in range(2)
        for vj in range(2)
    ]


class Spread:
    def __init__(self, o_ref, count, odd, by_row):
        self.o_ref, self.count, self.odd, self.by_row = o_ref, count, odd, by_row
        self.inside = edge_masks(odd, count, by_row)
        self.near = None
        self.first = self.second = jnp.zeros((8, 256), WIDE)

    def add(self, k):
        count, n = self.count, self.o_ref.shape[2]
        value = self.o_ref[k, :count] if self.by_row else self.o_ref[:count, k]
        if self.near is None:
            line = self.o_ref[1, 1 : count - 1] if self.by_row else self.o_ref[1 : count - 1, 1]
            line = jnp.sum(line.reshape(-1, 256), 0, keepdims=True)
            self.near = lane_fold(line) / (4 * n * (count - 2))
        rows = self.inside(k, value - self.near).reshape(-1, 8, 256)
        self.first = self.first + jnp.sum(rows, 0)
        self.second = self.second + jnp.sum(rows * rows, 0)

    def store(self, st_ref):
        side_cells = self.count - 1 if self.odd else self.count
        cells = self.o_ref.shape[2] * side_cells**2 * 4
        first = lane_fold(total_rows(self.first)) / cells
        second = lane_fold(total_rows(self.second))
        st_ref[0:1, :] = self.near + first
        st_ref[1:2, :] = second - first * first * cells


def mid_forward(odd, cells, st_ref, par_ref, held_ref, w_ref, state_ref, out_st_ref, far_ref, a_ref, sem):
    count = far_ref.shape[0]
    n = far_ref.shape[2]
    own = count + 1 if odd else count - 1
    v_ref, o_ref = (state_ref.at[0], state_ref.at[1]) if odd else (state_ref.at[1], state_ref.at[0])
    activation = Activation(v_ref, own, st_ref, par_ref, a_ref, odd, cells)
    spread = Spread(o_ref, count, not odd, True)
    copies = []

    def work(k, size):
        left = jnp.concatenate(four_views(a_ref, k, size, count), axis=1)
        value = jnp.dot(left, w_ref[...], preferred_element_type=WIDE).reshape(size, count, n, 256)
        o_ref[k : k + size, :count] = value if odd else value + o_ref[k : k + size, :count]
        copies.append(
            pltpu.make_async_copy(o_ref.at[k : k + size, :count], far_ref.at[k : k + size], sem.at[k])
        )
        copies[-1].start()

    def after(k):
        if k > 0 or count == 1:
            spread.add(k)
        if k == 1:
            spread.add(0)

    staged(own, count, odd, 1, activation.row, work, after)
    spread.store(out_st_ref)
    for copy in copies:
        copy.wait()


def rolled(value, shift):
    shift = shift % 128
    return value if shift == 0 else pltpu.roll(value, shift, 1)


def window_left(x_ref, spot, width):
    count = x_ref.shape[0] // 2 - 1
    n = x_ref.shape[1]
    columns = 128 // width
    first = 2 * spot - 2
    value = rolled(x_ref[...].reshape(-1, 128), -width * first).reshape(count + 1, 2, n, 128)
    if first < 0 or first + 4 > columns:
        column = lax.broadcasted_iota(jnp.int32, (count + 1, 2, n, 128), 3) // width + first
        value = jnp.where((column >= 0) & (column < columns), value, jnp.zeros_like(value))
    return jnp.concatenate(
        [value[r // 2 : r // 2 + count, r % 2].reshape(count * n, 128) for r in range(4)], axis=1
    ).astype(LOW)


def window_forward(width, x_ref, w_ref, state_ref, st_ref, far_ref, sem):
    count, n = far_ref.shape[0], far_ref.shape[2]
    o_ref = state_ref.at[0]
    spread = Spread(o_ref, count, True, False)
    done = []
    for spots in runs(count):
        left = jnp.concatenate([window_left(x_ref, spot, width) for spot in spots], axis=0)
        value = jnp.dot(left, w_ref[...], preferred_element_type=WIDE).reshape(len(spots), count, n, 256)
        for k, spot in enumerate(spots):
            o_ref[:, spot] = value[k]
        for spot in done:
            spread.add(spot)
        done = spots
    copy = pltpu.make_async_copy(o_ref, far_ref, sem.at[0])
    copy.start()
    for spot in done:
        spread.add(spot)
    spread.store(st_ref)
    copy.wait()


def to_rows(value_ref, step, items, store):
    count, n = value_ref.shape[0], value_ref.shape[2]
    room = 128 // items
    per = count // items
    sums = []
    for part in range(items):
        total = None
        for spot in range(part * per, part * per + per):
            moved = rolled(value_ref[:, spot].reshape(-1, 128), step * spot)
            total = moved if total is None else total + moved
        sums.append(total)
    lane = lax.broadcasted_iota(jnp.int32, (count * n, 128), 1) // room
    for item in range(items):
        value = sums[0]
        for part in range(1, items):
            value = jnp.where(lane == (item + part) % items, sums[part], value)
        store(item, rolled(value, -room * item).reshape(count, n, 128))


def exit_forward(cells, step, items, st_ref, par_ref, state_ref, w_ref, o_ref, a_ref, value_ref):
    count = value_ref.shape[0]
    n = value_ref.shape[2]
    activation = Activation(state_ref.at[0], count + 1, st_ref, par_ref, a_ref, True, cells)

    def work(k, size):
        left = jnp.concatenate(four_views(a_ref, k, size, count), axis=1)
        value = jnp.dot(left, w_ref[...], preferred_element_type=WIDE)
        value_ref[k : k + size] = value.reshape(size, count, n, 128)

    staged(count + 1, count, True, 1, activation.row, work, lambda k: None)

    def store(item, value):
        o_ref[item] = value

    to_rows(value_ref, step, items, store)


class ActivationGrads:
    def __init__(self, g_ref, v_ref, count, st_ref, par_ref, a_ref, odd, cells, by_row):
        mean, inv, self.gain, self.shift = norm_lines(st_ref, par_ref, cells)
        self.scale = 0.5 * self.gain * inv
        self.offset = 0.5 * self.shift - mean * self.scale
        self.inside = edge_masks(odd, count, by_row)
        self.pad = 0 if odd else 1
        self.g_ref, self.v_ref, self.a_ref = g_ref, v_ref, a_ref
        self.count, self.by_row = count, by_row
        self.first = self.second = jnp.zeros((8, 256), WIDE)
        if self.pad:
            clear_border(a_ref, count)

    def add(self, k):
        here = (k, slice(0, self.count)) if self.by_row else (slice(0, self.count), k)
        low, high = self.pad, self.pad + self.count
        there = (k + self.pad, slice(low, high)) if self.by_row else (slice(low, high), k + self.pad)
        half = self.v_ref[here] * self.scale + self.offset
        bend = jnp.tanh(half)
        rise = 1.0 + bend
        act = half * rise
        self.a_ref[there] = self.inside(k, act).astype(LOW)
        grad = self.inside(k, self.g_ref[here] * (rise + act * (1.0 - bend)))
        self.g_ref[here] = grad
        self.first = self.first + jnp.sum(grad.reshape(-1, 8, 256), 0)
        self.second = self.second + jnp.sum((grad * half).reshape(-1, 8, 256), 0)

    def store(self, sum_ref):
        first = lane_fold(total_rows(self.first))
        second = lane_fold(total_rows(self.second))
        sum_ref[0:1, :] = first
        sum_ref[1:2, :] = (2.0 * second - self.shift * first) / self.gain


class NormInputGrads:
    def __init__(self, sum_ref, st_ref, par_ref, state_ref, spot, count, low_ref, odd, cells, residual, keep):
        mean, inv, gain, shift = norm_lines(st_ref, par_ref, cells)
        self.scale = 0.5 * gain * inv
        self.slope = -self.scale * inv * sum_ref[1:2, :] / cells
        self.offset = -self.scale * sum_ref[0:1, :] / cells - self.slope * mean
        self.inside = edge_masks(odd, count)
        self.pad = 0 if odd else 1
        self.state_ref, self.low_ref, self.spot, self.count = state_ref, low_ref, spot, count
        self.residual, self.keep = residual, keep
        if self.pad:
            clear_border(low_ref, count)

    def row(self, i):
        state_ref, count = self.state_ref, self.count
        grad = state_ref[0, i, :count] * self.scale + state_ref[self.spot, i, :count] * self.slope + self.offset
        grad = self.inside(i, grad)
        if self.residual:
            grad = grad + state_ref[2, i]
        if self.keep:
            state_ref[2, i] = grad
        self.low_ref[i + self.pad, self.pad : self.pad + count] = grad.astype(LOW)


def pieces(count):
    edges = [count * k // 4 for k in range(5)]
    return list(zip(edges[:-1], edges[1:]))


def mid_backward(odd, residual, cells, *refs):
    sum_ref, st_ref, par_ref, held_ref, w_ref, in_st_ref, in_par_ref, in_v_far = refs[:8]
    state_ref, pair_ref, out_sum_ref, sem = refs[8:]
    count, n = in_v_far.shape[0], in_v_far.shape[2]
    own = count + 1 if odd else count - 1
    low_ref, a_ref = pair_ref.at[0], pair_ref.at[1]
    spot, next_spot = (1, 3) if odd else (3, 1)
    copies = {}
    for k, (low, high) in enumerate(pieces(count)):
        copies[low] = pltpu.make_async_copy(
            in_v_far.at[low:high], state_ref.at[next_spot, low:high, :count], sem.at[k]
        )
        copies[low].start()
    inputs = NormInputGrads(sum_ref, st_ref, par_ref, state_ref, spot, own, low_ref, odd, cells, residual, odd)
    outputs = ActivationGrads(
        state_ref.at[0], state_ref.at[next_spot], count, in_st_ref, in_par_ref, a_ref, not odd, cells, True
    )

    def work(k, size):
        left = jnp.concatenate(four_views(low_ref, k, size, count), axis=1)
        value = jnp.dot(left, w_ref[...], preferred_element_type=WIDE)
        state_ref[0, k : k + size, :count] = value.reshape(size, count, n, 256)

    def after(k):
        if k in copies:
            copies[k].wait()
        outputs.add(k)

    staged(own, count, odd, 17, inputs.row, work, after)
    outputs.store(out_sum_ref)


def window_backward(width, arrays, cells, *refs):
    d_refs = refs[:arrays]
    w_ref, st_ref, par_ref, v_far, state_ref, a_ref, sum_ref, sem = refs[arrays:]
    count, n = v_far.shape[0], v_far.shape[2]
    copy = pltpu.make_async_copy(v_far, state_ref.at[1], sem.at[0])
    copy.start()
    outputs = ActivationGrads(
        state_ref.at[0], state_ref.at[1], count, st_ref, par_ref, a_ref, True, cells, False
    )
    done = []
    for index, spots in enumerate(runs(count)):
        left = jnp.concatenate(
            [
                jnp.concatenate([window_left(d_ref, spot, width) for d_ref in d_refs], axis=1)
                for spot in spots
            ],
            axis=0,
        )
        value = jnp.dot(left, w_ref[...], preferred_element_type=WIDE).reshape(len(spots), count, n, 256)
        for k, spot in enumerate(spots):
            state_ref[0, :, spot] = value[k]
        if index == 1:
            copy.wait()
        for spot in done:
            outputs.add(spot)
        done = spots
    for spot in done:
        outputs.add(spot)
    outputs.store(sum_ref)


def entry_backward(cells, inputs, *refs):
    sum_ref, st_ref, par_ref, state_ref = refs[:4]
    low_ref = refs[5] if inputs else refs[4]
    count = low_ref.shape[0]
    grads = NormInputGrads(sum_ref, st_ref, par_ref, state_ref, 1, count, low_ref, True, cells, True, False)
    for i in range(count):
        grads.row(i)
    if inputs:
        w_ref, low_ref, o_ref, value_ref = refs[4:]
        count, n = value_ref.shape[0], value_ref.shape[2]
        for start, size in groups(count):
            left = jnp.concatenate(four_views(low_ref, start, size, count), axis=1)
            value = jnp.dot(left, w_ref[...], preferred_element_type=WIDE)
            value_ref[start : start + size] = value.reshape(size, count, n, 128)

        def store(item, value):
            o_ref[item] = value

        to_rows(value_ref, 16, 2, store)


def block_weight_grad(odd, spot, pair_ref, *refs):
    o_ref, acc_ref = refs[-2:]
    low_ref, a_ref = pair_ref.at[0], pair_ref.at[1]
    pad = 0 if odd else 1
    count = low_ref.shape[0] - (1 if odd else 2)
    n = low_ref.shape[2]
    for index, (start, size) in enumerate(groups(count)):
        grad = low_ref[start + pad : start + pad + size, pad : pad + count].reshape(size * count * n, 256)
        right = jnp.concatenate(four_views(a_ref, start, size, count), axis=1)
        part = lax.dot_general(grad, right, (((0,), (0,)), ((), ())), preferred_element_type=WIDE)
        if index == 0:
            acc_ref[...] = part
        else:
            acc_ref[...] += part
    for dy in range(3):
        for dx in range(3):
            total = None
            for q in range(2):
                for s in range(2):
                    r, c = dy + q, dx + s
                    lane = ((r // 2) * 2 + c // 2) * 256 + ((r % 2) * 2 + c % 2) * 64
                    part = acc_ref[(2 * q + s) * 64 : (2 * q + s) * 64 + 64, lane : lane + 64]
                    total = part if total is None else total + part
            total = total.T
            start = 288 * spot + 32 * (3 * dy + dx)
            o_ref[start : start + 32, :64] = total[:32]
            o_ref[start : start + 32, 64:] = total[32:]


def window_weight_grad(width, arrays, *refs):
    x_refs = refs[:arrays]
    b_ref, place_ref, o_ref, acc_ref = refs[arrays:]
    count, n = b_ref.shape[0], b_ref.shape[2]
    for spots in runs(count):
        right = jnp.concatenate(
            [
                jnp.concatenate([window_left(x_ref, spot, width) for x_ref in x_refs], axis=1)
                for spot in spots
            ],
            axis=0,
        )
        left = jnp.concatenate([b_ref[:, spot].reshape(count * n, 256) for spot in spots], axis=0)
        part = lax.dot_general(left, right, (((0,), (0,)), ((), ())), preferred_element_type=WIDE)
        if spots[0] == 0:
            acc_ref[...] = part
        else:
            acc_ref[...] += part
    lane = lax.broadcasted_iota(jnp.int32, (64, 128), 1) // 32
    total = None
    for p in range(4):
        parts = []
        for array in range(arrays):
            held = jnp.zeros((64, 128), WIDE)
            for r in range(4):
                start = 512 * array + 128 * r
                value = rolled(acc_ref[64 * p : 64 * p + 64, start : start + 128], 32 * r)
                held = jnp.where(lane == r, value, held)
            parts.append(held)
        one = jnp.where(hot(place_ref[p : p + 1], 72 * arrays), 1.0, 0.0)
        part = exact_dot(one, jnp.concatenate(parts, axis=1), ((1,), (1,)))
        total = part if total is None else total + part
    o_ref[...] = total


def lane_ids(shape):
    return lax.broadcasted_iota(jnp.int32, shape, len(shape) - 1)


def flat_roll(value, shift):
    return rolled(value.reshape(-1, 128), shift).reshape(value.shape)


def valid_lanes(cells):
    held = jnp.where(lane_ids(cells.shape) % 4 == 3, cells, 0.0)
    return flat_roll(held, -1) + flat_roll(held, -2) + flat_roll(held, -3)


def pad_rows(x_ref, values):
    rows, n = values.shape[0], values.shape[1]
    x_ref[0:2] = jnp.zeros((2, n, 128), x_ref.dtype)
    x_ref[2 : 2 + rows] = values.astype(x_ref.dtype)
    x_ref[2 + rows :] = jnp.zeros((2, n, 128), x_ref.dtype)


def column_line(value):
    return jnp.sum(value.reshape(-1, 128), axis=0, keepdims=True)


def checks(shape):
    lane = lane_ids(shape)
    row = lax.broadcasted_iota(jnp.int32, shape, 0)
    return ((row + lane // 4) % 2 == 1) & (lane % 4 != 3)


def prepare(cells_ref, x_ref, logits_ref, sum_ref):
    cells = cells_ref[...]
    lane = lane_ids(cells.shape)
    channel = lane % 4 != 3
    valid = valid_lanes(cells)
    prob = ALPHA + (1.0 - 2.0 * ALPHA) * (cells / 256.0)
    log_in = jnp.log(prob)
    log_out = jnp.log(1.0 - prob)
    logits = jnp.where(channel, log_in - log_out, 0.0)
    jacobian = math.log(1.0 - 2.0 * ALPHA) - log_in - log_out
    logits_ref[...] = logits
    sum_ref[0:1] = column_line(valid)
    sum_ref[1:2] = column_line(valid * (HALF_LOG_TAU + LOG_LEVELS - jacobian))
    odd = checks(cells.shape)
    pad_rows(x_ref, jnp.where(odd, 1.0, logits))


def couple(line_ref, raw_ref, logits_ref, cells_ref, top_ref, low_ref, bend_ref, sum_ref):
    logits = logits_ref[...]
    valid = valid_lanes(cells_ref[...])
    gain = line_ref[0:1].reshape(1, 1, 128)
    total = jnp.zeros((1, 128), WIDE)
    for q in range(2):
        raw = raw_ref[q] + line_ref[1 + q : 2 + q].reshape(1, 1, 128)
        own = logits_ref[pl.ds(q, raw.shape[0], 2)]
        cells = cells_ref[pl.ds(q, raw.shape[0], 2)]
        lane = lane_ids(raw.shape)
        odd = ((q + lane // 4) % 2 == 1) & (lane % 4 != 3)
        shift = flat_roll(raw, 4 if q == 0 else -4)
        bend = jnp.where(odd, jnp.tanh(raw), 0.0)
        scale = gain * bend
        coupled = jnp.where(odd, own * jnp.exp(scale) + shift, own)
        bend_ref[q] = bend
        total = total - column_line(valid_lanes(cells) * scale)
        (top_ref, low_ref)[q][...] = jnp.where(lane % 4 == 3, cells, coupled)
    sum_ref[...] = total


def enter_two(coupled_ref, x_ref):
    value = coupled_ref[...]
    pad_rows(x_ref, jnp.where(lane_ids(value.shape) % 4 == 3, 0.0, value))


def losses(mine_ref, line_ref, count_ref, raw_ref, top_ref, low_ref, other_ref, scale_d_ref, shift_d_ref, grad_ref, sum_ref):
    half = top_ref.shape[0]
    shape = top_ref.shape
    channel = lane_ids(shape) % 4 != 3
    top = top_ref[...]
    low = jnp.concatenate(
        [
            jnp.where(mine_ref[0] == 0, low_ref[...], other_ref[...]),
            jnp.where(mine_ref[0] == 0, other_ref[...], low_ref[...]),
        ],
        axis=1,
    )
    top_valid = valid_lanes(top)
    low_valid = valid_lanes(low)
    top = jnp.where(channel, top, 0.0)
    low = jnp.where(channel, low, 0.0)

    def rows(item):
        pair = jnp.stack([raw_ref[item], raw_ref[2 + item]], axis=1)
        return pair.reshape(shape) + line_ref[4 + item : 5 + item].reshape(1, 1, 128)

    gain = line_ref[3:4].reshape(1, 1, 128)
    unit = 1.0 / (LOG_TWO * jnp.sum(count_ref[0:1], axis=1, keepdims=True)).reshape(1, 1, 1)
    bend = jnp.tanh(rows(0))
    scale = gain * bend
    grow = jnp.exp(scale)
    latent = jnp.where(channel, low * grow + rows(1), 0.0)
    sum_ref[0:1] = column_line(top_valid * (0.5 * top * top) + low_valid * (0.5 * latent * latent - scale))
    moved = low_valid * unit * latent
    grad_scale = moved * low * grow - low_valid * unit
    raw_grad = grad_scale * gain * (1.0 - bend * bend)
    sum_ref[1:2] = column_line(grad_scale * bend)
    sum_ref[2:3] = column_line(raw_grad)
    sum_ref[3:4] = column_line(moved)
    pad_rows(scale_d_ref, raw_grad)
    pad_rows(shift_d_ref, moved)
    grad_ref[pl.ds(0, half, 2)] = top_valid * unit * top
    grad_ref[pl.ds(1, half, 2)] = moved * grow


def uncouple(mine_ref, line_ref, count_ref, entry_ref, grad_ref, logits_ref, bend_ref, cells_ref, d_ref, sum_ref):
    half = logits_ref.shape[0] // 2
    n = logits_ref.shape[1]
    own_part = pl.ds(pl.multiple_of(mine_ref[0], 8), n)
    gain = line_ref[0:1].reshape(1, 1, 128)
    unit = 1.0 / (LOG_TWO * jnp.sum(count_ref[0:1], axis=1, keepdims=True)).reshape(1, 1, 1)
    lines = [jnp.zeros((1, 128), WIDE)] * 3
    d_ref[0:2] = jnp.zeros((2, n, 128), d_ref.dtype)
    d_ref[2 * half + 2 :] = jnp.zeros((d_ref.shape[0] - 2 * half - 2, n, 128), d_ref.dtype)
    for q in range(2):
        grad = grad_ref[pl.ds(q, half, 2), own_part]
        if q == 0:
            grad = grad + jnp.stack([entry_ref[0, :, own_part], entry_ref[1, :, own_part]], axis=1).reshape(half, n, 128)
        own = logits_ref[pl.ds(q, half, 2)]
        valid = valid_lanes(cells_ref[pl.ds(q, half, 2)])
        bend = bend_ref[q]
        lane = lane_ids(grad.shape)
        odd = ((q + lane // 4) % 2 == 1) & (lane % 4 != 3)
        grad = jnp.where(odd, grad, 0.0)
        grad_scale = jnp.where(odd, grad * own * jnp.exp(gain * bend) - valid * unit, 0.0)
        raw_grad = grad_scale * gain * (1.0 - bend * bend)
        lines[0] = lines[0] + column_line(grad_scale * bend)
        lines[1] = lines[1] + column_line(raw_grad)
        lines[2] = lines[2] + column_line(grad)
        value = raw_grad + flat_roll(grad, -4 if q == 0 else 4)
        d_ref[pl.ds(2 + q, half, 2)] = value.astype(d_ref.dtype)
    for spot in range(3):
        sum_ref[spot : spot + 1] = lines[spot]


def call(kernel, outs, args, name, scratch=(), limit=16, far_in=(), far_out=(), sems=0, aliases=None, scalar_in=()):
    spaces = [
        pltpu.HBM if spot in far_in else pltpu.SMEM if spot in scalar_in else pltpu.VMEM
        for spot in range(len(args))
    ]
    out_spaces = [pltpu.HBM if spot in far_out else pltpu.VMEM for spot in range(len(outs))]
    held = [pltpu.VMEM(shape, dtype) for shape, dtype in scratch]
    args = [pltpu.with_memory_space_constraint(arg, space) if space is pltpu.HBM else arg for arg, space in zip(args, spaces)]
    if sems:
        held.append(pltpu.SemaphoreType.DMA(sems))
    return pl.pallas_call(
        kernel,
        out_shape=[space(shape, dtype) for space, (shape, dtype) in zip(out_spaces, outs)],
        in_specs=[pl.BlockSpec(memory_space=space) for space in spaces],
        out_specs=[pl.BlockSpec(memory_space=space) for space in out_spaces],
        scratch_shapes=held,
        compiler_params=pltpu.CompilerParams(vmem_limit_bytes=limit * 2**20),
        input_output_aliases=aliases or {},
        cost_estimate=pl.CostEstimate(
            flops=int(1e+09 * COSTS.get(name, 0.5)), bytes_accessed=0, transcendentals=0
        ),
        name=name,
    )(*args)


class Net:
    def __init__(self, name, blocks, n, width, group, total, pars, weights, turned_weights):
        self.name = name
        self.even = blocks
        self.odd = blocks + 1
        self.n = n
        self.width = width
        self.group = group
        self.cells = float(total)
        self.own = float(n * blocks * blocks * 4)
        self.pars = pars
        self.weights = weights
        self.turned_weights = turned_weights
        self.far = []
        self.stats = []

    def shape(self, odd, padded=False):
        count = self.odd if odd else self.even
        pad = 2 if padded and not odd else 0
        return (count + pad, count + pad, self.n, 256)

    def keep(self, stats, far):
        self.far.append(far)
        self.stats.append(merge_stats(stats, self.own, self.group))

    def forward(self, x, entry, exit_weights, items, beside):
        held = (2,) + self.shape(True)
        state, stats, far = call(
            functools.partial(window_forward, self.width),
            [(held, WIDE), ((2, 256), WIDE), (self.shape(True), WIDE)],
            [x, entry],
            self.name + "_entry",
            far_out=(2,),
            sems=(1,),
        )
        self.keep(stats, far)
        self.stats[0], beside = lax.optimization_barrier((self.stats[0], beside))
        for index in range(4):
            odd = index % 2 == 0
            state, stats, far = call(
                functools.partial(mid_forward, odd, self.cells),
                [(held, WIDE), ((2, 256), WIDE), (self.shape(not odd), WIDE)],
                [self.stats[index], self.pars[index], state, self.weights[index]],
                self.name + "_forward",
                [(self.shape(odd, True), LOW)],
                far_out=(2,),
                sems=(self.odd,),
                aliases={2: 0},
            )
            self.keep(stats, far)
        raw = call(
            functools.partial(exit_forward, self.cells, 2 * self.width, items),
            [((items, self.even, self.n, 128), WIDE)],
            [self.stats[4], self.pars[4], state, exit_weights],
            self.name + "_exit",
            [(self.shape(True), LOW), ((self.even, self.even, self.n, 128), WIDE)],
        )[0]
        return raw, beside

    def backward(self, grads, exit_turned, exit_place, x, entry_turned, entry_place, packets, slots):
        arrays = len(grads)
        held = (4,) + self.shape(True)
        pair_shape = (2, self.even + 2, self.even + 2, self.n, 256)
        state, act, sums = call(
            functools.partial(window_backward, self.width, arrays, self.cells),
            [(held, WIDE), (self.shape(True), LOW), ((2, 256), WIDE)],
            list(grads) + [exit_turned, self.stats[4], self.pars[4], self.far[4]],
            self.name + "_exit_back",
            far_in=(arrays + 3,),
            sems=(1,),
        )
        results_of = {}

        def exit_work(token):
            (held,) = tied([act], token)
            grad = call(
                functools.partial(window_weight_grad, self.width, arrays),
                [((72 * arrays, 64), WIDE)],
                list(grads) + [held, exit_place],
                self.name + "_exit_weights",
                [((256, 512 * arrays), WIDE)],
            )[0]
            return (grad,) + slots.get(4, lambda *held: ())(None, grad, token)

        sums, exit_grad, *done = travel(sums, self.group, exit_work)
        results_of[4] = done
        norm_grads = [None] * 5
        block_grads = []
        norm_grads[4] = sums
        for index in reversed(range(4)):
            odd = index % 2 == 1
            state, pair, sums = call(
                functools.partial(mid_backward, odd, index == 1, self.cells),
                [(held, WIDE), (pair_shape, LOW), ((2, 256), WIDE)],
                [
                    sums,
                    self.stats[index + 1],
                    self.pars[index + 1],
                    state,
                    self.turned_weights[index],
                    self.stats[index],
                    self.pars[index],
                    self.far[index],
                ],
                self.name + "_back",
                far_in=(7,),
                sems=(4,),
                aliases={3: 0},
            )
            packet = next(held for held in packets if index in held)
            spot = packet.index(index)
            fresh = index == packet[-1]

            def block_work(token):
                (held,) = tied([pair], token)
                grad = call(
                    functools.partial(block_weight_grad, odd, spot),
                    [((288 * len(packet), 128), WIDE)],
                    [held] + ([] if fresh else [block]),
                    self.name + "_weights",
                    [((256, 1024), WIDE)],
                    aliases=None if fresh else {1: 0},
                )[0]
                return (grad,) + slots.get(index, lambda *held: ())(block_grads, exit_grad, token)

            sums, block, *done = travel(sums, self.group, block_work)
            results_of[index] = done
            norm_grads[index] = sums
            if index == packet[0]:
                block_grads.append(swap_terms(block, self.group))
        args = [sums, self.stats[0], self.pars[0], state]
        outs = [(self.shape(True), LOW)]
        scratch = []
        if entry_turned is not None:
            args.append(entry_turned)
            outs.append(((2, self.even, self.n, 128), WIDE))
            scratch.append(((self.even, self.even, self.n, 128), WIDE))
        results = call(
            functools.partial(entry_backward, self.cells, entry_turned is not None),
            outs,
            args,
            self.name + "_entry_back",
            scratch,
        )

        def entry_grad(token):
            low, unused = lax.optimization_barrier((results[0], token))
            return call(
                functools.partial(window_weight_grad, self.width, 1),
                [((72, 64), WIDE)],
                [x, low, entry_place],
                self.name + "_entry_weights",
                [((256, 512), WIDE)],
            )[0]

        return entry_grad, block_grads, exit_grad, norm_grads, results_of, (results[1] if entry_turned is not None else None)


def adam_blocks(spots, fresh, places, *refs):
    count = 2 * (1 + max(place[0] for place in places))
    terms, refs = refs[:count], refs[count:]
    sources, refs = refs[:3], refs[3:]
    if not fresh:
        refs = refs[4:]
    targets, (held, out, out_low, in_sem, out_sem) = refs[:4], refs[4:]
    loads = []
    for k, spot in enumerate(spots):
        loads.append(
            [pltpu.make_async_copy(sources[j].at[spot], held.at[k, j], in_sem.at[k, j]) for j in range(3)]
        )
        for copy in loads[-1]:
            copy.start()
    stores = []
    for k, spot in enumerate(spots):
        for copy in loads[k]:
            copy.wait()
        for t in range(9):
            pair, row = 2 * places[k][0], 288 * places[k][1] + 32 * t
            packed = terms[pair][row : row + 32] + terms[pair + 1][row : row + 32]
            grad = jnp.concatenate([packed[:, :64], packed[:, 64:]], axis=0)
            news = adamw(held[k, 0, t], held[k, 1, t], held[k, 2, t], grad, RATE_CONV)
            for j in range(3):
                out[k, j, t] = news[j]
            out_low[k, t] = news[3]
        copies = [pltpu.make_async_copy(out.at[k, j], targets[j].at[spot], out_sem.at[k, j]) for j in range(3)]
        copies.append(pltpu.make_async_copy(out_low.at[k], targets[3].at[spot], out_sem.at[k, 3]))
        for copy in copies:
            copy.start()
        stores += copies
    for copy in stores:
        copy.wait()


def step_blocks(spots, pairs, places, sources, targets):
    count = len(spots)
    terms = [term for pair in pairs for term in pair]
    args = terms + list(sources) + list(targets or [])
    shape = sources[0].shape
    head = len(terms)
    return pl.pallas_call(
        functools.partial(adam_blocks, spots, targets is None, places),
        out_shape=[pltpu.HBM(shape, WIDE)] * 3 + [pltpu.HBM(shape, LOW)],
        in_specs=[pl.BlockSpec(memory_space=pltpu.VMEM)] * head
        + [pl.BlockSpec(memory_space=pltpu.HBM)] * (len(args) - head),
        out_specs=[pl.BlockSpec(memory_space=pltpu.HBM)] * 4,
        scratch_shapes=[
            pltpu.VMEM((count, 3) + shape[1:], WIDE),
            pltpu.VMEM((count, 3) + shape[1:], WIDE),
            pltpu.VMEM((count,) + shape[1:], LOW),
            pltpu.SemaphoreType.DMA((count, 3)),
            pltpu.SemaphoreType.DMA((count, 4)),
        ],
        input_output_aliases={} if targets is None else {head + 3 + j: j for j in range(4)},
        compiler_params=pltpu.CompilerParams(vmem_limit_bytes=12 * 2**20),
        cost_estimate=pl.CostEstimate(flops=int(1e+09 * (1 + count)), bytes_accessed=0, transcendentals=0),
        name="step_blocks",
    )(*args[:head], *[pltpu.with_memory_space_constraint(arg, pltpu.HBM) for arg in args[head:]])


def adamw(master, first, second, grad, rate):
    first_new = BETA_ONE * first + (1.0 - BETA_ONE) * grad
    second_new = BETA_TWO * second + (1.0 - BETA_TWO) * grad * grad
    direction = (
        first_new
        / (1.0 - BETA_ONE**STEP)
        / (jnp.sqrt(second_new / (1.0 - BETA_TWO**STEP)) + ADAM_EPS)
    )
    master_new = master - rate * (direction + DECAY * master)
    return (master_new, first_new, second_new, master_new.astype(jnp.bfloat16))


def entry_view(array):
    return array.transpose(1, 2, 3, 0, 4).reshape(54, 2, 64)


def exit_view(array):
    return array.transpose(0, 1, 3, 2).reshape(9, array.shape[3], 64)


def pack_rows(*refs):
    o_ref = refs[-1]
    o_ref[...] = jnp.zeros(o_ref.shape, WIDE)
    row = 0
    for ref in refs[:-1]:
        o_ref[row : row + ref.shape[0], : ref.shape[1]] = ref[...]
        row += ref.shape[0]


def entry_grads(one_ref, one_other, two_ref, two_other, o_ref):
    one = one_ref[...] + one_other[...]
    two = two_ref[0:72, :64] + two_other[0:72, :64]
    for t in range(9):
        o_ref[6 * t : 6 * t + 6, 0] = one[8 * t : 8 * t + 6]
        o_ref[6 * t : 6 * t + 6, 1] = two[8 * t : 8 * t + 6]


def finish_kernel(*refs):
    one_ref, one_other, two_ref, two_other, count_ref = refs[:5]
    norm_sums, place_ref = refs[5:15], refs[15]
    exit_one, exit_two, norm, head = refs[16:19], refs[19:22], refs[22:25], refs[25:28]
    far, near, sem = refs[28:46], refs[46:64], refs[64]
    loss_o, valid_o = near[0:2]
    exit_one_o, exit_two_o, norm_o, head_o = near[2:6], near[6:10], near[10:14], near[14:18]
    one = one_ref[...] + one_other[...]
    two = two_ref[...] + two_other[...]

    def store(outs, index, values):
        for o_ref, value in zip(outs, values):
            o_ref[index] = value

    for t in range(9):
        grad = one[8 * t : 8 * t + 6, :64]
        store(exit_one_o, t, adamw(exit_one[0][t], exit_one[1][t], exit_one[2][t], grad, RATE_CONV))
        grad = two[72 + 16 * t : 84 + 16 * t, :64]
        store(exit_two_o, t, adamw(exit_two[0][t], exit_two[1][t], exit_two[2][t], grad, RATE_CONV))
    for k in range(10):
        spot = (k // 5, k % 5)
        sums = norm_sums[k][...]
        grad = jnp.concatenate([sums[1:2, :64], sums[0:1, :64]], axis=0) * 0.5
        store(norm_o, spot, adamw(norm[0][spot], norm[1][spot], norm[2][spot], grad, RATE_SMALL))
    valid = jnp.sum(count_ref[0:1], axis=1, keepdims=True)
    constant = jnp.sum(count_ref[1:2], axis=1, keepdims=True)
    loss = jnp.sum(two[216:217], axis=1, keepdims=True) + jnp.sum(one[75:76], axis=1, keepdims=True)
    loss_o[...] = (loss + constant) / LOG_TWO
    valid_o[...] = valid

    def folded(line, spot):
        return exact_dot(line, jnp.where(hot(place_ref[spot : spot + 1], head[0].shape[1]), 1.0, 0.0), ((1,), (1,)))

    lane = lax.broadcasted_iota(jnp.int32, (1, 128), 1)
    raw, shift = one[73:74], one[74:75]
    grad = folded(one[72:73], 0) + folded(two[217:218], 3) + folded(two[218:219], 4) + folded(two[219:220], 5)
    grad = grad + folded(jnp.where((lane // 4) % 2 == 1, raw, 0.0), 1) + folded(jnp.where((lane // 4) % 2 == 0, raw, 0.0), 2)
    grad = grad + folded(jnp.where((lane // 4) % 2 == 0, shift, 0.0), 1) + folded(jnp.where((lane // 4) % 2 == 1, shift, 0.0), 2)
    for o_ref, value in zip(head_o, adamw(head[0][...], head[1][...], head[2][...], grad, RATE_SMALL)):
        o_ref[...] = value
    copies = [pltpu.make_async_copy(near[k], far[k], sem.at[k]) for k in range(18)]
    for copy in copies:
        copy.start()
    for copy in copies:
        copy.wait()


def finish(packs, sums, place, exit_one, exit_two, norm, head):
    outs = [((1, 1), WIDE)] * 2
    for first in (exit_one[0], exit_two[0], norm[0], head[0]):
        outs += [(first.shape, WIDE)] * 3 + [(first.shape, LOW)]
    return call(
        finish_kernel,
        outs,
        packs + sums + [place] + exit_one + exit_two + norm + head,
        "finish",
        outs,
        far_out=tuple(range(18)),
        sems=(18,),
    )


def body(
    pixels,
    valid,
    entry_conv,
    entry_first,
    entry_second,
    block_conv,
    block_first,
    block_second,
    exit_one,
    exit_one_first,
    exit_one_second,
    exit_two,
    exit_two_first,
    exit_two_second,
    norm_params,
    norm_first,
    norm_second,
    head_params,
    head_first,
    head_second,
):
    batch = pixels.shape[0] * lax.axis_size("batch")
    height = pixels.shape[1] * lax.axis_size("rows")
    group = group_bits(batch)
    small = group[:-1]
    last = group[-1]
    own = batch >> len(group)
    wide = 2 * own
    cells = jnp.concatenate([pixels, valid[..., None].astype(WIDE)], axis=3)
    cells = cells.reshape(pixels.shape[0], pixels.shape[1], 128).transpose(1, 0, 2)

    place = placements()
    small_places = [
        jnp.asarray(place[key])
        for key in (
            "entry_one",
            "entry_two",
            "entry_two_turned",
            "exit_one",
            "exit_one_turned",
            "exit_two",
            "exit_two_turned",
        )
    ]
    fold = [
        jnp.asarray(place[key + "_fold"])
        for key in ("entry_one", "entry_two", "exit_one_turned", "exit_two_turned")
    ]
    small_built = call(
        build_small,
        [
            ((512, 256), LOW),
            ((512, 256), LOW),
            ((1024, 128), LOW),
            ((1024, 128), LOW),
            ((512, 256), LOW),
            ((1024, 128), LOW),
            ((1024, 256), LOW),
            ((8, 128), WIDE),
        ]
        + [((2, 256), WIDE)] * 10,
        [
            entry_view(entry_conv),
            exit_view(exit_one),
            exit_view(exit_two),
            norm_params,
            head_params[None],
        ]
        + small_places
        + [jnp.asarray(place["head"])],
        "build_small",
        [((72, 64), WIDE), ((144, 64), WIDE)],
    )
    cells, small_built = distribute(cells, group, small_built)
    (
        entry_one_w,
        entry_two_w,
        entry_turned_w,
        exit_one_w,
        exit_one_turned_w,
        exit_two_w,
        exit_two_turned_w,
        head_lines,
        *par_lines,
    ) = small_built
    blocks = call(build_blocks, [((1024, 256), LOW)] * 16, [block_conv.reshape(8, 9, 64, 64)], "build_blocks")
    weights = [[blocks[4 * j + k] for k in range(4)] for j in range(2)]
    turned_w = [[blocks[8 + 4 * j + k] for k in range(4)] for j in range(2)]
    pars = [[par_lines[5 * j + k] for k in range(5)] for j in range(2)]

    one = Net("one", height // 2, own, 4, group, batch * height * height, pars[0], weights[0], turned_w[0])
    two = Net("two", height // 4, wide, 8, small, batch * (height // 2) ** 2, pars[1], weights[1], turned_w[1])

    rows = height
    x_one, logits, first_sums = call(
        prepare,
        [((rows + 4, own, 128), WIDE), ((rows, own, 128), WIDE), ((2, 128), WIDE)],
        [cells],
        "prepare",
    )
    first_sums = group_sum(first_sums, group)
    mine, x_one = lax.optimization_barrier((side(last) * own, x_one))
    raw_one, first_sums = one.forward(x_one, entry_one_w, exit_one_w, 2, first_sums)
    coupled_top, coupled_low, bend_one, couple_sums = call(
        couple,
        [((rows // 2, own, 128), WIDE)] * 2 + [((2, rows // 2, own, 128), WIDE), ((1, 128), WIDE)],
        [head_lines, raw_one, logits, cells],
        "couple",
    )
    coupled_top = joined(coupled_top, swap(coupled_top, last), mine, 1)
    other_low = swap(coupled_low, last)
    x_two = call(enter_two, [((rows // 2 + 4, wide, 128), WIDE)], [coupled_top], "enter_two")[0]
    raw_two, other_low = two.forward(x_two, entry_two_w, exit_two_w, 4, other_low)
    scale_d, shift_d, grad_coupled, loss_sums = call(
        losses,
        [
            ((rows // 2 + 4, wide, 128), WIDE),
            ((rows // 2 + 4, wide, 128), WIDE),
            ((rows, wide, 128), WIDE),
            ((4, 128), WIDE),
        ],
        [
            jnp.reshape(mine, (1,)),
            head_lines,
            first_sums,
            raw_two,
            coupled_top,
            coupled_low,
            other_low,
        ],
        "losses",
        scalar_in=(0,),
    )
    entry_two, blocks_two, exit_two_part, norms_two, unused, grad_first = two.backward(
        [scale_d, shift_d], exit_two_turned_w, fold[3], x_two, entry_turned_w, fold[1], [[0, 1, 2, 3]], {}
    )
    def send_two(held, exit_grad, token):
        rows = call(pack_rows, [((224, 128), WIDE)], [entry_two(token), exit_two_part, loss_sums], "pack_two")[0]
        return tuple(swap_terms(rows, small))

    def send_one(held, exit_grad, token):
        rows = call(pack_rows, [((80, 128), WIDE)], [exit_grad, one_sums, couple_sums], "pack_one")[0]
        return tuple(swap_terms(rows, group))

    sources = [part.reshape(8, 9, 64, 64) for part in (block_conv, block_first, block_second)]
    steps = {}

    def step(key, spots, terms, firsts):
        def run(held, exit_grad, token):
            steps[key] = tuple(
                step_blocks(spots, [tied(terms, token)], [(0, k) for k in firsts], sources, steps.get(key - 1))
            )
            return steps[key]

        return run

    one_d, one_sums = call(
        uncouple,
        [((rows + 4, own, 128), WIDE), ((3, 128), WIDE)],
        [jnp.reshape(mine, (1,)), head_lines, first_sums, grad_first, grad_coupled, logits, bend_one, cells],
        "uncouple",
        scalar_in=(0,),
    )
    slots = {
        4: send_two,
        3: send_one,
        2: step(0, (4, 5), blocks_two[0], (0, 1)),
        0: step(1, (6, 7), blocks_two[0], (2, 3)),
    }
    entry_one, blocks_one, exit_one_part, norms_one, done, unused = one.backward(
        [one_d], exit_one_turned_w, fold[2], x_one, None, fold[0], [[1, 2, 3], [0]], slots
    )
    entry_one, *blocks_done = lax.optimization_barrier((entry_one(first_sums), *blocks_one[0]))
    entry_one = swap_terms(entry_one, group)
    pack_two, pack_one = list(done[4]), list(done[3])
    stepped = step_blocks(
        (1, 2, 3), [blocks_done], [(0, 0), (0, 1), (0, 2)], sources, done[0]
    )
    finished = finish(
        pack_one + pack_two,
        [first_sums] + norms_one + norms_two,
        jnp.asarray(place["head"]),
        [exit_view(part) for part in (exit_one, exit_one_first, exit_one_second)],
        [exit_view(part) for part in (exit_two, exit_two_first, exit_two_second)],
        [norm_params, norm_first, norm_second],
        [part[None] for part in (head_params, head_first, head_second)],
    )
    stepped = step_blocks((0,), [blocks_one[1]], [(0, 0)], sources, stepped)
    entry_grad = call(
        entry_grads, [((54, 2, 64), WIDE)], entry_one + pack_two, "entry_grads"
    )[0]
    entry_steps = adamw(
        entry_view(entry_conv), entry_view(entry_first), entry_view(entry_second), entry_grad, RATE_CONV
    )
    entry_out = tuple(
        part.reshape(3, 3, 6, 2, 64).transpose(3, 0, 1, 2, 4) for part in entry_steps
    )
    one_out = tuple(part.reshape(3, 3, 6, 64).transpose(0, 1, 3, 2) for part in finished[2:6])
    two_out = tuple(part.reshape(3, 3, 12, 64).transpose(0, 1, 3, 2) for part in finished[6:10])
    return (
        (finished[0].reshape(()), finished[1].reshape(()))
        + entry_out
        + tuple(part.reshape(block_conv.shape) for part in stepped)
        + one_out
        + two_out
        + tuple(finished[10:14])
        + tuple(part.reshape(head_params.shape) for part in finished[14:18])
    )


def solution(mesh):
    placed = (P("batch", "rows", None, None), P("batch", "rows", None)) + (P(),) * 18
    return jax.shard_map(body, mesh=mesh, in_specs=placed, out_specs=(P(),) * 26, check_vma=False)
```

```python
import functools
import math

import jax
import jax.numpy as jnp
import numpy as np
from jax import lax
from jax.experimental import pallas as pl
from jax.experimental.pallas import tpu as pltpu
from jax.sharding import PartitionSpec as P

STEP = 10
ALPHA = 0.05
NORM_EPS = 1e-05
BETA_ONE = 0.9
BETA_TWO = 0.999
ADAM_EPS = 1e-08
DECAY = 0.01
RATE_CONV = 1.0
RATE_SMALL = 10.0
LOG_TWO = math.log(2.0)
HALF_LOG_TAU = 0.5 * math.log(2.0 * math.pi)
LOG_LEVELS = math.log(256.0)
IMAGES = 16
BITS = (("batch", 1), ("batch", 2), ("rows", 1), ("rows", 2), ("batch", 4), ("batch", 8), ("batch", 16), ("batch", 32))
LOW = jnp.bfloat16
WIDE = jnp.float32
COSTS = {
    "one_entry": 4.0,
    "one_forward": 3.7,
    "one_exit": 2.5,
    "one_exit_back": 5.7,
    "one_exit_weights": 2.6,
    "one_back": 5.4,
    "one_weights": 3.0,
    "one_entry_weights": 2.7,
    "two_entry": 2.7,
    "two_forward": 2.5,
    "two_exit": 1.4,
    "two_exit_back": 4.1,
    "two_exit_weights": 3.7,
    "two_back": 3.0,
    "two_weights": 1.9,
    "two_entry_back": 1.5,
    "two_entry_weights": 1.9,
    "build_small": 1.9,
    "build_blocks": 1.0,
    "finish": 1.2,
}


def axis_bits():
    return [bit for bit in BITS if bit[1] < lax.axis_size(bit[0])]


def group_bits(batch):
    bits = axis_bits()
    count = max(batch // IMAGES, 1).bit_length() - 1
    return bits[: min(count, len(bits))]


def swap(value, bit):
    axis, mask = bit
    return lax.ppermute(value, axis, [(i, i ^ mask) for i in range(lax.axis_size(axis))])


def side(bit):
    return (lax.axis_index(bit[0]) // bit[1]) % 2


def group_sum(value, bits):
    for bit in bits:
        value = jax.tree.map(lambda own: own + swap(own, bit), value)
    return value


def travel(sums, bits, work):
    held = sums
    if len(bits) > 1:
        held = sums + swap(sums, bits[0])
        bits = bits[1:]
    results = work(held)
    return lax.optimization_barrier((group_sum(held, bits),) + tuple(results))


def tied(values, token):
    return lax.optimization_barrier((tuple(values), token))[0]


def swap_terms(value, bits):
    value = group_sum(value, bits[:-1])
    return [value, swap(value, bits[-1])]


def joined(own, other, mine, dim):
    first = jnp.where(mine == 0, own, other)
    second = jnp.where(mine == 0, other, own)
    return jnp.concatenate([first, second], axis=dim)


def chosen_part(label, parts):
    found = []
    for k in range(len(parts)):
        value = parts[k]
        for own in range(1, len(parts)):
            value = jnp.where(label == own, parts[k ^ own], value)
        found.append(value)
    return found


def split_parts(label_ref, cells_ref, *o_refs):
    count = cells_ref.shape[1] // len(o_refs)
    parts = [cells_ref[:, count * k : count * k + count] for k in range(len(o_refs))]
    for o_ref, value in zip(o_refs, chosen_part(label_ref[0], parts)):
        o_ref[...] = value


def lay_parts(dim, label_ref, *refs):
    o_ref = refs[-1]
    parts = [ref[...] for ref in refs[:-1]]
    size = parts[0].shape[dim]
    for k, value in enumerate(chosen_part(label_ref[0], parts)):
        if dim == 0:
            o_ref[size * k : size * k + size] = value
        else:
            o_ref[:, size * k : size * k + size] = value


def distribute(cells, group, beside):
    bands = lax.axis_size("rows")
    rows, images = cells.shape[:2]
    row = lax.axis_index("rows")
    mask = sum(bit[1] for bit in group if bit[0] == "rows")
    share = images // (mask + 1)
    pieces = call(
        split_parts,
        [((rows, share, 128), WIDE)] * (mask + 1),
        [jnp.reshape(row & mask, (1,)), cells],
        "split_parts",
        scalar_in=(0,),
    )
    came = [pieces[0]] + [swap(pieces[k & mask], ("rows", k)) for k in range(1, bands)]
    came, beside = lax.optimization_barrier((came, beside))
    cells = call(
        functools.partial(lay_parts, 0),
        [((bands * rows, share, 128), WIDE)],
        [jnp.reshape(row, (1,))] + came,
        "lay_bands",
        scalar_in=(0,),
    )[0]
    others = [bit[1] for bit in axis_bits() if bit[0] == "batch" and bit not in group]
    if not others:
        return cells, beside
    low = others[0]
    came = [cells] + [swap(cells, ("batch", k * low)) for k in range(1, 2 ** len(others))]
    cells = call(
        functools.partial(lay_parts, 1),
        [((bands * rows, share * len(came), 128), WIDE)],
        [jnp.reshape(lax.axis_index("batch") // low, (1,))] + came,
        "lay_images",
        scalar_in=(0,),
    )[0]
    return cells, beside


def merge_stats(both, count, group):
    for bit in group:
        both = call(
            functools.partial(merge_pair, 0.5 * count), [((2, 256), WIDE)], [both, swap(both, bit)], "merge"
        )[0]
        count = 2 * count
    return both


def merge_pair(weight, own_ref, other_ref, o_ref):
    gap = own_ref[0:1] - other_ref[0:1]
    o_ref[0:1] = 0.5 * (own_ref[0:1] + other_ref[0:1])
    o_ref[1:2] = own_ref[1:2] + other_ref[1:2] + gap * gap * weight


def blockify(kernel):
    rows = np.stack([np.pad(kernel, ((q, 1 - q), (0, 0), (0, 0), (0, 0))) for q in range(2)], axis=3)
    return np.stack([np.pad(rows, ((0, 0), (s, 1 - s), (0, 0), (0, 0), (0, 0))) for s in range(2)], axis=4)


def turned(kernel):
    return np.flip(kernel, (0, 1)).transpose(0, 1, 3, 2)


def views(blocked):
    rest = blocked.shape[2:]
    split = blocked.reshape((2, 2, 2, 2) + rest)
    return split.transpose((0, 2, 1, 3) + tuple(range(4, 4 + len(rest)))).reshape((16,) + rest)


def mates(blocked):
    return np.flip(blocked.reshape(4, 2, 2, *blocked.shape[2:]), 2).reshape(blocked.shape)


def spread(values, axis):
    shape = values.shape
    cut = values.reshape(shape[:axis] + (2, 3) + shape[axis + 1 :])
    pad = [(0, 0)] * cut.ndim
    pad[axis + 1] = (0, 1)
    return np.pad(cut, pad).reshape(shape[:axis] + (8,) + shape[axis + 1 :])


def window_rows(weights):
    flat = weights.reshape(4, -1, 4)
    return np.pad(flat, ((0, 0), (0, 128 - flat.shape[1]), (0, 0))).reshape(512, 4)


def checker(odd):
    return ((np.arange(4)[:, None] + np.arange(4)[None, :]) % 2 == odd).reshape(4, 4, 1, 1)


def chosen(blocked, odd):
    both = np.where(checker(odd), blocked[:, :, :3], mates(blocked)[:, :, 3:])
    return window_rows(np.pad(both, ((0, 0), (0, 0), (0, 1), (0, 0))))


def numbered(channels, last):
    pad = 8 if channels == 6 else 16
    number = (pad * np.arange(9)[:, None] + np.arange(1, channels + 1)).reshape(3, 3, 1, channels)
    return number if last else number.transpose(0, 1, 3, 2)


@functools.cache
def placements():
    odd = (np.arange(2)[:, None] + np.arange(2)[None, :]) % 2 == 1
    found = {}
    blocked = blockify(numbered(6, False)).reshape(4, 4, 6, 4)
    found["entry_one"] = chosen(blocked, 0).T
    found["entry_two"] = window_rows(spread(blocked, 2)).T
    blocked = views(blockify(turned(numbered(6, False))))
    lanes = spread(blocked.reshape(16, 2, 2, 6), 3).reshape(16, 2, 16)
    lanes = np.pad(lanes, ((0, 0), (0, 0), (0, 48))).reshape(16, 128)
    found["entry_two_turned"] = lanes
    blocked = views(blockify(numbered(6, True))).reshape(16, 2, 2, 6)
    both = np.where(odd[None, :, :, None], blocked[..., :3], np.flip(blocked, 2)[..., 3:])
    lanes = np.pad(both, ((0, 0), (0, 0), (0, 0), (0, 1))).reshape(16, 2, 8)
    lanes = np.pad(lanes, ((0, 0), (0, 0), (0, 56))).reshape(16, 128)
    found["exit_one"] = lanes
    blocked = blockify(turned(numbered(6, True))).reshape(4, 4, 6, 4)
    found["exit_one_turned"] = chosen(blocked, 1).T
    blocked = views(blockify(numbered(12, True))).reshape(16, 2, 2, 2, 6)
    lanes = spread(blocked, 4).transpose(0, 1, 3, 2, 4).reshape(16, 4, 16)
    lanes = np.pad(lanes, ((0, 0), (0, 0), (0, 16))).reshape(16, 128)
    found["exit_two"] = lanes
    blocked = blockify(turned(numbered(12, True))).reshape(4, 4, 12, 4)
    pair = [window_rows(spread(blocked[:, :, 6 * s : 6 * s + 6], 2)) for s in range(2)]
    found["exit_two_turned"] = np.concatenate(pair).T
    for key in ("entry_one", "entry_two", "exit_one_turned", "exit_two_turned"):
        found[key + "_fold"] = found[key].reshape(4, -1, 128)[:, :, :32].reshape(4, -1)
    number = np.arange(1, 28)

    def line(values, lanes):
        cut = np.pad(values.reshape(-1, 3), ((0, 0), (0, 1))).reshape(-1)
        return np.tile(cut, 128 // lanes)

    pick = (np.arange(128) // 4) % 2
    scale, shift = line(number[9:12], 4), line(number[12:15], 4)
    lines = [
        line(number[0:3], 4),
        np.where(pick == 1, scale, shift),
        np.where(pick == 0, scale, shift),
        line(number[3:9], 8),
        line(number[15:21], 8),
        line(number[21:27], 8),
        np.zeros(128, int),
        np.zeros(128, int),
    ]
    found["head"] = np.stack(lines)
    return {key: value.astype(np.int32) for key, value in found.items()}


def exact_dot(left, right, dims):
    return lax.dot_general(
        left, right, (dims, ((), ())), precision=lax.Precision.HIGHEST, preferred_element_type=WIDE
    )


def hot(line, count):
    return lax.broadcasted_iota(jnp.int32, (count, line.shape[1]), 0) + 1 == line


def place_rows(place_ref, kernel, o_ref):
    for p in range(4):
        one = jnp.where(hot(place_ref[p : p + 1], kernel.shape[0]), 1.0, 0.0).astype(LOW)
        part = lax.dot_general(one, kernel, (((0,), (0,)), ((), ())), preferred_element_type=WIDE)
        o_ref[:, 64 * p : 64 * p + 64] = part.astype(LOW)


def place_lanes(place_ref, kernel, o_ref):
    for p in range(16):
        one = jnp.where(hot(place_ref[p : p + 1], kernel.shape[0]), 1.0, 0.0).astype(LOW)
        part = lax.dot_general(kernel, one, (((0,), (0,)), ((), ())), preferred_element_type=WIDE)
        o_ref[64 * p : 64 * p + 64] = part.astype(LOW)


def padded_kernel(rows, scratch, width):
    scratch[...] = jnp.zeros(scratch.shape, WIDE)
    for t in range(9):
        value = rows(t)
        scratch[width * t : width * t + value.shape[0]] = value
    return scratch[...].astype(LOW)


def build_small(entry_ref, one_ref, two_ref, norm_ref, head_ref, *refs):
    places = refs[:8]
    entry_one_o, entry_two_o, entry_turned_o, one_o, one_turned_o, two_o, two_turned_o, line_o = refs[8:16]
    par_refs, (small, large) = refs[16:26], refs[26:]
    entry_one = padded_kernel(lambda t: entry_ref[6 * t : 6 * t + 6, 0], small, 8)
    entry_two = padded_kernel(lambda t: entry_ref[6 * t : 6 * t + 6, 1], small, 8)
    exit_one = padded_kernel(lambda t: one_ref[t], small, 8)
    exit_two = padded_kernel(lambda t: two_ref[t], large, 16)
    place_rows(places[0], entry_one, entry_one_o)
    place_rows(places[1], entry_two, entry_two_o)
    place_lanes(places[2], entry_two, entry_turned_o)
    place_lanes(places[3], exit_one, one_o)
    place_rows(places[4], exit_one, one_turned_o)
    place_lanes(places[5], exit_two, two_o)
    place_rows(places[6], exit_two, two_turned_o)
    for norm, par_o in enumerate(par_refs):
        for spot in range(4):
            par_o[:, 64 * spot : 64 * spot + 64] = norm_ref[norm // 5, norm % 5]
    for spot in range(8):
        one = jnp.where(hot(places[7][spot : spot + 1], head_ref.shape[1]), 1.0, 0.0)
        line_o[spot : spot + 1] = exact_dot(head_ref[...], one, ((1,), (0,)))


def build_blocks(kernel_ref, *o_refs):
    count = kernel_ref.shape[0]
    for k, o_ref in enumerate(o_refs):
        if k < count:
            tap = [kernel_ref[k, t].astype(LOW) for t in range(9)]
        else:
            tap = [kernel_ref[k - count, 8 - t].T.astype(LOW) for t in range(9)]
        zero = jnp.zeros((64, 64), LOW)
        for r in range(4):
            for c in range(4):
                parts = [
                    tap[3 * (r - q) + c - s] if 0 <= r - q < 3 and 0 <= c - s < 3 else zero
                    for q in range(2)
                    for s in range(2)
                ]
                row = (((r // 2) * 2 + c // 2) * 4 + (r % 2) * 2 + c % 2) * 64
                o_ref[row : row + 64] = jnp.concatenate(parts, axis=1)


def groups(count):
    head = [(0, 1)] if count % 8 else []
    return head + [(start, 8) for start in range(count % 8, count, 8)]


def runs(count):
    return [list(range(start, min(start + 6, count))) for start in range(0, count, 6)]


def lane_fold(value):
    value = value + pltpu.roll(value, 128, 1)
    return value + pltpu.roll(value, 64, 1)


def total_rows(value):
    return jnp.sum(value, axis=0, keepdims=True)


def edge_masks(odd, count, by_row=True):
    if not odd:
        return lambda k, value: value
    lane = lax.broadcasted_iota(jnp.int32, (count, 1, 256), 2)
    spot = lax.broadcasted_iota(jnp.int32, (count, 1, 256), 0)
    low_column = (lane // 64) % 2 == 0
    low_row = lane < 128
    along, across = (low_column, low_row) if by_row else (low_row, low_column)
    line = jnp.where((spot == 0) & along | (spot == count - 1) & ~along, 0.0, 1.0)
    first = jnp.where(across, 0.0, line)
    last = jnp.where(across, line, 0.0)

    def apply(k, value):
        if k == 0 or k == count - 1:
            return value * (first if k == 0 else last)
        return jnp.concatenate([value[:1] * line[:1], value[1:-1], value[-1:] * line[-1:]], axis=0)

    return apply


def norm_lines(st_ref, par_ref, cells):
    mean = st_ref[0:1, :]
    inv = lax.rsqrt(st_ref[1:2, :] / cells + NORM_EPS)
    return mean, inv, par_ref[0:1, :], par_ref[1:2, :]


def clear_border(ref, count):
    ref[0] = jnp.zeros(ref.shape[1:], ref.dtype)
    ref[count + 1] = jnp.zeros(ref.shape[1:], ref.dtype)
    ref[:, 0] = jnp.zeros((ref.shape[0],) + ref.shape[2:], ref.dtype)
    ref[:, count + 1] = jnp.zeros((ref.shape[0],) + ref.shape[2:], ref.dtype)


class Activation:
    def __init__(self, v_ref, count, st_ref, par_ref, a_ref, odd, cells):
        mean, inv, gain, shift = norm_lines(st_ref, par_ref, cells)
        self.scale = 0.5 * gain * inv
        self.offset = 0.5 * shift - mean * self.scale
        self.inside = edge_masks(odd, count)
        self.pad = 0 if odd else 1
        self.v_ref, self.a_ref, self.count = v_ref, a_ref, count
        if self.pad:
            clear_border(a_ref, count)

    def row(self, i):
        half = self.v_ref[i, : self.count] * self.scale + self.offset
        act = self.inside(i, half * (1.0 + jnp.tanh(half)))
        self.a_ref[i + self.pad, self.pad : self.pad + self.count] = act.astype(LOW)


def staged(own, count, odd, size, before, work, after):
    done = 0
    last = range(0)
    for start in range(0, count, size):
        rows = range(start, min(start + size, count))
        ready = min(own, rows[-1] + 3 if odd else rows[-1] + 2)
        for i in range(done, ready):
            before(i)
        done = ready
        work(rows[0], len(rows))
        for k in last:
            after(k)
        last = rows
    for i in range(done, own):
        before(i)
    for k in last:
        after(k)


def four_views(ref, start, size, count):
    n = ref.shape[2]
    return [
        ref[start + vi : start + vi + size, vj : vj + count].reshape(size * count * n, 256)
        for vi in range(2)
        for vj in range(2)
    ]


class Spread:
    def __init__(self, o_ref, count, odd, by_row):
        self.o_ref, self.count, self.odd, self.by_row = o_ref, count, odd, by_row
        self.inside = edge_masks(odd, count, by_row)
        self.near = None
        self.first = self.second = jnp.zeros((8, 256), WIDE)

    def add(self, k):
        count, n = self.count, self.o_ref.shape[2]
        value = self.o_ref[k, :count] if self.by_row else self.o_ref[:count, k]
        if self.near is None:
            line = self.o_ref[1, 1 : count - 1] if self.by_row else self.o_ref[1 : count - 1, 1]
            line = jnp.sum(line.reshape(-1, 256), 0, keepdims=True)
            self.near = lane_fold(line) / (4 * n * (count - 2))
        rows = self.inside(k, value - self.near).reshape(-1, 8, 256)
        self.first = self.first + jnp.sum(rows, 0)
        self.second = self.second + jnp.sum(rows * rows, 0)

    def store(self, st_ref):
        side_cells = self.count - 1 if self.odd else self.count
        cells = self.o_ref.shape[2] * side_cells**2 * 4
        first = lane_fold(total_rows(self.first)) / cells
        second = lane_fold(total_rows(self.second))
        st_ref[0:1, :] = self.near + first
        st_ref[1:2, :] = second - first * first * cells


def mid_forward(odd, cells, st_ref, par_ref, held_ref, w_ref, state_ref, out_st_ref, far_ref, a_ref, sem):
    count = far_ref.shape[0]
    n = far_ref.shape[2]
    own = count + 1 if odd else count - 1
    v_ref, o_ref = (state_ref.at[0], state_ref.at[1]) if odd else (state_ref.at[1], state_ref.at[0])
    activation = Activation(v_ref, own, st_ref, par_ref, a_ref, odd, cells)
    spread = Spread(o_ref, count, not odd, True)
    copies = []

    def work(k, size):
        left = jnp.concatenate(four_views(a_ref, k, size, count), axis=1)
        value = jnp.dot(left, w_ref[...], preferred_element_type=WIDE).reshape(size, count, n, 256)
        o_ref[k : k + size, :count] = value if odd else value + o_ref[k : k + size, :count]
        copies.append(
            pltpu.make_async_copy(o_ref.at[k : k + size, :count], far_ref.at[k : k + size], sem.at[k])
        )
        copies[-1].start()

    def after(k):
        if k > 0 or count == 1:
            spread.add(k)
        if k == 1:
            spread.add(0)

    staged(own, count, odd, 1, activation.row, work, after)
    spread.store(out_st_ref)
    for copy in copies:
        copy.wait()


def rolled(value, shift):
    shift = shift % 128
    return value if shift == 0 else pltpu.roll(value, shift, 1)


def window_left(x_ref, spot, width):
    count = x_ref.shape[0] // 2 - 1
    n = x_ref.shape[1]
    columns = 128 // width
    first = 2 * spot - 2
    value = rolled(x_ref[...].reshape(-1, 128), -width * first).reshape(count + 1, 2, n, 128)
    if first < 0 or first + 4 > columns:
        column = lax.broadcasted_iota(jnp.int32, (count + 1, 2, n, 128), 3) // width + first
        value = jnp.where((column >= 0) & (column < columns), value, jnp.zeros_like(value))
    return jnp.concatenate(
        [value[r // 2 : r // 2 + count, r % 2].reshape(count * n, 128) for r in range(4)], axis=1
    ).astype(LOW)


def window_forward(width, x_ref, w_ref, state_ref, st_ref, far_ref, sem):
    count, n = far_ref.shape[0], far_ref.shape[2]
    o_ref = state_ref.at[0]
    spread = Spread(o_ref, count, True, False)
    done = []
    for spots in runs(count):
        left = jnp.concatenate([window_left(x_ref, spot, width) for spot in spots], axis=0)
        value = jnp.dot(left, w_ref[...], preferred_element_type=WIDE).reshape(len(spots), count, n, 256)
        for k, spot in enumerate(spots):
            o_ref[:, spot] = value[k]
        for spot in done:
            spread.add(spot)
        done = spots
    copy = pltpu.make_async_copy(o_ref, far_ref, sem.at[0])
    copy.start()
    for spot in done:
        spread.add(spot)
    spread.store(st_ref)
    copy.wait()


def to_rows(value_ref, step, items, store):
    count, n = value_ref.shape[0], value_ref.shape[2]
    room = 128 // items
    per = count // items
    sums = []
    for part in range(items):
        total = None
        for spot in range(part * per, part * per + per):
            moved = rolled(value_ref[:, spot].reshape(-1, 128), step * spot)
            total = moved if total is None else total + moved
        sums.append(total)
    lane = lax.broadcasted_iota(jnp.int32, (count * n, 128), 1) // room
    for item in range(items):
        value = sums[0]
        for part in range(1, items):
            value = jnp.where(lane == (item + part) % items, sums[part], value)
        store(item, rolled(value, -room * item).reshape(count, n, 128))


def exit_forward(cells, step, items, st_ref, par_ref, state_ref, w_ref, o_ref, a_ref, value_ref):
    count = value_ref.shape[0]
    n = value_ref.shape[2]
    activation = Activation(state_ref.at[0], count + 1, st_ref, par_ref, a_ref, True, cells)

    def work(k, size):
        left = jnp.concatenate(four_views(a_ref, k, size, count), axis=1)
        value = jnp.dot(left, w_ref[...], preferred_element_type=WIDE)
        value_ref[k : k + size] = value.reshape(size, count, n, 128)

    staged(count + 1, count, True, 4, activation.row, work, lambda k: None)

    def store(item, value):
        o_ref[item] = value

    to_rows(value_ref, step, items, store)


class ActivationGrads:
    def __init__(self, g_ref, v_ref, count, st_ref, par_ref, a_ref, odd, cells, by_row):
        mean, inv, self.gain, self.shift = norm_lines(st_ref, par_ref, cells)
        self.scale = 0.5 * self.gain * inv
        self.offset = 0.5 * self.shift - mean * self.scale
        self.inside = edge_masks(odd, count, by_row)
        self.pad = 0 if odd else 1
        self.g_ref, self.v_ref, self.a_ref = g_ref, v_ref, a_ref
        self.count, self.by_row = count, by_row
        self.first = self.second = jnp.zeros((8, 256), WIDE)
        if self.pad:
            clear_border(a_ref, count)

    def add(self, k):
        here = (k, slice(0, self.count)) if self.by_row else (slice(0, self.count), k)
        low, high = self.pad, self.pad + self.count
        there = (k + self.pad, slice(low, high)) if self.by_row else (slice(low, high), k + self.pad)
        half = self.v_ref[here] * self.scale + self.offset
        bend = jnp.tanh(half)
        rise = 1.0 + bend
        act = half * rise
        self.a_ref[there] = self.inside(k, act).astype(LOW)
        grad = self.inside(k, self.g_ref[here] * (rise + act * (1.0 - bend)))
        self.g_ref[here] = grad
        self.first = self.first + jnp.sum(grad.reshape(-1, 8, 256), 0)
        self.second = self.second + jnp.sum((grad * half).reshape(-1, 8, 256), 0)

    def store(self, sum_ref):
        first = lane_fold(total_rows(self.first))
        second = lane_fold(total_rows(self.second))
        sum_ref[0:1, :] = first
        sum_ref[1:2, :] = (2.0 * second - self.shift * first) / self.gain


class NormInputGrads:
    def __init__(self, sum_ref, st_ref, par_ref, state_ref, spot, count, low_ref, odd, cells, residual, keep):
        mean, inv, gain, shift = norm_lines(st_ref, par_ref, cells)
        self.scale = 0.5 * gain * inv
        self.slope = -self.scale * inv * sum_ref[1:2, :] / cells
        self.offset = -self.scale * sum_ref[0:1, :] / cells - self.slope * mean
        self.inside = edge_masks(odd, count)
        self.pad = 0 if odd else 1
        self.state_ref, self.low_ref, self.spot, self.count = state_ref, low_ref, spot, count
        self.residual, self.keep = residual, keep
        if self.pad:
            clear_border(low_ref, count)

    def row(self, i):
        state_ref, count = self.state_ref, self.count
        grad = state_ref[0, i, :count] * self.scale + state_ref[self.spot, i, :count] * self.slope + self.offset
        grad = self.inside(i, grad)
        if self.residual:
            grad = grad + state_ref[2, i]
        if self.keep:
            state_ref[2, i] = grad
        self.low_ref[i + self.pad, self.pad : self.pad + count] = grad.astype(LOW)


def pieces(count):
    edges = [count * k // 4 for k in range(5)]
    return list(zip(edges[:-1], edges[1:]))


def mid_backward(odd, residual, cells, *refs):
    sum_ref, st_ref, par_ref, held_ref, w_ref, in_st_ref, in_par_ref, in_v_far = refs[:8]
    state_ref, pair_ref, out_sum_ref, sem = refs[8:]
    count, n = in_v_far.shape[0], in_v_far.shape[2]
    own = count + 1 if odd else count - 1
    low_ref, a_ref = pair_ref.at[0], pair_ref.at[1]
    spot, next_spot = (1, 3) if odd else (3, 1)
    copies = {}
    for k, (low, high) in enumerate(pieces(count)):
        copies[low] = pltpu.make_async_copy(
            in_v_far.at[low:high], state_ref.at[next_spot, low:high, :count], sem.at[k]
        )
        copies[low].start()
    inputs = NormInputGrads(sum_ref, st_ref, par_ref, state_ref, spot, own, low_ref, odd, cells, residual, odd)
    outputs = ActivationGrads(
        state_ref.at[0], state_ref.at[next_spot], count, in_st_ref, in_par_ref, a_ref, not odd, cells, True
    )

    def work(k, size):
        left = jnp.concatenate(four_views(low_ref, k, size, count), axis=1)
        value = jnp.dot(left, w_ref[...], preferred_element_type=WIDE)
        state_ref[0, k : k + size, :count] = value.reshape(size, count, n, 256)

    def after(k):
        if k in copies:
            copies[k].wait()
        outputs.add(k)

    staged(own, count, odd, 17, inputs.row, work, after)
    outputs.store(out_sum_ref)


def window_backward(width, arrays, cells, *refs):
    d_refs = refs[:arrays]
    w_ref, st_ref, par_ref, v_far, state_ref, a_ref, sum_ref, sem = refs[arrays:]
    count, n = v_far.shape[0], v_far.shape[2]
    copy = pltpu.make_async_copy(v_far, state_ref.at[1], sem.at[0])
    copy.start()
    outputs = ActivationGrads(
        state_ref.at[0], state_ref.at[1], count, st_ref, par_ref, a_ref, True, cells, False
    )
    done = []
    for index, spots in enumerate(runs(count)):
        left = jnp.concatenate(
            [
                jnp.concatenate([window_left(d_ref, spot, width) for d_ref in d_refs], axis=1)
                for spot in spots
            ],
            axis=0,
        )
        value = jnp.dot(left, w_ref[...], preferred_element_type=WIDE).reshape(len(spots), count, n, 256)
        for k, spot in enumerate(spots):
            state_ref[0, :, spot] = value[k]
        if index == 1:
            copy.wait()
        for spot in done:
            outputs.add(spot)
        done = spots
    for spot in done:
        outputs.add(spot)
    outputs.store(sum_ref)


def entry_backward(cells, inputs, *refs):
    sum_ref, st_ref, par_ref, state_ref = refs[:4]
    low_ref = refs[5] if inputs else refs[4]
    count = low_ref.shape[0]
    grads = NormInputGrads(sum_ref, st_ref, par_ref, state_ref, 1, count, low_ref, True, cells, True, False)
    for i in range(count):
        grads.row(i)
    if inputs:
        w_ref, low_ref, o_ref, value_ref = refs[4:]
        count, n = value_ref.shape[0], value_ref.shape[2]
        for start, size in groups(count):
            left = jnp.concatenate(four_views(low_ref, start, size, count), axis=1)
            value = jnp.dot(left, w_ref[...], preferred_element_type=WIDE)
            value_ref[start : start + size] = value.reshape(size, count, n, 128)

        def store(item, value):
            o_ref[item] = value

        to_rows(value_ref, 16, 2, store)


def block_weight_grad(odd, spot, pair_ref, *refs):
    o_ref, acc_ref = refs[-2:]
    low_ref, a_ref = pair_ref.at[0], pair_ref.at[1]
    pad = 0 if odd else 1
    count = low_ref.shape[0] - (1 if odd else 2)
    n = low_ref.shape[2]
    for index, (start, size) in enumerate(groups(count)):
        grad = low_ref[start + pad : start + pad + size, pad : pad + count].reshape(size * count * n, 256)
        right = jnp.concatenate(four_views(a_ref, start, size, count), axis=1)
        part = lax.dot_general(grad, right, (((0,), (0,)), ((), ())), preferred_element_type=WIDE)
        if index == 0:
            acc_ref[...] = part
        else:
            acc_ref[...] += part
    for dy in range(3):
        for dx in range(3):
            total = None
            for q in range(2):
                for s in range(2):
                    r, c = dy + q, dx + s
                    lane = ((r // 2) * 2 + c // 2) * 256 + ((r % 2) * 2 + c % 2) * 64
                    part = acc_ref[(2 * q + s) * 64 : (2 * q + s) * 64 + 64, lane : lane + 64]
                    total = part if total is None else total + part
            total = total.T
            start = 288 * spot + 32 * (3 * dy + dx)
            o_ref[start : start + 32, :64] = total[:32]
            o_ref[start : start + 32, 64:] = total[32:]


def window_weight_grad(width, arrays, *refs):
    x_refs = refs[:arrays]
    b_ref, place_ref, o_ref, acc_ref = refs[arrays:]
    count, n = b_ref.shape[0], b_ref.shape[2]
    for spots in runs(count):
        right = jnp.concatenate(
            [
                jnp.concatenate([window_left(x_ref, spot, width) for x_ref in x_refs], axis=1)
                for spot in spots
            ],
            axis=0,
        )
        left = jnp.concatenate([b_ref[:, spot].reshape(count * n, 256) for spot in spots], axis=0)
        part = lax.dot_general(left, right, (((0,), (0,)), ((), ())), preferred_element_type=WIDE)
        if spots[0] == 0:
            acc_ref[...] = part
        else:
            acc_ref[...] += part
    lane = lax.broadcasted_iota(jnp.int32, (64, 128), 1) // 32
    total = None
    for p in range(4):
        parts = []
        for array in range(arrays):
            held = jnp.zeros((64, 128), WIDE)
            for r in range(4):
                start = 512 * array + 128 * r
                value = rolled(acc_ref[64 * p : 64 * p + 64, start : start + 128], 32 * r)
                held = jnp.where(lane == r, value, held)
            parts.append(held)
        one = jnp.where(hot(place_ref[p : p + 1], 72 * arrays), 1.0, 0.0)
        part = exact_dot(one, jnp.concatenate(parts, axis=1), ((1,), (1,)))
        total = part if total is None else total + part
    o_ref[...] = total


def lane_ids(shape):
    return lax.broadcasted_iota(jnp.int32, shape, len(shape) - 1)


def flat_roll(value, shift):
    return rolled(value.reshape(-1, 128), shift).reshape(value.shape)


def valid_lanes(cells):
    held = jnp.where(lane_ids(cells.shape) % 4 == 3, cells, 0.0)
    return flat_roll(held, -1) + flat_roll(held, -2) + flat_roll(held, -3)


def pad_rows(x_ref, values):
    rows, n = values.shape[0], values.shape[1]
    x_ref[0:2] = jnp.zeros((2, n, 128), x_ref.dtype)
    x_ref[2 : 2 + rows] = values.astype(x_ref.dtype)
    x_ref[2 + rows :] = jnp.zeros((2, n, 128), x_ref.dtype)


def column_line(value):
    return jnp.sum(value.reshape(-1, 128), axis=0, keepdims=True)


def checks(shape):
    lane = lane_ids(shape)
    row = lax.broadcasted_iota(jnp.int32, shape, 0)
    return ((row + lane // 4) % 2 == 1) & (lane % 4 != 3)


def prepare(cells_ref, x_ref, logits_ref, sum_ref):
    cells = cells_ref[...]
    lane = lane_ids(cells.shape)
    channel = lane % 4 != 3
    valid = valid_lanes(cells)
    prob = ALPHA + (1.0 - 2.0 * ALPHA) * (cells / 256.0)
    log_in = jnp.log(prob)
    log_out = jnp.log(1.0 - prob)
    logits = jnp.where(channel, log_in - log_out, 0.0)
    jacobian = math.log(1.0 - 2.0 * ALPHA) - log_in - log_out
    logits_ref[...] = logits
    sum_ref[0:1] = column_line(valid)
    sum_ref[1:2] = column_line(valid * (HALF_LOG_TAU + LOG_LEVELS - jacobian))
    odd = checks(cells.shape)
    pad_rows(x_ref, jnp.where(odd, 1.0, logits))


def couple(line_ref, raw_ref, logits_ref, cells_ref, top_ref, low_ref, bend_ref, sum_ref):
    logits = logits_ref[...]
    valid = valid_lanes(cells_ref[...])
    gain = line_ref[0:1].reshape(1, 1, 128)
    total = jnp.zeros((1, 128), WIDE)
    for q in range(2):
        raw = raw_ref[q] + line_ref[1 + q : 2 + q].reshape(1, 1, 128)
        own = logits_ref[pl.ds(q, raw.shape[0], 2)]
        cells = cells_ref[pl.ds(q, raw.shape[0], 2)]
        lane = lane_ids(raw.shape)
        odd = ((q + lane // 4) % 2 == 1) & (lane % 4 != 3)
        shift = flat_roll(raw, 4 if q == 0 else -4)
        bend = jnp.where(odd, jnp.tanh(raw), 0.0)
        scale = gain * bend
        coupled = jnp.where(odd, own * jnp.exp(scale) + shift, own)
        bend_ref[q] = bend
        total = total - column_line(valid_lanes(cells) * scale)
        (top_ref, low_ref)[q][...] = jnp.where(lane % 4 == 3, cells, coupled)
    sum_ref[...] = total


def enter_two(coupled_ref, x_ref):
    value = coupled_ref[...]
    pad_rows(x_ref, jnp.where(lane_ids(value.shape) % 4 == 3, 0.0, value))


def losses(mine_ref, line_ref, count_ref, raw_ref, top_ref, low_ref, other_ref, scale_d_ref, shift_d_ref, grad_ref, sum_ref):
    half = top_ref.shape[0]
    shape = top_ref.shape
    channel = lane_ids(shape) % 4 != 3
    top = top_ref[...]
    low = jnp.concatenate(
        [
            jnp.where(mine_ref[0] == 0, low_ref[...], other_ref[...]),
            jnp.where(mine_ref[0] == 0, other_ref[...], low_ref[...]),
        ],
        axis=1,
    )
    top_valid = valid_lanes(top)
    low_valid = valid_lanes(low)
    top = jnp.where(channel, top, 0.0)
    low = jnp.where(channel, low, 0.0)

    def rows(item):
        pair = jnp.stack([raw_ref[item], raw_ref[2 + item]], axis=1)
        return pair.reshape(shape) + line_ref[4 + item : 5 + item].reshape(1, 1, 128)

    gain = line_ref[3:4].reshape(1, 1, 128)
    unit = 1.0 / (LOG_TWO * jnp.sum(count_ref[0:1], axis=1, keepdims=True)).reshape(1, 1, 1)
    bend = jnp.tanh(rows(0))
    scale = gain * bend
    grow = jnp.exp(scale)
    latent = jnp.where(channel, low * grow + rows(1), 0.0)
    sum_ref[0:1] = column_line(top_valid * (0.5 * top * top) + low_valid * (0.5 * latent * latent - scale))
    moved = low_valid * unit * latent
    grad_scale = moved * low * grow - low_valid * unit
    raw_grad = grad_scale * gain * (1.0 - bend * bend)
    sum_ref[1:2] = column_line(grad_scale * bend)
    sum_ref[2:3] = column_line(raw_grad)
    sum_ref[3:4] = column_line(moved)
    pad_rows(scale_d_ref, raw_grad)
    pad_rows(shift_d_ref, moved)
    grad_ref[pl.ds(0, half, 2)] = top_valid * unit * top
    grad_ref[pl.ds(1, half, 2)] = moved * grow


def uncouple(mine_ref, line_ref, count_ref, entry_ref, grad_ref, logits_ref, bend_ref, cells_ref, d_ref, sum_ref):
    half = logits_ref.shape[0] // 2
    n = logits_ref.shape[1]
    own_part = pl.ds(pl.multiple_of(mine_ref[0], 8), n)
    gain = line_ref[0:1].reshape(1, 1, 128)
    unit = 1.0 / (LOG_TWO * jnp.sum(count_ref[0:1], axis=1, keepdims=True)).reshape(1, 1, 1)
    lines = [jnp.zeros((1, 128), WIDE)] * 3
    d_ref[0:2] = jnp.zeros((2, n, 128), d_ref.dtype)
    d_ref[2 * half + 2 :] = jnp.zeros((d_ref.shape[0] - 2 * half - 2, n, 128), d_ref.dtype)
    for q in range(2):
        grad = grad_ref[pl.ds(q, half, 2), own_part]
        if q == 0:
            grad = grad + jnp.stack([entry_ref[0, :, own_part], entry_ref[1, :, own_part]], axis=1).reshape(half, n, 128)
        own = logits_ref[pl.ds(q, half, 2)]
        valid = valid_lanes(cells_ref[pl.ds(q, half, 2)])
        bend = bend_ref[q]
        lane = lane_ids(grad.shape)
        odd = ((q + lane // 4) % 2 == 1) & (lane % 4 != 3)
        grad = jnp.where(odd, grad, 0.0)
        grad_scale = jnp.where(odd, grad * own * jnp.exp(gain * bend) - valid * unit, 0.0)
        raw_grad = grad_scale * gain * (1.0 - bend * bend)
        lines[0] = lines[0] + column_line(grad_scale * bend)
        lines[1] = lines[1] + column_line(raw_grad)
        lines[2] = lines[2] + column_line(grad)
        value = raw_grad + flat_roll(grad, -4 if q == 0 else 4)
        d_ref[pl.ds(2 + q, half, 2)] = value.astype(d_ref.dtype)
    for spot in range(3):
        sum_ref[spot : spot + 1] = lines[spot]


def call(kernel, outs, args, name, scratch=(), limit=16, far_in=(), far_out=(), sems=0, aliases=None, scalar_in=()):
    spaces = [
        pltpu.HBM if spot in far_in else pltpu.SMEM if spot in scalar_in else pltpu.VMEM
        for spot in range(len(args))
    ]
    out_spaces = [pltpu.HBM if spot in far_out else pltpu.VMEM for spot in range(len(outs))]
    held = [pltpu.VMEM(shape, dtype) for shape, dtype in scratch]
    args = [pltpu.with_memory_space_constraint(arg, space) if space is pltpu.HBM else arg for arg, space in zip(args, spaces)]
    if sems:
        held.append(pltpu.SemaphoreType.DMA(sems))
    return pl.pallas_call(
        kernel,
        out_shape=[space(shape, dtype) for space, (shape, dtype) in zip(out_spaces, outs)],
        in_specs=[pl.BlockSpec(memory_space=space) for space in spaces],
        out_specs=[pl.BlockSpec(memory_space=space) for space in out_spaces],
        scratch_shapes=held,
        compiler_params=pltpu.CompilerParams(vmem_limit_bytes=limit * 2**20),
        input_output_aliases=aliases or {},
        cost_estimate=pl.CostEstimate(
            flops=int(1e+09 * COSTS.get(name, 0.5)), bytes_accessed=0, transcendentals=0
        ),
        name=name,
    )(*args)


class Net:
    def __init__(self, name, blocks, n, width, group, total, pars, weights, turned_weights):
        self.name = name
        self.even = blocks
        self.odd = blocks + 1
        self.n = n
        self.width = width
        self.group = group
        self.cells = float(total)
        self.own = float(n * blocks * blocks * 4)
        self.pars = pars
        self.weights = weights
        self.turned_weights = turned_weights
        self.far = []
        self.stats = []

    def shape(self, odd, padded=False):
        count = self.odd if odd else self.even
        pad = 2 if padded and not odd else 0
        return (count + pad, count + pad, self.n, 256)

    def keep(self, stats, far):
        self.far.append(far)
        self.stats.append(merge_stats(stats, self.own, self.group))

    def forward(self, x, entry, exit_weights, items, beside):
        held = (2,) + self.shape(True)
        state, stats, far = call(
            functools.partial(window_forward, self.width),
            [(held, WIDE), ((2, 256), WIDE), (self.shape(True), WIDE)],
            [x, entry],
            self.name + "_entry",
            far_out=(2,),
            sems=(1,),
        )
        self.keep(stats, far)
        self.stats[0], beside = lax.optimization_barrier((self.stats[0], beside))
        for index in range(4):
            odd = index % 2 == 0
            state, stats, far = call(
                functools.partial(mid_forward, odd, self.cells),
                [(held, WIDE), ((2, 256), WIDE), (self.shape(not odd), WIDE)],
                [self.stats[index], self.pars[index], state, self.weights[index]],
                self.name + "_forward",
                [(self.shape(odd, True), LOW)],
                far_out=(2,),
                sems=(self.odd,),
                aliases={2: 0},
            )
            self.keep(stats, far)
        raw = call(
            functools.partial(exit_forward, self.cells, 2 * self.width, items),
            [((items, self.even, self.n, 128), WIDE)],
            [self.stats[4], self.pars[4], state, exit_weights],
            self.name + "_exit",
            [(self.shape(True), LOW), ((self.even, self.even, self.n, 128), WIDE)],
        )[0]
        return raw, beside

    def backward(self, grads, exit_turned, exit_place, x, entry_turned, entry_place, packets, slots):
        arrays = len(grads)
        held = (4,) + self.shape(True)
        pair_shape = (2, self.even + 2, self.even + 2, self.n, 256)
        state, act, sums = call(
            functools.partial(window_backward, self.width, arrays, self.cells),
            [(held, WIDE), (self.shape(True), LOW), ((2, 256), WIDE)],
            list(grads) + [exit_turned, self.stats[4], self.pars[4], self.far[4]],
            self.name + "_exit_back",
            far_in=(arrays + 3,),
            sems=(1,),
        )
        results_of = {}

        def exit_work(token):
            (held,) = tied([act], token)
            grad = call(
                functools.partial(window_weight_grad, self.width, arrays),
                [((72 * arrays, 64), WIDE)],
                list(grads) + [held, exit_place],
                self.name + "_exit_weights",
                [((256, 512 * arrays), WIDE)],
            )[0]
            return (grad,) + slots.get(4, lambda *held: ())(None, grad, token)

        sums, exit_grad, *done = travel(sums, self.group, exit_work)
        results_of[4] = done
        norm_grads = [None] * 5
        block_grads = []
        norm_grads[4] = sums
        for index in reversed(range(4)):
            odd = index % 2 == 1
            state, pair, sums = call(
                functools.partial(mid_backward, odd, index == 1, self.cells),
                [(held, WIDE), (pair_shape, LOW), ((2, 256), WIDE)],
                [
                    sums,
                    self.stats[index + 1],
                    self.pars[index + 1],
                    state,
                    self.turned_weights[index],
                    self.stats[index],
                    self.pars[index],
                    self.far[index],
                ],
                self.name + "_back",
                far_in=(7,),
                sems=(4,),
                aliases={3: 0},
            )
            packet = next(held for held in packets if index in held)
            spot = packet.index(index)
            fresh = index == packet[-1]

            def block_work(token):
                (held,) = tied([pair], token)
                grad = call(
                    functools.partial(block_weight_grad, odd, spot),
                    [((288 * len(packet), 128), WIDE)],
                    [held] + ([] if fresh else [block]),
                    self.name + "_weights",
                    [((256, 1024), WIDE)],
                    aliases=None if fresh else {1: 0},
                )[0]
                return (grad,) + slots.get(index, lambda *held: ())(block_grads, exit_grad, token)

            sums, block, *done = travel(sums, self.group, block_work)
            results_of[index] = done
            norm_grads[index] = sums
            if index == packet[0]:
                block_grads.append(swap_terms(block, self.group))
        args = [sums, self.stats[0], self.pars[0], state]
        outs = [(self.shape(True), LOW)]
        scratch = []
        if entry_turned is not None:
            args.append(entry_turned)
            outs.append(((2, self.even, self.n, 128), WIDE))
            scratch.append(((self.even, self.even, self.n, 128), WIDE))
        results = call(
            functools.partial(entry_backward, self.cells, entry_turned is not None),
            outs,
            args,
            self.name + "_entry_back",
            scratch,
        )

        def entry_grad(token):
            low, unused = lax.optimization_barrier((results[0], token))
            return call(
                functools.partial(window_weight_grad, self.width, 1),
                [((72, 64), WIDE)],
                [x, low, entry_place],
                self.name + "_entry_weights",
                [((256, 512), WIDE)],
            )[0]

        return entry_grad, block_grads, exit_grad, norm_grads, results_of, (results[1] if entry_turned is not None else None)


def adam_blocks(spots, fresh, places, *refs):
    count = 2 * (1 + max(place[0] for place in places))
    terms, refs = refs[:count], refs[count:]
    sources, refs = refs[:3], refs[3:]
    if not fresh:
        refs = refs[4:]
    targets, (held, out, out_low, in_sem, out_sem) = refs[:4], refs[4:]
    loads = []
    for k, spot in enumerate(spots):
        loads.append(
            [pltpu.make_async_copy(sources[j].at[spot], held.at[k, j], in_sem.at[k, j]) for j in range(3)]
        )
        for copy in loads[-1]:
            copy.start()
    stores = []
    for k, spot in enumerate(spots):
        for copy in loads[k]:
            copy.wait()
        for t in range(9):
            pair, row = 2 * places[k][0], 288 * places[k][1] + 32 * t
            packed = terms[pair][row : row + 32] + terms[pair + 1][row : row + 32]
            grad = jnp.concatenate([packed[:, :64], packed[:, 64:]], axis=0)
            news = adamw(held[k, 0, t], held[k, 1, t], held[k, 2, t], grad, RATE_CONV)
            for j in range(3):
                out[k, j, t] = news[j]
            out_low[k, t] = news[3]
        copies = [pltpu.make_async_copy(out.at[k, j], targets[j].at[spot], out_sem.at[k, j]) for j in range(3)]
        copies.append(pltpu.make_async_copy(out_low.at[k], targets[3].at[spot], out_sem.at[k, 3]))
        for copy in copies:
            copy.start()
        stores += copies
    for copy in stores:
        copy.wait()


def step_blocks(spots, pairs, places, sources, targets):
    count = len(spots)
    terms = [term for pair in pairs for term in pair]
    args = terms + list(sources) + list(targets or [])
    shape = sources[0].shape
    head = len(terms)
    return pl.pallas_call(
        functools.partial(adam_blocks, spots, targets is None, places),
        out_shape=[pltpu.HBM(shape, WIDE)] * 3 + [pltpu.HBM(shape, LOW)],
        in_specs=[pl.BlockSpec(memory_space=pltpu.VMEM)] * head
        + [pl.BlockSpec(memory_space=pltpu.HBM)] * (len(args) - head),
        out_specs=[pl.BlockSpec(memory_space=pltpu.HBM)] * 4,
        scratch_shapes=[
            pltpu.VMEM((count, 3) + shape[1:], WIDE),
            pltpu.VMEM((count, 3) + shape[1:], WIDE),
            pltpu.VMEM((count,) + shape[1:], LOW),
            pltpu.SemaphoreType.DMA((count, 3)),
            pltpu.SemaphoreType.DMA((count, 4)),
        ],
        input_output_aliases={} if targets is None else {head + 3 + j: j for j in range(4)},
        compiler_params=pltpu.CompilerParams(vmem_limit_bytes=12 * 2**20),
        cost_estimate=pl.CostEstimate(flops=int(1e+09 * (1 + count)), bytes_accessed=0, transcendentals=0),
        name="step_blocks",
    )(*args[:head], *[pltpu.with_memory_space_constraint(arg, pltpu.HBM) for arg in args[head:]])


def adamw(master, first, second, grad, rate):
    first_new = BETA_ONE * first + (1.0 - BETA_ONE) * grad
    second_new = BETA_TWO * second + (1.0 - BETA_TWO) * grad * grad
    direction = (
        first_new
        / (1.0 - BETA_ONE**STEP)
        / (jnp.sqrt(second_new / (1.0 - BETA_TWO**STEP)) + ADAM_EPS)
    )
    master_new = master - rate * (direction + DECAY * master)
    return (master_new, first_new, second_new, master_new.astype(jnp.bfloat16))


def entry_view(array):
    return array.transpose(1, 2, 3, 0, 4).reshape(54, 2, 64)


def exit_view(array):
    return array.transpose(0, 1, 3, 2).reshape(9, array.shape[3], 64)


def pack_rows(*refs):
    o_ref = refs[-1]
    o_ref[...] = jnp.zeros(o_ref.shape, WIDE)
    row = 0
    for ref in refs[:-1]:
        o_ref[row : row + ref.shape[0], : ref.shape[1]] = ref[...]
        row += ref.shape[0]


def entry_grads(one_ref, one_other, two_ref, two_other, o_ref):
    one = one_ref[...] + one_other[...]
    two = two_ref[0:72, :64] + two_other[0:72, :64]
    for t in range(9):
        o_ref[6 * t : 6 * t + 6, 0] = one[8 * t : 8 * t + 6]
        o_ref[6 * t : 6 * t + 6, 1] = two[8 * t : 8 * t + 6]


def finish_kernel(*refs):
    one_ref, one_other, two_ref, two_other, count_ref = refs[:5]
    norm_sums, place_ref = refs[5:15], refs[15]
    exit_one, exit_two, norm, head = refs[16:19], refs[19:22], refs[22:25], refs[25:28]
    far, near, sem = refs[28:46], refs[46:64], refs[64]
    loss_o, valid_o = near[0:2]
    exit_one_o, exit_two_o, norm_o, head_o = near[2:6], near[6:10], near[10:14], near[14:18]
    one = one_ref[...] + one_other[...]
    two = two_ref[...] + two_other[...]

    def store(outs, index, values):
        for o_ref, value in zip(outs, values):
            o_ref[index] = value

    for t in range(9):
        grad = one[8 * t : 8 * t + 6, :64]
        store(exit_one_o, t, adamw(exit_one[0][t], exit_one[1][t], exit_one[2][t], grad, RATE_CONV))
        grad = two[72 + 16 * t : 84 + 16 * t, :64]
        store(exit_two_o, t, adamw(exit_two[0][t], exit_two[1][t], exit_two[2][t], grad, RATE_CONV))
    for k in range(10):
        spot = (k // 5, k % 5)
        sums = norm_sums[k][...]
        grad = jnp.concatenate([sums[1:2, :64], sums[0:1, :64]], axis=0) * 0.5
        store(norm_o, spot, adamw(norm[0][spot], norm[1][spot], norm[2][spot], grad, RATE_SMALL))
    valid = jnp.sum(count_ref[0:1], axis=1, keepdims=True)
    constant = jnp.sum(count_ref[1:2], axis=1, keepdims=True)
    loss = jnp.sum(two[216:217], axis=1, keepdims=True) + jnp.sum(one[75:76], axis=1, keepdims=True)
    loss_o[...] = (loss + constant) / LOG_TWO
    valid_o[...] = valid

    def folded(line, spot):
        return exact_dot(line, jnp.where(hot(place_ref[spot : spot + 1], head[0].shape[1]), 1.0, 0.0), ((1,), (1,)))

    lane = lax.broadcasted_iota(jnp.int32, (1, 128), 1)
    raw, shift = one[73:74], one[74:75]
    grad = folded(one[72:73], 0) + folded(two[217:218], 3) + folded(two[218:219], 4) + folded(two[219:220], 5)
    grad = grad + folded(jnp.where((lane // 4) % 2 == 1, raw, 0.0), 1) + folded(jnp.where((lane // 4) % 2 == 0, raw, 0.0), 2)
    grad = grad + folded(jnp.where((lane // 4) % 2 == 0, shift, 0.0), 1) + folded(jnp.where((lane // 4) % 2 == 1, shift, 0.0), 2)
    for o_ref, value in zip(head_o, adamw(head[0][...], head[1][...], head[2][...], grad, RATE_SMALL)):
        o_ref[...] = value
    copies = [pltpu.make_async_copy(near[k], far[k], sem.at[k]) for k in range(18)]
    for copy in copies:
        copy.start()
    for copy in copies:
        copy.wait()


def finish(packs, sums, place, exit_one, exit_two, norm, head):
    outs = [((1, 1), WIDE)] * 2
    for first in (exit_one[0], exit_two[0], norm[0], head[0]):
        outs += [(first.shape, WIDE)] * 3 + [(first.shape, LOW)]
    return call(
        finish_kernel,
        outs,
        packs + sums + [place] + exit_one + exit_two + norm + head,
        "finish",
        outs,
        far_out=tuple(range(18)),
        sems=(18,),
    )


def body(
    pixels,
    valid,
    entry_conv,
    entry_first,
    entry_second,
    block_conv,
    block_first,
    block_second,
    exit_one,
    exit_one_first,
    exit_one_second,
    exit_two,
    exit_two_first,
    exit_two_second,
    norm_params,
    norm_first,
    norm_second,
    head_params,
    head_first,
    head_second,
):
    batch = pixels.shape[0] * lax.axis_size("batch")
    height = pixels.shape[1] * lax.axis_size("rows")
    group = group_bits(batch)
    small = group[:-1]
    last = group[-1]
    own = batch >> len(group)
    wide = 2 * own
    cells = jnp.concatenate([pixels, valid[..., None].astype(WIDE)], axis=3)
    cells = cells.reshape(pixels.shape[0], pixels.shape[1], 128).transpose(1, 0, 2)

    place = placements()
    small_places = [
        jnp.asarray(place[key])
        for key in (
            "entry_one",
            "entry_two",
            "entry_two_turned",
            "exit_one",
            "exit_one_turned",
            "exit_two",
            "exit_two_turned",
        )
    ]
    fold = [
        jnp.asarray(place[key + "_fold"])
        for key in ("entry_one", "entry_two", "exit_one_turned", "exit_two_turned")
    ]
    small_built = call(
        build_small,
        [
            ((512, 256), LOW),
            ((512, 256), LOW),
            ((1024, 128), LOW),
            ((1024, 128), LOW),
            ((512, 256), LOW),
            ((1024, 128), LOW),
            ((1024, 256), LOW),
            ((8, 128), WIDE),
        ]
        + [((2, 256), WIDE)] * 10,
        [
            entry_view(entry_conv),
            exit_view(exit_one),
            exit_view(exit_two),
            norm_params,
            head_params[None],
        ]
        + small_places
        + [jnp.asarray(place["head"])],
        "build_small",
        [((72, 64), WIDE), ((144, 64), WIDE)],
    )
    cells, small_built = distribute(cells, group, small_built)
    (
        entry_one_w,
        entry_two_w,
        entry_turned_w,
        exit_one_w,
        exit_one_turned_w,
        exit_two_w,
        exit_two_turned_w,
        head_lines,
        *par_lines,
    ) = small_built
    blocks = call(build_blocks, [((1024, 256), LOW)] * 16, [block_conv.reshape(8, 9, 64, 64)], "build_blocks")
    weights = [[blocks[4 * j + k] for k in range(4)] for j in range(2)]
    turned_w = [[blocks[8 + 4 * j + k] for k in range(4)] for j in range(2)]
    pars = [[par_lines[5 * j + k] for k in range(5)] for j in range(2)]

    one = Net("one", height // 2, own, 4, group, batch * height * height, pars[0], weights[0], turned_w[0])
    two = Net("two", height // 4, wide, 8, small, batch * (height // 2) ** 2, pars[1], weights[1], turned_w[1])

    rows = height
    x_one, logits, first_sums = call(
        prepare,
        [((rows + 4, own, 128), WIDE), ((rows, own, 128), WIDE), ((2, 128), WIDE)],
        [cells],
        "prepare",
    )
    first_sums = group_sum(first_sums, group)
    mine, x_one = lax.optimization_barrier((side(last) * own, x_one))
    raw_one, first_sums = one.forward(x_one, entry_one_w, exit_one_w, 2, first_sums)
    coupled_top, coupled_low, bend_one, couple_sums = call(
        couple,
        [((rows // 2, own, 128), WIDE)] * 2 + [((2, rows // 2, own, 128), WIDE), ((1, 128), WIDE)],
        [head_lines, raw_one, logits, cells],
        "couple",
    )
    coupled_top = joined(coupled_top, swap(coupled_top, last), mine, 1)
    other_low = swap(coupled_low, last)
    x_two = call(enter_two, [((rows // 2 + 4, wide, 128), WIDE)], [coupled_top], "enter_two")[0]
    raw_two, other_low = two.forward(x_two, entry_two_w, exit_two_w, 4, other_low)
    scale_d, shift_d, grad_coupled, loss_sums = call(
        losses,
        [
            ((rows // 2 + 4, wide, 128), WIDE),
            ((rows // 2 + 4, wide, 128), WIDE),
            ((rows, wide, 128), WIDE),
            ((4, 128), WIDE),
        ],
        [
            jnp.reshape(mine, (1,)),
            head_lines,
            first_sums,
            raw_two,
            coupled_top,
            coupled_low,
            other_low,
        ],
        "losses",
        scalar_in=(0,),
    )
    entry_two, blocks_two, exit_two_part, norms_two, unused, grad_first = two.backward(
        [scale_d, shift_d], exit_two_turned_w, fold[3], x_two, entry_turned_w, fold[1], [[0, 1, 2, 3]], {}
    )
    def send_two(held, exit_grad, token):
        rows = call(pack_rows, [((224, 128), WIDE)], [entry_two(token), exit_two_part, loss_sums], "pack_two")[0]
        return tuple(swap_terms(rows, small))

    def send_one(held, exit_grad, token):
        rows = call(pack_rows, [((80, 128), WIDE)], [exit_grad, one_sums, couple_sums], "pack_one")[0]
        return tuple(swap_terms(rows, group))

    sources = [part.reshape(8, 9, 64, 64) for part in (block_conv, block_first, block_second)]
    steps = {}

    def step(key, spots, terms, firsts):
        def run(held, exit_grad, token):
            steps[key] = tuple(
                step_blocks(spots, [tied(terms, token)], [(0, k) for k in firsts], sources, steps.get(key - 1))
            )
            return steps[key]

        return run

    one_d, one_sums = call(
        uncouple,
        [((rows + 4, own, 128), WIDE), ((3, 128), WIDE)],
        [jnp.reshape(mine, (1,)), head_lines, first_sums, grad_first, grad_coupled, logits, bend_one, cells],
        "uncouple",
        scalar_in=(0,),
    )
    slots = {
        4: send_two,
        3: send_one,
        2: step(0, (4, 5), blocks_two[0], (0, 1)),
        0: step(1, (6, 7), blocks_two[0], (2, 3)),
    }
    entry_one, blocks_one, exit_one_part, norms_one, done, unused = one.backward(
        [one_d], exit_one_turned_w, fold[2], x_one, None, fold[0], [[1, 2, 3], [0]], slots
    )
    entry_one, *blocks_done = lax.optimization_barrier((entry_one(first_sums), *blocks_one[0]))
    entry_one = swap_terms(entry_one, group)
    pack_two, pack_one = list(done[4]), list(done[3])
    stepped = step_blocks(
        (1, 2, 3), [blocks_done], [(0, 0), (0, 1), (0, 2)], sources, done[0]
    )
    finished = finish(
        pack_one + pack_two,
        [first_sums] + norms_one + norms_two,
        jnp.asarray(place["head"]),
        [exit_view(part) for part in (exit_one, exit_one_first, exit_one_second)],
        [exit_view(part) for part in (exit_two, exit_two_first, exit_two_second)],
        [norm_params, norm_first, norm_second],
        [part[None] for part in (head_params, head_first, head_second)],
    )
    stepped = step_blocks((0,), [blocks_one[1]], [(0, 0)], sources, stepped)
    entry_grad = call(
        entry_grads, [((54, 2, 64), WIDE)], entry_one + pack_two, "entry_grads"
    )[0]
    entry_steps = adamw(
        entry_view(entry_conv), entry_view(entry_first), entry_view(entry_second), entry_grad, RATE_CONV
    )
    entry_out = tuple(
        part.reshape(3, 3, 6, 2, 64).transpose(3, 0, 1, 2, 4) for part in entry_steps
    )
    one_out = tuple(part.reshape(3, 3, 6, 64).transpose(0, 1, 3, 2) for part in finished[2:6])
    two_out = tuple(part.reshape(3, 3, 12, 64).transpose(0, 1, 3, 2) for part in finished[6:10])
    return (
        (finished[0].reshape(()), finished[1].reshape(()))
        + entry_out
        + tuple(part.reshape(block_conv.shape) for part in stepped)
        + one_out
        + two_out
        + tuple(finished[10:14])
        + tuple(part.reshape(head_params.shape) for part in finished[14:18])
    )


def solution(mesh):
    placed = (P("batch", "rows", None, None), P("batch", "rows", None)) + (P(),) * 18
    return jax.shard_map(body, mesh=mesh, in_specs=placed, out_specs=(P(),) * 26, check_vma=False)
```
